32 devices in a mesh: groups: 2 (over y), seq: 4 (over z), weight: 4 (over x, core).
Axes of the slice: x: 2, y: 2, z: 4, core: 2. Of those that a mesh axis runs over, the one named last changes fastest.
Arguments:
- tokens: bfloat16 [8, 512, 1536], P(('groups', 'weight'), 'seq'), parts along dimension 0, may hold values from -20 to 20
- upstream_grad: bfloat16 [8, 512, 1536], P(('groups', 'weight'), 'seq'), parts along dimension 0, may hold values from -6 to 6
- norm_gain: float32 [1536], replicated, may hold values from 0.5 to 1.5
- norm_bias: float32 [1536], replicated, may hold values from -3 to 3
- input_codes: bfloat16 [1536, 2304], P('weight'), may hold values from -10 to 10
- input_scales: float32 [12, 18], P('weight'), may hold values from 0.02 to 0.06
- input_bias: float32 [2304], replicated, may hold values from -3 to 3
- output_codes: bfloat16 [768, 1536], replicated, may hold values from -4 to 4
- output_scales: float32 [6, 12], replicated, may hold values from 0.02 to 0.06
- layer_scale: float32 [1536], replicated, may hold values from 0.3 to 3
Outputs:
- input_grad: float32 [8, 512, 1536], P(('groups', 'weight'), 'seq'), parts along dimension 0
The draws below stay inside these ranges and needn't reach their ends.
There are 2 independent parts, one for each index of `groups`. The reference program is written for one: setup_inputs(seed, part) draws one part's arguments, and reference() takes and returns one part's arrays. A program takes and returns all parts, laid end to end along the dimension named above; an argument that names none is the same for every part. Nothing has to cross between parts.
All inputs are finite; a program needn't handle non-finite values.
Results may differ from the reference program's by a relative error of at most 0.024.
Values may be sent and summed in bfloat16 or wider, within the bound.
No kernel may reach another device: no remote copies, remote signals or barrier semaphores. Data moves between devices by JAX's collectives and lax.ppermute only.
A program may use at most 128 MiB of HBM per device.

```python
import math
import jax
import jax.numpy as jnp
from jax import lax

D = 1536
HEADS = 12
HEAD_DIM = 64
QBLOCK = 128
TOK_DEV = 128
HD = 768
SEQ = 512
IMAGES = 4
N_SEQ = 4


def draw_tokens(key, part):
    first_key = jax.random.fold_in(key, 0)
    sample = jax.random.normal(first_key, (IMAGES, SEQ, D), jnp.float32)
    return jnp.clip(sample, -6.0, 6.0).astype(jnp.bfloat16)


def draw_input_codes(key, part):
    first_key = jax.random.fold_in(key, 0)
    sample = jnp.clip(jax.random.normal(first_key, (D, 3 * HD), jnp.float32), -4.0, 4.0)
    return sample.astype(jnp.bfloat16)


def levels(stream_key, shape, cuts, low, high):
    loudness = 1.0
    for axis_at, blocks in cuts:
        steps = jax.random.uniform(jax.random.fold_in(jax.random.fold_in(stream_key, 6), axis_at), (blocks,), jnp.float32, low / len(cuts), high / len(cuts))
        loudness = loudness * jnp.repeat(jnp.exp(steps), shape[axis_at] // blocks).reshape((-1,) + (1,) * (len(shape) - 1 - axis_at))
    return loudness


def normal_values(stream_key, shape, scale, bound, shards=(), dtype=jnp.bfloat16):
    result = jax.random.normal(stream_key, shape, jnp.float32) * scale
    if len(shards) > 0:
        result = levels(stream_key, shape, shards, -0.22, 0.18) * result
    return jnp.clip(result, min=-bound, max=bound).astype(dtype)


def setup_inputs(seed: int = 0, part: int = 0) -> dict:
    keys = jax.random.split(jax.random.key(seed), 11)
    part_splits = jax.random.split(jax.random.fold_in(keys[10], part), 11)
    return {
        "tokens": draw_tokens(jax.random.fold_in(jax.random.fold_in(keys[10], part), 71), part),
        "upstream_grad": normal_values(part_splits[1], (IMAGES, SEQ, D), 1.0, 6.0, ((0, 4), (1, 4))),
        "norm_gain": jnp.clip(1.0 + 0.1 * jax.random.normal(keys[2], (D,), jnp.float32), 0.5, 1.5),
        "norm_bias": normal_values(keys[3], (D,), 0.5, 3.0, (), jnp.float32),
        "input_codes": draw_input_codes(jax.random.fold_in(keys[10], 71), part),
        "input_scales": jnp.clip(jnp.exp(math.log(0.06) - 1.0986123 * jax.random.uniform(keys[5], (D // QBLOCK, 3 * HD // QBLOCK), jnp.float32) ** levels(keys[5], (D // QBLOCK, 3 * HD // QBLOCK), ((0, 4),), -0.2, 0.2)), 0.02, 0.06),
        "input_bias": normal_values(keys[6], (3 * HD,), 0.5, 3.0, (), jnp.float32),
        "output_codes": normal_values(keys[7], (HD, D), 1.0, 4.0),
        "output_scales": jnp.clip(jnp.exp(jax.random.uniform(keys[8], (HD // QBLOCK, D // QBLOCK), jnp.float32, math.log(0.02), math.log(0.06))), 0.02, 0.06),
        "layer_scale": jnp.clip(jnp.exp(jax.random.uniform(keys[9], (D,), jnp.float32, math.log(0.3), math.log(3.0))), 0.3, 3.0),
    }


def dequantize(codes, scales):
    expanded = jnp.repeat(jnp.repeat(scales, QBLOCK, axis=0), QBLOCK, axis=1)
    return (codes.astype(jnp.float32) * expanded).astype(jnp.bfloat16)

def normalize(rows, gain, shift):
    mean_value = lax.optimization_barrier(jnp.mean(rows, axis=-1, keepdims=True))
    centered = rows - mean_value
    variance = lax.optimization_barrier(jnp.mean(centered * centered, axis=-1, keepdims=True))
    inverse = lax.rsqrt(variance + 1e-06)
    normed = centered * inverse
    return (normed, inverse, (normed * gain + shift).astype(jnp.bfloat16))

def norm_backward(grad_norm, normed, inverse, gain):
    grad_hat = grad_norm * gain
    first_mean = lax.optimization_barrier(jnp.mean(grad_hat, axis=-1, keepdims=True))
    second_mean = lax.optimization_barrier(jnp.mean(grad_hat * normed, axis=-1, keepdims=True))
    return inverse * (grad_hat - first_mean - normed * second_mean)

def rounded_total(terms):
    rounded = lax.optimization_barrier(terms.astype(jnp.bfloat16))
    return lax.optimization_barrier(jnp.sum(rounded.astype(jnp.float32), axis=0))

def head_backward(queries, keys_head, values_head, grads_head):
    head_scale = HEAD_DIM ** (-0.5)
    scores = jnp.dot(queries, keys_head.T, preferred_element_type=jnp.float32) * head_scale
    row_top = lax.optimization_barrier(jnp.max(scores, axis=1, keepdims=True))
    log_total = row_top + jnp.log(lax.optimization_barrier(jnp.sum(jnp.exp(scores - row_top), axis=1, keepdims=True)))
    dprob = jnp.dot(grads_head, values_head.T, preferred_element_type=jnp.float32)
    weights = jnp.exp(scores - log_total)
    row_delta = lax.optimization_barrier(jnp.sum(weights * dprob, axis=1, keepdims=True))
    prob_weights = weights.astype(jnp.bfloat16)
    dscore = (weights * (dprob - row_delta)).astype(jnp.bfloat16)
    query_grad = jnp.dot(dscore, keys_head, preferred_element_type=jnp.float32) * head_scale
    dscore_parts = dscore.astype(jnp.float32).reshape(N_SEQ, TOK_DEV, SEQ)
    prob_parts = prob_weights.astype(jnp.float32).reshape(N_SEQ, TOK_DEV, SEQ)
    query_parts = queries.astype(jnp.float32).reshape(N_SEQ, TOK_DEV, HEAD_DIM)
    grad_parts = grads_head.astype(jnp.float32).reshape(N_SEQ, TOK_DEV, HEAD_DIM)
    key_grad = rounded_total(jnp.einsum('sqk,sqd->skd', dscore_parts, query_parts) * head_scale)
    value_grad = rounded_total(jnp.einsum('sqk,sqd->skd', prob_parts, grad_parts))
    return (query_grad, key_grad, value_grad)

def split_heads(columns):
    return columns.reshape(SEQ, HEADS, HEAD_DIM).transpose(1, 0, 2)

def merge_heads(stacked):
    return stacked.transpose(1, 0, 2).reshape(SEQ, HD)

def reference(tokens, upstream_grad, norm_gain, norm_bias, input_codes, input_scales, input_bias, output_codes, output_scales, layer_scale):
    input_weight = dequantize(input_codes, input_scales)
    output_weight = dequantize(output_codes, output_scales)

    def one_image(packed):
        image_rows, image_grads = packed
        normed, inverse, norm_out = normalize(image_rows.astype(jnp.float32), norm_gain, norm_bias)
        projected = (jnp.dot(norm_out, input_weight, preferred_element_type=jnp.float32) + input_bias).astype(jnp.bfloat16)
        scaled_grad = (image_grads.astype(jnp.float32) * layer_scale).astype(jnp.bfloat16)
        head_grads = jnp.dot(scaled_grad, output_weight.T, preferred_element_type=jnp.float32).astype(jnp.bfloat16)
        heads_in = (split_heads(projected[:, :HD]), split_heads(projected[:, HD:2 * HD]), split_heads(projected[:, 2 * HD:]), split_heads(head_grads))
        query_grad, key_grad, value_grad = lax.map(lambda member: head_backward(*member), heads_in)
        grad_proj = jnp.concatenate([merge_heads(query_grad), merge_heads(key_grad), merge_heads(value_grad)], axis=1).astype(jnp.bfloat16)
        grad_norm = jnp.dot(grad_proj, input_weight.T, preferred_element_type=jnp.float32)
        return norm_backward(grad_norm, normed, inverse, norm_gain)
    return lax.map(one_image, (tokens, upstream_grad))
```

```python
import math

import jax
import jax.numpy as jnp
from jax import lax
from jax.experimental import pallas as pl
from jax.experimental.pallas import tpu as pltpu
from jax.sharding import PartitionSpec as P

HEADS = 12
HEAD_DIM = 64
QBLOCK = 128
HD = 768
HALF = HD // 2
EPSILON = 1e-06
VMEM = pltpu.VMEM
SMEM = pltpu.SMEM


def half_index():
    return lax.axis_index("seq") * 2 // lax.axis_size("seq")


def spec(memory_space=VMEM):
    return pl.BlockSpec(memory_space=memory_space)


def norm_rows(rows):
    mean_value = jnp.mean(rows, axis=-1, keepdims=True)
    centered = rows - mean_value
    variance = jnp.mean(centered * centered, axis=-1, keepdims=True)
    inverse = lax.rsqrt(variance + EPSILON)
    return centered * inverse, inverse


def copy_columns(codes_ref, held, sems, half):
    copies = []
    for part in range(3):
        start = pl.multiple_of(part * HD + half * HALF, QBLOCK)
        copies.append(
            pltpu.make_async_copy(
                codes_ref.at[:, pl.ds(start, HALF)],
                held.at[:, pl.ds(part * HALF, HALF)],
                sems.at[part],
            )
        )
        copies[-1].start()
    return copies


def scale_columns(copies, held, scales_ref, out_ref, half):
    row_blocks = held.shape[0] // QBLOCK
    for part in range(3):
        copies[part].wait()
        for r in range(row_blocks):
            for c in range(HALF // QBLOCK):
                scale = scales_ref[r, (part * HD + c * QBLOCK) // QBLOCK + half * (HALF // QBLOCK)]
                at = (
                    slice(r * QBLOCK, (r + 1) * QBLOCK),
                    slice(part * HALF + c * QBLOCK, part * HALF + (c + 1) * QBLOCK),
                )
                out_ref[at] = (held[at].astype(jnp.float32) * scale).astype(jnp.bfloat16)


def first_kernel(tokens_ref, gain_ref, shift_ref, scales_ref, codes_ref, norm_ref, weight_ref, held, sems):
    half = half_index()
    copies = copy_columns(codes_ref, held, sems, half)
    gain = gain_ref[...]
    shift = shift_ref[...]
    for r in range(0, tokens_ref.shape[1], 16):
        normed, _ = norm_rows(tokens_ref[0, r : r + 16, :].astype(jnp.float32))
        norm_ref[r : r + 16, :] = (normed * gain + shift).astype(jnp.bfloat16)
    scale_columns(copies, held, scales_ref, weight_ref, half)


def first_step(tokens, gain, shift, scales, codes):
    rows = codes.shape[0]
    return pl.pallas_call(
        first_kernel,
        out_shape=(
            jax.ShapeDtypeStruct(tokens.shape[1:], jnp.bfloat16),
            jax.ShapeDtypeStruct((rows, 3 * HALF), jnp.bfloat16),
        ),
        in_specs=[spec(), spec(), spec(), spec(SMEM), spec(pl.ANY)],
        out_specs=(spec(), spec()),
        scratch_shapes=[VMEM((rows, 3 * HALF), codes.dtype), pltpu.SemaphoreType.DMA((3,))],
        name="norm_and_near_weight",
    )(tokens, gain, shift, scales, codes)


def second_kernel(
    grad_ref, layer_ref, out_scales_ref, out_codes_ref, scales_ref, codes_ref,
    near_ref, far_ref, weight_ref, held, sems, scaled, out_weight
):
    half = half_index()
    other = 1 - half
    copies = copy_columns(codes_ref, held, sems, other)
    scaled[...] = (grad_ref[0].astype(jnp.float32) * layer_ref[...]).astype(jnp.bfloat16)
    width = grad_ref.shape[2]
    for out_ref, which in ((far_ref, other), (near_ref, half)):
        for r in range(HALF // QBLOCK):
            first = pl.multiple_of(which * HALF + r * QBLOCK, QBLOCK)
            for c in range(width // QBLOCK):
                scale = out_scales_ref[which * (HALF // QBLOCK) + r, c]
                cols = slice(c * QBLOCK, (c + 1) * QBLOCK)
                out_weight[r * QBLOCK : (r + 1) * QBLOCK, cols] = (
                    out_codes_ref[pl.ds(first, QBLOCK), cols].astype(jnp.float32) * scale
                ).astype(jnp.bfloat16)
        out_ref[...] = lax.dot_general(
            scaled[...], out_weight[...], (((1,), (1,)), ((), ())), preferred_element_type=jnp.float32
        ).astype(jnp.bfloat16)
    scale_columns(copies, held, scales_ref, weight_ref, other)


def second_step(grad, layer_scale, out_scales, out_codes, scales, codes):
    rows = codes.shape[0]
    tokens, width = grad.shape[1:]
    return pl.pallas_call(
        second_kernel,
        out_shape=(
            jax.ShapeDtypeStruct((tokens, HALF), jnp.bfloat16),
            jax.ShapeDtypeStruct((tokens, HALF), jnp.bfloat16),
            jax.ShapeDtypeStruct((rows, 3 * HALF), jnp.bfloat16),
        ),
        in_specs=[spec(), spec(), spec(SMEM), spec(), spec(SMEM), spec(pl.ANY)],
        out_specs=(spec(), spec(), spec()),
        scratch_shapes=[
            VMEM((rows, 3 * HALF), codes.dtype),
            pltpu.SemaphoreType.DMA((3,)),
            VMEM((tokens, width), jnp.bfloat16),
            VMEM((HALF, width), jnp.bfloat16),
        ],
        name="head_grads_and_far_weight",
    )(grad, layer_scale, out_scales, out_codes, scales, codes)


def dot_last(a, b):
    return lax.dot_general(a, b, (((1,), (1,)), ((), ())), preferred_element_type=jnp.float32)


def dot_plain(a, b):
    return jnp.dot(a, b, preferred_element_type=jnp.float32)


def attention_kernel(*refs):
    norms, weights, grads = refs[0:4], refs[4:8], refs[8:12]
    bias_ref = refs[12]
    outs = refs[13:17]
    proj = refs[17]
    mine = lax.axis_index("weight")
    half = half_index()
    depth = weights[0].shape[0]
    tokens = norms[0].shape[0]
    total = tokens * len(norms)

    rows = []
    for norm_ref in norms:
        rows.append(
            jnp.concatenate(
                [
                    norm_ref[:, pl.ds(pl.multiple_of((mine ^ j) * depth, QBLOCK), depth)]
                    for j in range(len(weights))
                ],
                axis=1,
            )
        )
    rows = jnp.concatenate(rows, axis=0)
    for part in range(3):
        columns = jnp.concatenate([w[:, part * HALF : (part + 1) * HALF] for w in weights], axis=0)
        bias = bias_ref[:, pl.ds(pl.multiple_of(part * HD + half * HALF, QBLOCK), HALF)]
        value = (dot_plain(rows, columns) + bias).astype(jnp.bfloat16)
        if part == 0:
            value = value * jnp.bfloat16(HEAD_DIM**-0.5)
        proj[:, part * HALF : (part + 1) * HALF] = value

    pair = 2 * HEAD_DIM
    low = lax.broadcasted_iota(jnp.int32, (total, pair), 1) < HEAD_DIM
    zero = jnp.zeros((total, pair), jnp.bfloat16)
    step = 256
    for t in range(HALF // pair):
        query = proj[:, t * pair : (t + 1) * pair]
        key = proj[:, HALF + t * pair : HALF + (t + 1) * pair]
        value = proj[:, 2 * HALF + t * pair : 2 * HALF + (t + 1) * pair]
        grad = jnp.concatenate([g[:, t * pair : (t + 1) * pair] for g in grads], axis=0)
        key_t = key.T
        key_grad = jnp.zeros((total, pair), jnp.float32)
        value_grad = jnp.zeros((total, pair), jnp.float32)
        query_grad_t = []
        for side in range(2):
            mask = low if side == 0 else ~low
            key_m = jnp.where(mask, key, zero)
            value_m = jnp.where(mask, value, zero)
            query_m = jnp.where(mask, query, zero)
            grad_m = jnp.where(mask, grad, zero)
            blocks = []
            for first in range(0, total, step):
                at = slice(first, first + step)
                scores = dot_last(key_m, query[at])
                dprob = dot_last(value_m, grad[at])
                expo = jnp.exp(scores - jnp.max(scores, axis=0, keepdims=True))
                scale = 1.0 / jnp.sum(expo, axis=0, keepdims=True)
                delta = jnp.sum(expo * dprob, axis=0, keepdims=True) * scale
                prob = expo * scale
                dscore = (prob * (dprob - delta)).astype(jnp.bfloat16)
                key_grad += dot_plain(dscore, query_m[at])
                value_grad += dot_plain(prob.astype(jnp.bfloat16), grad_m[at])
                blocks.append(dot_plain(key_t[side * HEAD_DIM : (side + 1) * HEAD_DIM], dscore))
            query_grad_t.append(jnp.concatenate(blocks, axis=1))
        query_grad = jnp.concatenate(query_grad_t, axis=0).T * HEAD_DIM**-0.5
        for part, piece in enumerate((query_grad, key_grad, value_grad)):
            piece = piece.astype(jnp.bfloat16)
            for i, out in enumerate(outs):
                out[:, part * HALF + t * pair : part * HALF + (t + 1) * pair] = piece[
                    i * tokens : (i + 1) * tokens
                ]


def attention_step(norms, weights, grads, bias):
    tokens = norms[0].shape[0]
    return pl.pallas_call(
        attention_kernel,
        out_shape=tuple(jax.ShapeDtypeStruct((tokens, 3 * HALF), jnp.bfloat16) for _ in norms),
        in_specs=[spec()] * 13,
        out_specs=(spec(),) * 4,
        scratch_shapes=[VMEM((tokens * len(norms), 3 * HALF), jnp.bfloat16)],
        compiler_params=pltpu.CompilerParams(vmem_limit_bytes=40 * 2**20),
        name="attention",
    )(*norms, *weights, *grads, bias)


def last_kernel(*refs):
    near_w, far_w = refs[0:4], refs[4:8]
    own_ref, back_ref, cross_ref, skip_ref, tokens_ref, gain_ref, out_ref, grad_norm = refs[8:]
    mine = lax.axis_index("weight")
    place = lax.axis_index("seq")
    middle = (place == 1) | (place == 2)
    near = jnp.where(middle, own_ref[...], back_ref[...])
    far = jnp.where(middle, cross_ref[...], skip_ref[...])
    depth = near_w[0].shape[0]
    for j in range(4):
        value = dot_last(near, near_w[j][...]) + dot_last(far, far_w[j][...])
        grad_norm[:, pl.ds(pl.multiple_of((mine ^ j) * depth, QBLOCK), depth)] = value
    gain = gain_ref[...]
    for r in range(0, tokens_ref.shape[1], 16):
        normed, inverse = norm_rows(tokens_ref[0, r : r + 16, :].astype(jnp.float32))
        grad_hat = grad_norm[r : r + 16, :] * gain
        first_mean = jnp.mean(grad_hat, axis=-1, keepdims=True)
        second_mean = jnp.mean(grad_hat * normed, axis=-1, keepdims=True)
        out_ref[0, r : r + 16, :] = inverse * (grad_hat - first_mean - normed * second_mean)


def last_step(near_w, far_w, own, back, cross, skip, tokens, gain):
    return pl.pallas_call(
        last_kernel,
        out_shape=jax.ShapeDtypeStruct(tokens.shape, jnp.float32),
        in_specs=[spec()] * 14,
        out_specs=spec(),
        scratch_shapes=[VMEM(tokens.shape[1:], jnp.float32)],
        compiler_params=pltpu.CompilerParams(vmem_limit_bytes=40 * 2**20),
        name="input_grad",
    )(*near_w, *far_w, own, back, cross, skip, tokens, gain)


END_TO_MIDDLE = [(0, 1), (3, 2)]
MIDDLE = [(1, 2), (2, 1)]
END_TO_FAR = [(0, 2), (3, 1)]
MIDDLE_TO_END = [(1, 0), (2, 3)]
FAR_TO_END = [(1, 3), (2, 0)]


def flip(bit):
    return [(i, i ^ bit) for i in range(4)]


def spread_weight(mine):
    across = lax.ppermute(mine, "weight", flip(2))
    beside = lax.ppermute(mine, "weight", flip(1))
    diagonal = lax.ppermute(across, "weight", flip(1))
    return (mine, beside, across, diagonal)


def local_middle(
    tokens,
    upstream_grad,
    norm_gain,
    norm_bias,
    input_codes,
    input_scales,
    input_bias,
    output_codes,
    output_scales,
    layer_scale,
):
    gain = norm_gain[None]
    norm_out, near_mine = first_step(tokens, gain, norm_bias[None], input_scales, input_codes)
    near_w = spread_weight(near_mine)
    norm_far = lax.ppermute(norm_out, "seq", END_TO_FAR)
    norm_mid = lax.ppermute(norm_out, "seq", MIDDLE)
    norm_end = lax.ppermute(norm_out, "seq", END_TO_MIDDLE)
    grad_near, grad_far, far_mine = second_step(
        upstream_grad, layer_scale[None], output_scales, output_codes, input_scales, input_codes
    )
    head_far = lax.ppermute(grad_far, "seq", END_TO_FAR)
    head_mid = lax.ppermute(grad_far, "seq", MIDDLE)
    head_end = lax.ppermute(grad_near, "seq", END_TO_MIDDLE)
    own, end, mid, far = attention_step(
        (norm_out, norm_end, norm_mid, norm_far),
        near_w,
        (grad_near, head_end, head_mid, head_far),
        input_bias[None],
    )
    far_mine, _ = lax.optimization_barrier((far_mine, near_w[2]))
    far_w = spread_weight(far_mine)
    skip = lax.ppermute(far, "seq", FAR_TO_END)
    cross = lax.ppermute(mid, "seq", MIDDLE)
    back = lax.ppermute(end, "seq", MIDDLE_TO_END)
    return last_step(near_w, far_w, own, back, cross, skip, tokens, gain)


def dequantize(codes, scales):
    expanded = jnp.repeat(jnp.repeat(scales, QBLOCK, axis=0), QBLOCK, axis=1)
    return (codes.astype(jnp.float32) * expanded).astype(jnp.bfloat16)


def normalize(rows, gain, shift):
    mean_value = jnp.mean(rows, axis=-1, keepdims=True)
    centered = rows - mean_value
    variance = jnp.mean(centered * centered, axis=-1, keepdims=True)
    inverse = lax.rsqrt(variance + 1e-06)
    normed = centered * inverse
    return (normed, inverse, (normed * gain + shift).astype(jnp.bfloat16))


def norm_backward(grad_norm, normed, inverse, gain):
    grad_hat = grad_norm * gain
    first_mean = jnp.mean(grad_hat, axis=-1, keepdims=True)
    second_mean = jnp.mean(grad_hat * normed, axis=-1, keepdims=True)
    return inverse * (grad_hat - first_mean - normed * second_mean)


def score_block(queries, head_grads, pair_block):
    row_count = pair_block.shape[0]
    keys_blk = pair_block[:, :HD].reshape(row_count, HEADS, HEAD_DIM)
    values_blk = pair_block[:, HD:].reshape(row_count, HEADS, HEAD_DIM)
    scores = jnp.einsum(
        "qhd,khd->hqk", queries, keys_blk, preferred_element_type=jnp.float32
    ) * HEAD_DIM ** (-0.5)
    dprob = jnp.einsum("qhd,khd->hqk", head_grads, values_blk, preferred_element_type=jnp.float32)
    return (keys_blk, scores, dprob)


def update_stats(statistics, queries, head_grads, pair_rows):
    sub_size = math.gcd(pair_rows.shape[0], 512)

    def visit_block(block_index, running):
        run_max, run_total, run_mix = running
        pair_block = lax.dynamic_slice_in_dim(pair_rows, block_index * sub_size, sub_size, 0)
        keys_blk, scores, dprob = score_block(queries, head_grads, pair_block)
        new_max = jnp.maximum(run_max, jnp.max(scores, axis=-1))
        factor = jnp.exp(run_max - new_max)
        expo = jnp.exp(scores - new_max[..., None])
        return (
            new_max,
            run_total * factor + jnp.sum(expo, axis=-1),
            run_mix * factor + jnp.sum(expo * dprob, axis=-1),
        )

    return lax.fori_loop(0, pair_rows.shape[0] // sub_size, visit_block, statistics)


def block_backward(queries, head_grads, pair_block, log_total, row_delta):
    keys_blk, scores, dprob = score_block(queries, head_grads, pair_block)
    weights = jnp.exp(scores - log_total[..., None])
    prob_weights = weights.astype(jnp.bfloat16)
    dscore = (weights * (dprob - row_delta[..., None])).astype(jnp.bfloat16)
    return (keys_blk, prob_weights, dscore)


def key_terms_from(queries, head_grads, prob_weights, dscore):
    key_part = jnp.einsum(
        "hqk,qhd->khd", dscore, queries, preferred_element_type=jnp.float32
    ) * HEAD_DIM ** (-0.5)
    value_part = jnp.einsum(
        "hqk,qhd->khd", prob_weights, head_grads, preferred_element_type=jnp.float32
    )
    row_count = key_part.shape[0]
    return jnp.concatenate(
        [key_part.reshape(row_count, HD), value_part.reshape(row_count, HD)], axis=1
    )


def query_side(queries, head_grads, keys_values, local_rows):
    seq_rows = local_rows * lax.axis_size("seq")
    start_stats = (
        jnp.full((HEADS, local_rows), -1e30, jnp.float32),
        jnp.zeros((HEADS, local_rows), jnp.float32),
        jnp.zeros((HEADS, local_rows), jnp.float32),
    )
    all_pairs = lax.all_gather(keys_values, "seq", axis=0, tiled=True)
    statistics = update_stats(start_stats, queries, head_grads, all_pairs)
    row_max, row_total, row_mix = statistics
    log_total = row_max + jnp.log(row_total)
    row_delta = row_mix / row_total
    sub_size = math.gcd(seq_rows, 512)
    block_count = seq_rows // sub_size
    empty_query = jnp.zeros((local_rows, HEADS, HEAD_DIM), jnp.float32)

    def backward_step(block_index, running):
        query_grad, buffer = running
        pair_block = lax.dynamic_slice_in_dim(all_pairs, block_index * sub_size, sub_size, 0)
        keys_blk, prob_weights, dscore = block_backward(
            queries, head_grads, pair_block, log_total, row_delta
        )
        query_grad = query_grad + jnp.einsum(
            "hqk,khd->qhd", dscore, keys_blk, preferred_element_type=jnp.float32
        )
        block_terms = key_terms_from(queries, head_grads, prob_weights, dscore)
        buffer = lax.dynamic_update_slice_in_dim(buffer, block_terms, block_index * sub_size, 0)
        return (query_grad, buffer)

    empty_terms = jnp.zeros((seq_rows, 2 * HD), jnp.float32)
    query_grad, buffer = lax.fori_loop(0, block_count, backward_step, (empty_query, empty_terms))
    pair_grads = lax.psum_scatter(
        buffer.astype(jnp.bfloat16), "seq", scatter_dimension=0, tiled=True
    ).astype(jnp.float32)
    return (query_grad, pair_grads)


def local(
    tokens,
    upstream_grad,
    norm_gain,
    norm_bias,
    input_codes,
    input_scales,
    input_bias,
    output_codes,
    output_scales,
    layer_scale,
):
    all_codes, all_scales = (
        lax.all_gather(input_codes.astype(jnp.float32), "weight", axis=0, tiled=True).astype(
            input_codes.dtype
        ),
        lax.all_gather(input_scales, "weight", axis=0, tiled=True),
    )
    input_weight = dequantize(all_codes, all_scales)
    output_weight = dequantize(output_codes, output_scales)
    normed, inverse, norm_out = normalize(tokens[0].astype(jnp.float32), norm_gain, norm_bias)
    projected = (
        jnp.dot(norm_out, input_weight, preferred_element_type=jnp.float32) + input_bias
    ).astype(jnp.bfloat16)
    local_rows = projected.shape[0]
    queries = projected[:, :HD].reshape(local_rows, HEADS, HEAD_DIM)
    keys_values = projected[:, HD:]
    scaled_grad = (upstream_grad[0].astype(jnp.float32) * layer_scale).astype(jnp.bfloat16)
    head_grads = jnp.dot(scaled_grad, output_weight.T, preferred_element_type=jnp.float32).astype(
        jnp.bfloat16
    )
    head_grads = head_grads.reshape(local_rows, HEADS, HEAD_DIM)
    query_grad, pair_grads = query_side(queries, head_grads, keys_values, local_rows)
    query_grad = (query_grad * HEAD_DIM ** (-0.5)).reshape(local_rows, HD)
    grad_proj = jnp.concatenate([query_grad, pair_grads], axis=1).astype(jnp.bfloat16)
    grad_norm = jnp.dot(grad_proj, input_weight.T, preferred_element_type=jnp.float32)
    result = norm_backward(grad_norm, normed, inverse, norm_gain)
    return result[None]


def solution(mesh):
    in_specs = (
        P(("groups", "weight"), "seq", None),
        P(("groups", "weight"), "seq", None),
        P(),
        P(),
        P("weight", None),
        P("weight", None),
        P(),
        P(),
        P(),
        P(),
    )
    out_specs = P(("groups", "weight"), "seq", None)
    fits = mesh.shape["seq"] == 4 and mesh.shape["weight"] == 4
    plan = local_middle if fits else local
    return jax.shard_map(plan, mesh=mesh, in_specs=in_specs, out_specs=out_specs, check_vma=False)
```

```python
import functools
import math

import jax
import jax.numpy as jnp
from jax import lax
from jax.experimental import pallas as pl
from jax.experimental.pallas import tpu as pltpu
from jax.sharding import PartitionSpec as P

HEADS = 12
HEAD_DIM = 64
QBLOCK = 128
HD = 768
HALF = HD // 2
EPSILON = 1e-06
VMEM = pltpu.VMEM
SMEM = pltpu.SMEM


def half_index():
    return lax.axis_index("seq") * 2 // lax.axis_size("seq")


def cost(micros):
    return pl.CostEstimate(flops=int(micros * 1.0e9), bytes_accessed=int(micros * 3.0e6), transcendentals=0)


def spec(memory_space=VMEM):
    return pl.BlockSpec(memory_space=memory_space)


def norm_rows(rows):
    mean_value = jnp.mean(rows, axis=-1, keepdims=True)
    centered = rows - mean_value
    variance = jnp.mean(centered * centered, axis=-1, keepdims=True)
    inverse = lax.rsqrt(variance + EPSILON)
    return centered * inverse, inverse


def row_vector(ref):
    return ref[...].reshape(1, ref.shape[0])


def scale_block(codes, scale):
    return (codes.astype(jnp.float32) * scale).astype(jnp.bfloat16)


def first_kernel(
    tokens_ref, gain_ref, shift_ref, scales_ref, codes_ref, grad_ref, layer_ref, out_scales_ref, out_codes_ref,
    weight_out, near_out, far_out,
    tokens, gain, shift, scales, codes, grad, layer, out_scales, out_codes, scaled, weight, sems
):
    half = half_index()
    other = 1 - half
    blocks = HALF // QBLOCK

    def copy(source, target, at):
        started = pltpu.make_async_copy(source, target, sems.at[at])
        started.start()
        return started

    def columns(part):
        return codes_ref.at[:, pl.ds(pl.multiple_of(part * HD + half * HALF, QBLOCK), HALF)]

    def rows(which):
        return out_codes_ref.at[pl.ds(pl.multiple_of(which * HALF, QBLOCK), HALF), :]

    scales_copy = copy(scales_ref, scales, 0)
    codes_copies = [copy(columns(part), codes.at[part], 1 + part) for part in range(3)]
    tokens_copies = [
        copy(tokens_ref, tokens, 4), copy(gain_ref, gain, 5), copy(shift_ref, shift, 6)
    ]
    grad_copies = [
        copy(grad_ref, grad, 7), copy(layer_ref, layer, 8), copy(out_scales_ref, out_scales, 9)
    ]
    out_copies = [copy(rows(other), out_codes.at[0], 10), copy(rows(half), out_codes.at[1], 11)]

    scales_copy.wait()
    for part in range(3):
        codes_copies[part].wait()
        for r in range(codes_ref.shape[0] // QBLOCK):
            for c in range(blocks):
                scale = scales[r, (part * HD) // QBLOCK + half * blocks + c]
                lines = slice(r * QBLOCK, (r + 1) * QBLOCK)
                weight_out[lines, part * HALF + c * QBLOCK : part * HALF + (c + 1) * QBLOCK] = scale_block(
                    codes[part, lines, c * QBLOCK : (c + 1) * QBLOCK], scale
                )

    for started in tokens_copies:
        started.wait()
    width = tokens.shape[2]
    gain_row = row_vector(gain)
    shift_row = row_vector(shift)
    for r in range(0, tokens.shape[1], 16):
        normed, _ = norm_rows(tokens[0, r : r + 16, :].astype(jnp.float32))
        norm_out = (normed * gain_row + shift_row).astype(jnp.bfloat16)
        near_out[r : r + 16, :width] = norm_out
        far_out[r : r + 16, :width] = norm_out

    for started in grad_copies:
        started.wait()
    scaled[...] = (grad[0].astype(jnp.float32) * row_vector(layer)).astype(jnp.bfloat16)
    for i, (out_ref, which) in enumerate(((far_out, other), (near_out, half))):
        out_copies[i].wait()
        for r in range(blocks):
            lines = slice(r * QBLOCK, (r + 1) * QBLOCK)
            for c in range(width // QBLOCK):
                at = slice(c * QBLOCK, (c + 1) * QBLOCK)
                weight[lines, at] = scale_block(out_codes[i, lines, at], out_scales[which * blocks + r, c])
        out_ref[:, width:] = dot_last(scaled[...], weight[...]).astype(jnp.bfloat16)


def first_step(tokens, gain, shift, scales, codes, grad, layer_scale, out_scales, out_codes):
    lines, width = tokens.shape[1:]
    depth = codes.shape[0]
    both = jax.ShapeDtypeStruct((lines, width + HALF), jnp.bfloat16)
    return pl.pallas_call(
        first_kernel,
        out_shape=(jax.ShapeDtypeStruct((depth, 3 * HALF), jnp.bfloat16), both, both),
        in_specs=[spec(pltpu.HBM)] * 9,
        out_specs=(spec(),) * 3,
        scratch_shapes=[
            VMEM(tokens.shape, tokens.dtype),
            VMEM(gain.shape, gain.dtype),
            VMEM(shift.shape, shift.dtype),
            SMEM(scales.shape, scales.dtype),
            VMEM((3, depth, HALF), codes.dtype),
            VMEM(grad.shape, grad.dtype),
            VMEM(layer_scale.shape, layer_scale.dtype),
            SMEM(out_scales.shape, out_scales.dtype),
            VMEM((2, HALF, width), out_codes.dtype),
            VMEM((lines, width), jnp.bfloat16),
            VMEM((HALF, width), jnp.bfloat16),
            pltpu.SemaphoreType.DMA((12,)),
        ],
        compiler_params=pltpu.CompilerParams(vmem_limit_bytes=60 * 2**20),
        cost_estimate=cost(3),
        name="first_weights_and_rows",
    )(tokens, gain, shift, scales, codes, grad, layer_scale, out_scales, out_codes)


def far_kernel(scales_ref, codes_ref, after_ref, weight_out, scales, codes, sems):
    other = 1 - half_index()
    blocks = HALF // QBLOCK
    copies = [pltpu.make_async_copy(scales_ref, scales, sems.at[3])]
    for part in range(3):
        at = pl.ds(pl.multiple_of(part * HD + other * HALF, QBLOCK), HALF)
        copies.append(pltpu.make_async_copy(codes_ref.at[:, at], codes.at[part], sems.at[part]))
    for started in copies:
        started.start()
    for started in copies:
        started.wait()
    for part in range(3):
        for r in range(codes_ref.shape[0] // QBLOCK):
            for c in range(blocks):
                scale = scales[r, (part * HD) // QBLOCK + other * blocks + c]
                lines = slice(r * QBLOCK, (r + 1) * QBLOCK)
                weight_out[lines, part * HALF + c * QBLOCK : part * HALF + (c + 1) * QBLOCK] = scale_block(
                    codes[part, lines, c * QBLOCK : (c + 1) * QBLOCK], scale
                )


def far_step(scales, codes, after):
    depth = codes.shape[0]
    return pl.pallas_call(
        far_kernel,
        out_shape=jax.ShapeDtypeStruct((depth, 3 * HALF), jnp.bfloat16),
        in_specs=[spec(pltpu.HBM), spec(pltpu.HBM), spec()],
        out_specs=spec(),
        scratch_shapes=[
            SMEM(scales.shape, scales.dtype),
            VMEM((3, depth, HALF), codes.dtype),
            pltpu.SemaphoreType.DMA((4,)),
        ],
        compiler_params=pltpu.CompilerParams(vmem_limit_bytes=16 * 2**20),
        cost_estimate=cost(0.01),
        name="far_weight",
    )(scales, codes, after)


def dot_last(a, b):
    return lax.dot_general(a, b, (((1,), (1,)), ((), ())), preferred_element_type=jnp.float32)


def dot_plain(a, b):
    return jnp.dot(a, b, preferred_element_type=jnp.float32)


def norm_columns(norms, picks, depth):
    mine = lax.axis_index("weight")
    return jnp.concatenate(
        [
            jnp.concatenate(
                [norm_ref[:, pl.ds(pl.multiple_of((mine ^ j) * depth, QBLOCK), depth)] for j in picks],
                axis=1,
            )
            for norm_ref in norms
        ],
        axis=0,
    )


def project_kernel(*refs):
    norms, weights, sums = refs[0:4], refs[4:7], refs[7]
    rows = norm_columns(norms, range(3), weights[0].shape[0])
    for part in range(3):
        columns = jnp.concatenate([w[:, part * HALF : (part + 1) * HALF] for w in weights], axis=0)
        sums[:, part * HALF : (part + 1) * HALF] = dot_plain(rows, columns)


def project_step(norms, weights):
    tokens = norms[0].shape[0]
    return pl.pallas_call(
        project_kernel,
        out_shape=jax.ShapeDtypeStruct((tokens * len(norms), 3 * HALF), jnp.float32),
        in_specs=[spec()] * 7,
        out_specs=spec(),
        compiler_params=pltpu.CompilerParams(vmem_limit_bytes=24 * 2**20),
        cost_estimate=cost(6),
        name="projection_part",
    )(*norms, *weights)


def finish_kernel(*refs):
    norms = refs[0:4]
    weight, sums, bias_ref, proj = refs[4:]
    half = half_index()
    rows = norm_columns(norms, (3,), weight.shape[0])
    bias = row_vector(bias_ref)
    for part in range(3):
        at = slice(part * HALF, (part + 1) * HALF)
        shift = jnp.where(
            half == 0,
            bias[:, part * HD : part * HD + HALF],
            bias[:, part * HD + HALF : (part + 1) * HD],
        )
        value = (sums[:, at] + dot_plain(rows, weight[:, at]) + shift).astype(jnp.bfloat16)
        if part == 0:
            value = value * jnp.bfloat16(HEAD_DIM**-0.5)
        proj[:, at] = value


def finish_step(norms, weight, sums, bias):
    return pl.pallas_call(
        finish_kernel,
        out_shape=jax.ShapeDtypeStruct(sums.shape, jnp.bfloat16),
        in_specs=[spec()] * 7,
        out_specs=spec(),
        compiler_params=pltpu.CompilerParams(vmem_limit_bytes=24 * 2**20),
        cost_estimate=cost(0.01),
        name="projection",
    )(*norms, weight, sums, bias)


PAIR = 2 * HEAD_DIM


def attention_kernel(pairs, *refs):
    proj, grads, outs = refs[0], refs[1:5], refs[-4:]
    total = proj.shape[0]
    tokens = grads[0].shape[0]
    low = lax.broadcasted_iota(jnp.int32, (total, PAIR), 1) < HEAD_DIM
    zero = jnp.zeros((total, PAIR), jnp.bfloat16)
    for place, t in enumerate(pairs):
        query = proj[:, t * PAIR : (t + 1) * PAIR]
        key = proj[:, HALF + t * PAIR : HALF + (t + 1) * PAIR]
        value = proj[:, 2 * HALF + t * PAIR : 2 * HALF + (t + 1) * PAIR]
        grad = jnp.concatenate(
            [g[:, g.shape[1] - HALF + t * PAIR : g.shape[1] - HALF + (t + 1) * PAIR] for g in grads], axis=0
        )
        key_t = key.T
        key_grad = value_grad = None
        query_grad = []
        for side in range(2):
            mask = low if side == 0 else ~low
            scores = dot_last(jnp.where(mask, key, zero), query)
            dprob = dot_last(jnp.where(mask, value, zero), grad)
            expo = jnp.exp(scores - jnp.max(scores, axis=0, keepdims=True))
            scale = 1.0 / jnp.sum(expo, axis=0, keepdims=True)
            delta = jnp.sum(expo * dprob, axis=0, keepdims=True) * scale
            prob = expo * scale
            dscore = (prob * (dprob - delta)).astype(jnp.bfloat16)
            key_part = dot_plain(dscore, jnp.where(mask, query, zero))
            value_part = dot_plain(prob.astype(jnp.bfloat16), jnp.where(mask, grad, zero))
            key_grad = key_part if side == 0 else key_grad + key_part
            value_grad = value_part if side == 0 else value_grad + value_part
            query_grad.append(dot_plain(key_t[side * HEAD_DIM : (side + 1) * HEAD_DIM], dscore))
        query_grad = jnp.concatenate(query_grad, axis=0).T * HEAD_DIM**-0.5
        for part, piece in enumerate((query_grad, key_grad, value_grad)):
            piece = piece.astype(jnp.bfloat16)
            first = (part * len(pairs) + place) * PAIR
            for i, out in enumerate(outs):
                out[:, first : first + PAIR] = piece[i * tokens : (i + 1) * tokens]


def attention_step(proj, grads, pairs, *after):
    tokens = grads[0].shape[0]
    out = jax.ShapeDtypeStruct((tokens, 3 * len(pairs) * PAIR), jnp.bfloat16)
    return pl.pallas_call(
        functools.partial(attention_kernel, pairs),
        out_shape=(out,) * 4,
        in_specs=[spec()] * 5 + [spec()] * len(after),
        out_specs=(spec(),) * 4,
        compiler_params=pltpu.CompilerParams(vmem_limit_bytes=24 * 2**20),
        cost_estimate=cost(12),
        name="attention",
    )(proj, *grads, *after)


def pick_grads(own_ref, back_ref, cross_ref, skip_ref):
    place = lax.axis_index("seq")
    middle = (place == 1) | (place == 2)
    return (
        jnp.where(middle, own_ref[...], back_ref[...]),
        jnp.where(middle, cross_ref[...], skip_ref[...]),
    )


def part_kernel(*refs):
    near_w, far_w, sums = refs[0:4], refs[4:7], refs[-1]
    near, far = pick_grads(*refs[7:11])
    mine = lax.axis_index("weight")
    depth = near_w[0].shape[0]
    for j in range(4):
        value = dot_last(near, near_w[j][...])
        if j < len(far_w):
            value += dot_last(far, far_w[j][...])
        sums[:, pl.ds(pl.multiple_of((mine ^ j) * depth, QBLOCK), depth)] = value


def part_step(near_w, far_w, pieces):
    rows = pieces[0].shape[0]
    return pl.pallas_call(
        part_kernel,
        out_shape=jax.ShapeDtypeStruct((rows, 4 * near_w[0].shape[0]), jnp.float32),
        in_specs=[spec()] * 11,
        out_specs=spec(),
        compiler_params=pltpu.CompilerParams(vmem_limit_bytes=24 * 2**20),
        cost_estimate=cost(6),
        name="grad_norm_part",
    )(*near_w, *far_w, *pieces)


def last_kernel(far_w, *refs):
    sums, tokens_ref, gain_ref, out_ref, grad_norm = refs[4:]
    _, far = pick_grads(*refs[0:4])
    depth = far_w.shape[0]
    at = pl.ds(pl.multiple_of((lax.axis_index("weight") ^ 3) * depth, QBLOCK), depth)
    grad_norm[...] = sums[...]
    grad_norm[:, at] += dot_last(far, far_w[...])
    gain = row_vector(gain_ref)
    for r in range(0, tokens_ref.shape[1], 16):
        normed, inverse = norm_rows(tokens_ref[0, r : r + 16, :].astype(jnp.float32))
        grad_hat = grad_norm[r : r + 16, :] * gain
        first_mean = jnp.mean(grad_hat, axis=-1, keepdims=True)
        second_mean = jnp.mean(grad_hat * normed, axis=-1, keepdims=True)
        out_ref[0, r : r + 16, :] = inverse * (grad_hat - first_mean - normed * second_mean)


def last_step(far_w, pieces, sums, tokens, gain):
    return pl.pallas_call(
        last_kernel,
        out_shape=jax.ShapeDtypeStruct(tokens.shape, jnp.float32),
        in_specs=[spec()] * 8,
        out_specs=spec(),
        scratch_shapes=[VMEM(tokens.shape[1:], jnp.float32)],
        compiler_params=pltpu.CompilerParams(vmem_limit_bytes=24 * 2**20),
        cost_estimate=cost(2),
        name="input_grad",
    )(far_w, *pieces, sums, tokens, gain)


def pass_kernel(value_ref, *refs):
    refs[-1][...] = value_ref[...]


def pass_after(value, *after):
    return pl.pallas_call(
        pass_kernel,
        out_shape=jax.ShapeDtypeStruct(value.shape, value.dtype),
        in_specs=[spec()] * (1 + len(after)),
        out_specs=spec(),
        input_output_aliases={0: 0},
        compiler_params=pltpu.CompilerParams(vmem_limit_bytes=16 * 2**20),
        cost_estimate=cost(0.01),
        name="pass_after",
    )(value, *after)


END_TO_MIDDLE = [(0, 1), (3, 2)]
MIDDLE = [(1, 2), (2, 1)]
END_TO_FAR = [(0, 2), (3, 1)]
MIDDLE_TO_END = [(1, 0), (2, 3)]
FAR_TO_END = [(1, 3), (2, 0)]


def flip(bit):
    return [(i, i ^ bit) for i in range(4)]


def local_middle(
    tokens,
    upstream_grad,
    norm_gain,
    norm_bias,
    input_codes,
    input_scales,
    input_bias,
    output_codes,
    output_scales,
    layer_scale,
):
    near, both_near, both_other = first_step(
        tokens, norm_gain, norm_bias, input_scales, input_codes, upstream_grad, layer_scale, output_scales, output_codes
    )
    both_mid = lax.ppermute(both_other, "seq", MIDDLE)
    both_far = lax.ppermute(both_other, "seq", END_TO_FAR)
    both_end = lax.ppermute(both_near, "seq", END_TO_MIDDLE)
    near_across = lax.ppermute(near, "weight", flip(2))
    near_beside = lax.ppermute(near, "weight", flip(1))
    near_diagonal = lax.ppermute(near_across, "weight", flip(1))
    far = far_step(input_scales, input_codes, near_across)
    far_across = lax.ppermute(far, "weight", flip(2))
    far_beside = lax.ppermute(far, "weight", flip(1))
    rows = (both_near, both_end, both_mid, both_far)
    sums = project_step(rows, (near, near_beside, near_across))
    proj = finish_step(rows, near_diagonal, sums, input_bias)
    own, end, mid, skip = attention_step(proj, rows, (0, 1, 2))
    skip = lax.ppermute(skip, "seq", FAR_TO_END)
    cross = lax.ppermute(mid, "seq", MIDDLE)
    back = lax.ppermute(end, "seq", MIDDLE_TO_END)
    pieces = (own, back, cross, skip)
    far_across = pass_after(far_across, cross, skip, back)
    far_diagonal = lax.ppermute(far_across, "weight", flip(1))
    near_w = (near, near_beside, near_across, near_diagonal)
    sums = part_step(near_w, (far, far_beside, far_across), pieces)
    return last_step(far_diagonal, pieces, sums, tokens, norm_gain)


def dequantize(codes, scales):
    expanded = jnp.repeat(jnp.repeat(scales, QBLOCK, axis=0), QBLOCK, axis=1)
    return (codes.astype(jnp.float32) * expanded).astype(jnp.bfloat16)


def normalize(rows, gain, shift):
    mean_value = jnp.mean(rows, axis=-1, keepdims=True)
    centered = rows - mean_value
    variance = jnp.mean(centered * centered, axis=-1, keepdims=True)
    inverse = lax.rsqrt(variance + 1e-06)
    normed = centered * inverse
    return (normed, inverse, (normed * gain + shift).astype(jnp.bfloat16))


def norm_backward(grad_norm, normed, inverse, gain):
    grad_hat = grad_norm * gain
    first_mean = jnp.mean(grad_hat, axis=-1, keepdims=True)
    second_mean = jnp.mean(grad_hat * normed, axis=-1, keepdims=True)
    return inverse * (grad_hat - first_mean - normed * second_mean)


def score_block(queries, head_grads, pair_block):
    row_count = pair_block.shape[0]
    keys_blk = pair_block[:, :HD].reshape(row_count, HEADS, HEAD_DIM)
    values_blk = pair_block[:, HD:].reshape(row_count, HEADS, HEAD_DIM)
    scores = jnp.einsum(
        "qhd,khd->hqk", queries, keys_blk, preferred_element_type=jnp.float32
    ) * HEAD_DIM ** (-0.5)
    dprob = jnp.einsum("qhd,khd->hqk", head_grads, values_blk, preferred_element_type=jnp.float32)
    return (keys_blk, scores, dprob)


def update_stats(statistics, queries, head_grads, pair_rows):
    sub_size = math.gcd(pair_rows.shape[0], 512)

    def visit_block(block_index, running):
        run_max, run_total, run_mix = running
        pair_block = lax.dynamic_slice_in_dim(pair_rows, block_index * sub_size, sub_size, 0)
        keys_blk, scores, dprob = score_block(queries, head_grads, pair_block)
        new_max = jnp.maximum(run_max, jnp.max(scores, axis=-1))
        factor = jnp.exp(run_max - new_max)
        expo = jnp.exp(scores - new_max[..., None])
        return (
            new_max,
            run_total * factor + jnp.sum(expo, axis=-1),
            run_mix * factor + jnp.sum(expo * dprob, axis=-1),
        )

    return lax.fori_loop(0, pair_rows.shape[0] // sub_size, visit_block, statistics)


def block_backward(queries, head_grads, pair_block, log_total, row_delta):
    keys_blk, scores, dprob = score_block(queries, head_grads, pair_block)
    weights = jnp.exp(scores - log_total[..., None])
    prob_weights = weights.astype(jnp.bfloat16)
    dscore = (weights * (dprob - row_delta[..., None])).astype(jnp.bfloat16)
    return (keys_blk, prob_weights, dscore)


def key_terms_from(queries, head_grads, prob_weights, dscore):
    key_part = jnp.einsum(
        "hqk,qhd->khd", dscore, queries, preferred_element_type=jnp.float32
    ) * HEAD_DIM ** (-0.5)
    value_part = jnp.einsum(
        "hqk,qhd->khd", prob_weights, head_grads, preferred_element_type=jnp.float32
    )
    row_count = key_part.shape[0]
    return jnp.concatenate(
        [key_part.reshape(row_count, HD), value_part.reshape(row_count, HD)], axis=1
    )


def query_side(queries, head_grads, keys_values, local_rows):
    seq_rows = local_rows * lax.axis_size("seq")
    start_stats = (
        jnp.full((HEADS, local_rows), -1e30, jnp.float32),
        jnp.zeros((HEADS, local_rows), jnp.float32),
        jnp.zeros((HEADS, local_rows), jnp.float32),
    )
    all_pairs = lax.all_gather(keys_values, "seq", axis=0, tiled=True)
    statistics = update_stats(start_stats, queries, head_grads, all_pairs)
    row_max, row_total, row_mix = statistics
    log_total = row_max + jnp.log(row_total)
    row_delta = row_mix / row_total
    sub_size = math.gcd(seq_rows, 512)
    block_count = seq_rows // sub_size
    empty_query = jnp.zeros((local_rows, HEADS, HEAD_DIM), jnp.float32)

    def backward_step(block_index, running):
        query_grad, buffer = running
        pair_block = lax.dynamic_slice_in_dim(all_pairs, block_index * sub_size, sub_size, 0)
        keys_blk, prob_weights, dscore = block_backward(
            queries, head_grads, pair_block, log_total, row_delta
        )
        query_grad = query_grad + jnp.einsum(
            "hqk,khd->qhd", dscore, keys_blk, preferred_element_type=jnp.float32
        )
        block_terms = key_terms_from(queries, head_grads, prob_weights, dscore)
        buffer = lax.dynamic_update_slice_in_dim(buffer, block_terms, block_index * sub_size, 0)
        return (query_grad, buffer)

    empty_terms = jnp.zeros((seq_rows, 2 * HD), jnp.float32)
    query_grad, buffer = lax.fori_loop(0, block_count, backward_step, (empty_query, empty_terms))
    pair_grads = lax.psum_scatter(
        buffer.astype(jnp.bfloat16), "seq", scatter_dimension=0, tiled=True
    ).astype(jnp.float32)
    return (query_grad, pair_grads)


def local(
    tokens,
    upstream_grad,
    norm_gain,
    norm_bias,
    input_codes,
    input_scales,
    input_bias,
    output_codes,
    output_scales,
    layer_scale,
):
    all_codes, all_scales = (
        lax.all_gather(input_codes.astype(jnp.float32), "weight", axis=0, tiled=True).astype(
            input_codes.dtype
        ),
        lax.all_gather(input_scales, "weight", axis=0, tiled=True),
    )
    input_weight = dequantize(all_codes, all_scales)
    output_weight = dequantize(output_codes, output_scales)
    normed, inverse, norm_out = normalize(tokens[0].astype(jnp.float32), norm_gain, norm_bias)
    projected = (
        jnp.dot(norm_out, input_weight, preferred_element_type=jnp.float32) + input_bias
    ).astype(jnp.bfloat16)
    local_rows = projected.shape[0]
    queries = projected[:, :HD].reshape(local_rows, HEADS, HEAD_DIM)
    keys_values = projected[:, HD:]
    scaled_grad = (upstream_grad[0].astype(jnp.float32) * layer_scale).astype(jnp.bfloat16)
    head_grads = jnp.dot(scaled_grad, output_weight.T, preferred_element_type=jnp.float32).astype(
        jnp.bfloat16
    )
    head_grads = head_grads.reshape(local_rows, HEADS, HEAD_DIM)
    query_grad, pair_grads = query_side(queries, head_grads, keys_values, local_rows)
    query_grad = (query_grad * HEAD_DIM ** (-0.5)).reshape(local_rows, HD)
    grad_proj = jnp.concatenate([query_grad, pair_grads], axis=1).astype(jnp.bfloat16)
    grad_norm = jnp.dot(grad_proj, input_weight.T, preferred_element_type=jnp.float32)
    result = norm_backward(grad_norm, normed, inverse, norm_gain)
    return result[None]


def solution(mesh):
    in_specs = (
        P(("groups", "weight"), "seq", None),
        P(("groups", "weight"), "seq", None),
        P(),
        P(),
        P("weight", None),
        P("weight", None),
        P(),
        P(),
        P(),
        P(),
    )
    out_specs = P(("groups", "weight"), "seq", None)
    fits = mesh.shape["seq"] == 4 and mesh.shape["weight"] == 4
    plan = local_middle if fits else local
    return jax.shard_map(plan, mesh=mesh, in_specs=in_specs, out_specs=out_specs, check_vma=False)
```

```python
import functools
import math

import jax
import jax.numpy as jnp
from jax import lax
from jax.experimental import pallas as pl
from jax.experimental.pallas import tpu as pltpu
from jax.sharding import PartitionSpec as P

HEADS = 12
HEAD_DIM = 64
QBLOCK = 128
HD = 768
HALF = HD // 2
EPSILON = 1e-06
VMEM = pltpu.VMEM
SMEM = pltpu.SMEM


def half_index():
    return lax.axis_index("seq") * 2 // lax.axis_size("seq")


def cost(micros):
    return pl.CostEstimate(flops=int(micros * 1.0e9), bytes_accessed=int(micros * 3.0e6), transcendentals=0)


def spec(memory_space=VMEM):
    return pl.BlockSpec(memory_space=memory_space)


def norm_rows(rows):
    mean_value = jnp.mean(rows, axis=-1, keepdims=True)
    centered = rows - mean_value
    variance = jnp.mean(centered * centered, axis=-1, keepdims=True)
    inverse = lax.rsqrt(variance + EPSILON)
    return centered * inverse, inverse


def row_vector(ref):
    return ref[...].reshape(1, ref.shape[0])


def scale_block(codes, scale):
    return (codes.astype(jnp.float32) * scale).astype(jnp.bfloat16)


def first_kernel(
    tokens_ref, gain_ref, shift_ref, scales_ref, codes_ref, grad_ref, layer_ref, out_scales_ref, out_codes_ref,
    weight_out, near_out, far_out,
    tokens, gain, shift, scales, codes, grad, layer, out_scales, out_codes, scaled, weight, sems
):
    half = half_index()
    other = 1 - half
    blocks = HALF // QBLOCK

    def copy(source, target, at):
        started = pltpu.make_async_copy(source, target, sems.at[at])
        started.start()
        return started

    def columns(part):
        return codes_ref.at[:, pl.ds(pl.multiple_of(part * HD + half * HALF, QBLOCK), HALF)]

    def rows(which):
        return out_codes_ref.at[pl.ds(pl.multiple_of(which * HALF, QBLOCK), HALF), :]

    scales_copy = copy(scales_ref, scales, 0)
    codes_copies = [copy(columns(part), codes.at[part], 1 + part) for part in range(3)]
    tokens_copies = [
        copy(tokens_ref, tokens, 4), copy(gain_ref, gain, 5), copy(shift_ref, shift, 6)
    ]
    grad_copies = [
        copy(grad_ref, grad, 7), copy(layer_ref, layer, 8), copy(out_scales_ref, out_scales, 9)
    ]
    out_copies = [copy(rows(other), out_codes.at[0], 10), copy(rows(half), out_codes.at[1], 11)]

    scales_copy.wait()
    for part in range(3):
        codes_copies[part].wait()
        for r in range(codes_ref.shape[0] // QBLOCK):
            for c in range(blocks):
                scale = scales[r, (part * HD) // QBLOCK + half * blocks + c]
                lines = slice(r * QBLOCK, (r + 1) * QBLOCK)
                weight_out[lines, part * HALF + c * QBLOCK : part * HALF + (c + 1) * QBLOCK] = scale_block(
                    codes[part, lines, c * QBLOCK : (c + 1) * QBLOCK], scale
                )

    for started in tokens_copies:
        started.wait()
    width = tokens.shape[2]
    gain_row = row_vector(gain)
    shift_row = row_vector(shift)
    for r in range(0, tokens.shape[1], 16):
        normed, _ = norm_rows(tokens[0, r : r + 16, :].astype(jnp.float32))
        norm_out = (normed * gain_row + shift_row).astype(jnp.bfloat16)
        near_out[r : r + 16, :width] = norm_out
        far_out[r : r + 16, :width] = norm_out

    for started in grad_copies:
        started.wait()
    scaled[...] = (grad[0].astype(jnp.float32) * row_vector(layer)).astype(jnp.bfloat16)
    for i, (out_ref, which) in enumerate(((far_out, other), (near_out, half))):
        out_copies[i].wait()
        for r in range(blocks):
            lines = slice(r * QBLOCK, (r + 1) * QBLOCK)
            for c in range(width // QBLOCK):
                at = slice(c * QBLOCK, (c + 1) * QBLOCK)
                weight[lines, at] = scale_block(out_codes[i, lines, at], out_scales[which * blocks + r, c])
        out_ref[:, width:] = dot_last(scaled[...], weight[...]).astype(jnp.bfloat16)


def first_step(tokens, gain, shift, scales, codes, grad, layer_scale, out_scales, out_codes):
    lines, width = tokens.shape[1:]
    depth = codes.shape[0]
    both = jax.ShapeDtypeStruct((lines, width + HALF), jnp.bfloat16)
    return pl.pallas_call(
        first_kernel,
        out_shape=(jax.ShapeDtypeStruct((depth, 3 * HALF), jnp.bfloat16), both, both),
        in_specs=[spec(pltpu.HBM)] * 9,
        out_specs=(spec(),) * 3,
        scratch_shapes=[
            VMEM(tokens.shape, tokens.dtype),
            VMEM(gain.shape, gain.dtype),
            VMEM(shift.shape, shift.dtype),
            SMEM(scales.shape, scales.dtype),
            VMEM((3, depth, HALF), codes.dtype),
            VMEM(grad.shape, grad.dtype),
            VMEM(layer_scale.shape, layer_scale.dtype),
            SMEM(out_scales.shape, out_scales.dtype),
            VMEM((2, HALF, width), out_codes.dtype),
            VMEM((lines, width), jnp.bfloat16),
            VMEM((HALF, width), jnp.bfloat16),
            pltpu.SemaphoreType.DMA((12,)),
        ],
        compiler_params=pltpu.CompilerParams(vmem_limit_bytes=60 * 2**20),
        cost_estimate=cost(3),
        name="first_weights_and_rows",
    )(tokens, gain, shift, scales, codes, grad, layer_scale, out_scales, out_codes)


def far_kernel(scales_ref, codes_ref, after_ref, weight_out, scales, codes, sems):
    other = 1 - half_index()
    blocks = HALF // QBLOCK
    copies = [pltpu.make_async_copy(scales_ref, scales, sems.at[3])]
    for part in range(3):
        at = pl.ds(pl.multiple_of(part * HD + other * HALF, QBLOCK), HALF)
        copies.append(pltpu.make_async_copy(codes_ref.at[:, at], codes.at[part], sems.at[part]))
    for started in copies:
        started.start()
    for started in copies:
        started.wait()
    for part in range(3):
        for r in range(codes_ref.shape[0] // QBLOCK):
            for c in range(blocks):
                scale = scales[r, (part * HD) // QBLOCK + other * blocks + c]
                lines = slice(r * QBLOCK, (r + 1) * QBLOCK)
                weight_out[lines, part * HALF + c * QBLOCK : part * HALF + (c + 1) * QBLOCK] = scale_block(
                    codes[part, lines, c * QBLOCK : (c + 1) * QBLOCK], scale
                )


def far_step(scales, codes, after):
    depth = codes.shape[0]
    return pl.pallas_call(
        far_kernel,
        out_shape=jax.ShapeDtypeStruct((depth, 3 * HALF), jnp.bfloat16),
        in_specs=[spec(pltpu.HBM), spec(pltpu.HBM), spec()],
        out_specs=spec(),
        scratch_shapes=[
            SMEM(scales.shape, scales.dtype),
            VMEM((3, depth, HALF), codes.dtype),
            pltpu.SemaphoreType.DMA((4,)),
        ],
        compiler_params=pltpu.CompilerParams(vmem_limit_bytes=16 * 2**20),
        cost_estimate=cost(0.01),
        name="far_weight",
    )(scales, codes, after)


def dot_last(a, b):
    return lax.dot_general(a, b, (((1,), (1,)), ((), ())), preferred_element_type=jnp.float32)


def dot_plain(a, b):
    return jnp.dot(a, b, preferred_element_type=jnp.float32)


def norm_columns(norms, picks, depth):
    mine = lax.axis_index("weight")
    return jnp.concatenate(
        [
            jnp.concatenate(
                [norm_ref[:, pl.ds(pl.multiple_of((mine ^ j) * depth, QBLOCK), depth)] for j in picks],
                axis=1,
            )
            for norm_ref in norms
        ],
        axis=0,
    )


def project_kernel(first, *refs):
    norms, weights, bias_ref, proj = refs[0:2], refs[2:7], refs[7], refs[-1]
    half = half_index()
    rows = norm_columns(norms, range(4), weights[0].shape[0])
    bias = row_vector(bias_ref)
    for part in range(3):
        at = slice(part * HALF, (part + 1) * HALF)
        shift = jnp.where(
            half == 0,
            bias[:, part * HD : part * HD + HALF],
            bias[:, part * HD + HALF : (part + 1) * HD],
        )
        columns = jnp.concatenate([w[:, at] for w in weights], axis=0)
        value = (dot_plain(rows, columns) + shift).astype(jnp.bfloat16)
        if part == 0:
            value = value * jnp.bfloat16(HEAD_DIM**-0.5)
        proj[first : first + rows.shape[0], at] = value


def project_step(norms, weights, bias, *before):
    tokens = norms[0].shape[0]
    first = 2 * tokens * len(before)
    return pl.pallas_call(
        functools.partial(project_kernel, first),
        out_shape=jax.ShapeDtypeStruct((4 * tokens, 3 * HALF), jnp.bfloat16),
        in_specs=[spec()] * (8 + len(before)),
        out_specs=spec(),
        input_output_aliases={8: 0} if before else {},
        compiler_params=pltpu.CompilerParams(vmem_limit_bytes=24 * 2**20),
        cost_estimate=cost(0.01),
        name="projection",
    )(*norms, *weights, bias, *before)


PAIR = 2 * HEAD_DIM


def attention_kernel(pairs, *refs):
    proj, grads, outs = refs[0], refs[1:5], refs[-4:]
    total = proj.shape[0]
    tokens = grads[0].shape[0]
    low = lax.broadcasted_iota(jnp.int32, (total, PAIR), 1) < HEAD_DIM
    zero = jnp.zeros((total, PAIR), jnp.bfloat16)
    for place, t in enumerate(pairs):
        query = proj[:, t * PAIR : (t + 1) * PAIR]
        key = proj[:, HALF + t * PAIR : HALF + (t + 1) * PAIR]
        value = proj[:, 2 * HALF + t * PAIR : 2 * HALF + (t + 1) * PAIR]
        grad = jnp.concatenate(
            [g[:, g.shape[1] - HALF + t * PAIR : g.shape[1] - HALF + (t + 1) * PAIR] for g in grads], axis=0
        )
        key_t = key.T
        key_grad = value_grad = None
        query_grad = []
        for side in range(2):
            mask = low if side == 0 else ~low
            scores = dot_last(jnp.where(mask, key, zero), query)
            dprob = dot_last(jnp.where(mask, value, zero), grad)
            expo = jnp.exp(scores - jnp.max(scores, axis=0, keepdims=True))
            scale = 1.0 / jnp.sum(expo, axis=0, keepdims=True)
            delta = jnp.sum(expo * dprob, axis=0, keepdims=True) * scale
            prob = expo * scale
            dscore = (prob * (dprob - delta)).astype(jnp.bfloat16)
            key_part = dot_plain(dscore, jnp.where(mask, query, zero))
            value_part = dot_plain(prob.astype(jnp.bfloat16), jnp.where(mask, grad, zero))
            key_grad = key_part if side == 0 else key_grad + key_part
            value_grad = value_part if side == 0 else value_grad + value_part
            query_grad.append(dot_plain(key_t[side * HEAD_DIM : (side + 1) * HEAD_DIM], dscore))
        query_grad = jnp.concatenate(query_grad, axis=0).T * HEAD_DIM**-0.5
        for part, piece in enumerate((query_grad, key_grad, value_grad)):
            piece = piece.astype(jnp.bfloat16)
            first = (part * len(pairs) + place) * PAIR
            for i, out in enumerate(outs):
                out[:, first : first + PAIR] = piece[i * tokens : (i + 1) * tokens]


def attention_step(proj, grads, pairs, *after):
    tokens = grads[0].shape[0]
    out = jax.ShapeDtypeStruct((tokens, 3 * len(pairs) * PAIR), jnp.bfloat16)
    return pl.pallas_call(
        functools.partial(attention_kernel, pairs),
        out_shape=(out,) * 4,
        in_specs=[spec()] * 5 + [spec()] * len(after),
        out_specs=(spec(),) * 4,
        compiler_params=pltpu.CompilerParams(vmem_limit_bytes=24 * 2**20),
        cost_estimate=cost(12),
        name="attention",
    )(proj, *grads, *after)


def join_halves(weights):
    return [w[...] for w in weights[:3]] + [jnp.concatenate([w[...] for w in weights[3:]], axis=0)]


def on_middle():
    place = lax.axis_index("seq")
    return (place == 1) | (place == 2)


def early_kernel(*refs):
    near_w, far_w = join_halves(refs[0:5]), refs[5:8]
    own_ref, skip_ref, tokens_ref, sums, normed_out, inverse_out = refs[8:]
    middle = on_middle()
    mine = lax.axis_index("weight")
    depth = far_w[0].shape[0]

    def fill(value_ref, weights, far):
        value = value_ref[...]
        for j in range(4):
            at = pl.ds(pl.multiple_of((mine ^ j) * depth, QBLOCK), depth)
            if j < len(weights):
                sums[:, at] = dot_last(value, weights[j][...] if far else weights[j])
            else:
                sums[:, at] = jnp.zeros((value.shape[0], depth), jnp.float32)

    pl.when(middle)(lambda: fill(own_ref, near_w, False))
    pl.when(jnp.logical_not(middle))(lambda: fill(skip_ref, far_w, True))
    for r in range(0, tokens_ref.shape[1], 16):
        normed, inverse = norm_rows(tokens_ref[0, r : r + 16, :].astype(jnp.float32))
        normed_out[r : r + 16, :] = normed
        inverse_out[r : r + 16, :] = jnp.broadcast_to(inverse, (16, QBLOCK))


def early_step(near_w, far_w, own, skip, tokens):
    rows, width = tokens.shape[1:]
    full = jax.ShapeDtypeStruct((rows, width), jnp.float32)
    return pl.pallas_call(
        early_kernel,
        out_shape=(full, full, jax.ShapeDtypeStruct((rows, QBLOCK), jnp.float32)),
        in_specs=[spec()] * 11,
        out_specs=(spec(),) * 3,
        compiler_params=pltpu.CompilerParams(vmem_limit_bytes=24 * 2**20),
        cost_estimate=cost(20),
        name="grad_norm_part",
    )(*near_w, *far_w, own, skip, tokens)


def last_kernel(*refs):
    near_w, far_w = join_halves(refs[0:5]), refs[5:9]
    cross_ref, back_ref, skip_ref, sums, normed_ref, inverse_ref, gain_ref, out_ref, grad_norm = refs[9:]
    middle = on_middle()
    mine = lax.axis_index("weight")
    depth = far_w[0].shape[0]

    def fill(value_ref, weights, far):
        value = value_ref[...]
        for j in range(4):
            at = pl.ds(pl.multiple_of((mine ^ j) * depth, QBLOCK), depth)
            total = sums[:, at] + dot_last(value, weights[j][...] if far else weights[j])
            if j == 3 and not far:
                total += dot_last(skip_ref[...], far_w[3][...])
            grad_norm[:, at] = total

    pl.when(middle)(lambda: fill(cross_ref, far_w, True))
    pl.when(jnp.logical_not(middle))(lambda: fill(back_ref, near_w, False))
    gain = row_vector(gain_ref)
    for r in range(0, normed_ref.shape[0], 16):
        normed = normed_ref[r : r + 16, :]
        grad_hat = grad_norm[r : r + 16, :] * gain
        first_mean = jnp.mean(grad_hat, axis=-1, keepdims=True)
        second_mean = jnp.mean(grad_hat * normed, axis=-1, keepdims=True)
        out_ref[0, r : r + 16, :] = inverse_ref[r : r + 16, :1] * (grad_hat - first_mean - normed * second_mean)


def last_step(near_w, far_w, cross, back, skip, sums, normed, inverse, gain):
    return pl.pallas_call(
        last_kernel,
        out_shape=jax.ShapeDtypeStruct((1, *normed.shape), jnp.float32),
        in_specs=[spec()] * 16,
        out_specs=spec(),
        scratch_shapes=[VMEM(normed.shape, jnp.float32)],
        compiler_params=pltpu.CompilerParams(vmem_limit_bytes=24 * 2**20),
        cost_estimate=cost(2),
        name="input_grad",
    )(*near_w, *far_w, cross, back, skip, sums, normed, inverse, gain)


def split_kernel(value_ref, upper_ref, lower_ref):
    middle = upper_ref.shape[0]
    upper_ref[...] = value_ref[:middle]
    lower_ref[...] = value_ref[middle:]


def split_step(value):
    half = jax.ShapeDtypeStruct((value.shape[0] // 2, value.shape[1]), value.dtype)
    return pl.pallas_call(
        split_kernel,
        out_shape=(half, half),
        in_specs=[spec()],
        out_specs=(spec(), spec()),
        compiler_params=pltpu.CompilerParams(vmem_limit_bytes=16 * 2**20),
        cost_estimate=cost(0.01),
        name="split_rows",
    )(value)


def pass_kernel(value_ref, *refs):
    refs[-1][...] = value_ref[...]


def pass_after(value, *after):
    return pl.pallas_call(
        pass_kernel,
        out_shape=jax.ShapeDtypeStruct(value.shape, value.dtype),
        in_specs=[spec()] * (1 + len(after)),
        out_specs=spec(),
        input_output_aliases={0: 0},
        compiler_params=pltpu.CompilerParams(vmem_limit_bytes=16 * 2**20),
        cost_estimate=cost(0.01),
        name="pass_after",
    )(value, *after)


END_TO_MIDDLE = [(0, 1), (3, 2)]
MIDDLE = [(1, 2), (2, 1)]
END_TO_FAR = [(0, 2), (3, 1)]
MIDDLE_TO_END = [(1, 0), (2, 3)]
FAR_TO_END = [(1, 3), (2, 0)]


def flip(bit):
    return [(i, i ^ bit) for i in range(4)]


def local_middle(
    tokens,
    upstream_grad,
    norm_gain,
    norm_bias,
    input_codes,
    input_scales,
    input_bias,
    output_codes,
    output_scales,
    layer_scale,
):
    near, both_near, both_other = first_step(
        tokens, norm_gain, norm_bias, input_scales, input_codes, upstream_grad, layer_scale, output_scales, output_codes
    )
    both_mid = lax.ppermute(both_other, "seq", MIDDLE)
    both_far = lax.ppermute(both_other, "seq", END_TO_FAR)
    both_end = lax.ppermute(both_near, "seq", END_TO_MIDDLE)
    near_across = lax.ppermute(near, "weight", flip(2))
    near_beside = lax.ppermute(near, "weight", flip(1))
    near_diagonal = [lax.ppermute(w, "weight", flip(1)) for w in split_step(near_across)]
    far = far_step(input_scales, input_codes, near_across)
    far_across = lax.ppermute(far, "weight", flip(2))
    rows = (both_near, both_end, both_mid, both_far)
    near_w = (near, near_beside, near_across, *near_diagonal)
    proj = project_step(rows[:2], near_w, input_bias)
    proj = project_step(rows[2:], near_w, input_bias, proj)
    own, end, mid, skip = attention_step(proj, rows, (0, 1, 2))
    skip = lax.ppermute(skip, "seq", FAR_TO_END)
    cross = lax.ppermute(mid, "seq", MIDDLE)
    back = lax.ppermute(end, "seq", MIDDLE_TO_END)
    far_beside = lax.ppermute(pass_after(far, own), "weight", flip(1))
    far_w = (far, far_beside, far_across)
    early = early_step(near_w, far_w, own, skip, tokens)
    far_diagonal = lax.ppermute(pass_after(far_across, skip), "weight", flip(1))
    return last_step(near_w, (*far_w, far_diagonal), cross, back, skip, *early, norm_gain)


def dequantize(codes, scales):
    expanded = jnp.repeat(jnp.repeat(scales, QBLOCK, axis=0), QBLOCK, axis=1)
    return (codes.astype(jnp.float32) * expanded).astype(jnp.bfloat16)


def normalize(rows, gain, shift):
    mean_value = jnp.mean(rows, axis=-1, keepdims=True)
    centered = rows - mean_value
    variance = jnp.mean(centered * centered, axis=-1, keepdims=True)
    inverse = lax.rsqrt(variance + 1e-06)
    normed = centered * inverse
    return (normed, inverse, (normed * gain + shift).astype(jnp.bfloat16))


def norm_backward(grad_norm, normed, inverse, gain):
    grad_hat = grad_norm * gain
    first_mean = jnp.mean(grad_hat, axis=-1, keepdims=True)
    second_mean = jnp.mean(grad_hat * normed, axis=-1, keepdims=True)
    return inverse * (grad_hat - first_mean - normed * second_mean)


def score_block(queries, head_grads, pair_block):
    row_count = pair_block.shape[0]
    keys_blk = pair_block[:, :HD].reshape(row_count, HEADS, HEAD_DIM)
    values_blk = pair_block[:, HD:].reshape(row_count, HEADS, HEAD_DIM)
    scores = jnp.einsum(
        "qhd,khd->hqk", queries, keys_blk, preferred_element_type=jnp.float32
    ) * HEAD_DIM ** (-0.5)
    dprob = jnp.einsum("qhd,khd->hqk", head_grads, values_blk, preferred_element_type=jnp.float32)
    return (keys_blk, scores, dprob)


def update_stats(statistics, queries, head_grads, pair_rows):
    sub_size = math.gcd(pair_rows.shape[0], 512)

    def visit_block(block_index, running):
        run_max, run_total, run_mix = running
        pair_block = lax.dynamic_slice_in_dim(pair_rows, block_index * sub_size, sub_size, 0)
        keys_blk, scores, dprob = score_block(queries, head_grads, pair_block)
        new_max = jnp.maximum(run_max, jnp.max(scores, axis=-1))
        factor = jnp.exp(run_max - new_max)
        expo = jnp.exp(scores - new_max[..., None])
        return (
            new_max,
            run_total * factor + jnp.sum(expo, axis=-1),
            run_mix * factor + jnp.sum(expo * dprob, axis=-1),
        )

    return lax.fori_loop(0, pair_rows.shape[0] // sub_size, visit_block, statistics)


def block_backward(queries, head_grads, pair_block, log_total, row_delta):
    keys_blk, scores, dprob = score_block(queries, head_grads, pair_block)
    weights = jnp.exp(scores - log_total[..., None])
    prob_weights = weights.astype(jnp.bfloat16)
    dscore = (weights * (dprob - row_delta[..., None])).astype(jnp.bfloat16)
    return (keys_blk, prob_weights, dscore)


def key_terms_from(queries, head_grads, prob_weights, dscore):
    key_part = jnp.einsum(
        "hqk,qhd->khd", dscore, queries, preferred_element_type=jnp.float32
    ) * HEAD_DIM ** (-0.5)
    value_part = jnp.einsum(
        "hqk,qhd->khd", prob_weights, head_grads, preferred_element_type=jnp.float32
    )
    row_count = key_part.shape[0]
    return jnp.concatenate(
        [key_part.reshape(row_count, HD), value_part.reshape(row_count, HD)], axis=1
    )


def query_side(queries, head_grads, keys_values, local_rows):
    seq_rows = local_rows * lax.axis_size("seq")
    start_stats = (
        jnp.full((HEADS, local_rows), -1e30, jnp.float32),
        jnp.zeros((HEADS, local_rows), jnp.float32),
        jnp.zeros((HEADS, local_rows), jnp.float32),
    )
    all_pairs = lax.all_gather(keys_values, "seq", axis=0, tiled=True)
    statistics = update_stats(start_stats, queries, head_grads, all_pairs)
    row_max, row_total, row_mix = statistics
    log_total = row_max + jnp.log(row_total)
    row_delta = row_mix / row_total
    sub_size = math.gcd(seq_rows, 512)
    block_count = seq_rows // sub_size
    empty_query = jnp.zeros((local_rows, HEADS, HEAD_DIM), jnp.float32)

    def backward_step(block_index, running):
        query_grad, buffer = running
        pair_block = lax.dynamic_slice_in_dim(all_pairs, block_index * sub_size, sub_size, 0)
        keys_blk, prob_weights, dscore = block_backward(
            queries, head_grads, pair_block, log_total, row_delta
        )
        query_grad = query_grad + jnp.einsum(
            "hqk,khd->qhd", dscore, keys_blk, preferred_element_type=jnp.float32
        )
        block_terms = key_terms_from(queries, head_grads, prob_weights, dscore)
        buffer = lax.dynamic_update_slice_in_dim(buffer, block_terms, block_index * sub_size, 0)
        return (query_grad, buffer)

    empty_terms = jnp.zeros((seq_rows, 2 * HD), jnp.float32)
    query_grad, buffer = lax.fori_loop(0, block_count, backward_step, (empty_query, empty_terms))
    pair_grads = lax.psum_scatter(
        buffer.astype(jnp.bfloat16), "seq", scatter_dimension=0, tiled=True
    ).astype(jnp.float32)
    return (query_grad, pair_grads)


def local(
    tokens,
    upstream_grad,
    norm_gain,
    norm_bias,
    input_codes,
    input_scales,
    input_bias,
    output_codes,
    output_scales,
    layer_scale,
):
    all_codes, all_scales = (
        lax.all_gather(input_codes.astype(jnp.float32), "weight", axis=0, tiled=True).astype(
            input_codes.dtype
        ),
        lax.all_gather(input_scales, "weight", axis=0, tiled=True),
    )
    input_weight = dequantize(all_codes, all_scales)
    output_weight = dequantize(output_codes, output_scales)
    normed, inverse, norm_out = normalize(tokens[0].astype(jnp.float32), norm_gain, norm_bias)
    projected = (
        jnp.dot(norm_out, input_weight, preferred_element_type=jnp.float32) + input_bias
    ).astype(jnp.bfloat16)
    local_rows = projected.shape[0]
    queries = projected[:, :HD].reshape(local_rows, HEADS, HEAD_DIM)
    keys_values = projected[:, HD:]
    scaled_grad = (upstream_grad[0].astype(jnp.float32) * layer_scale).astype(jnp.bfloat16)
    head_grads = jnp.dot(scaled_grad, output_weight.T, preferred_element_type=jnp.float32).astype(
        jnp.bfloat16
    )
    head_grads = head_grads.reshape(local_rows, HEADS, HEAD_DIM)
    query_grad, pair_grads = query_side(queries, head_grads, keys_values, local_rows)
    query_grad = (query_grad * HEAD_DIM ** (-0.5)).reshape(local_rows, HD)
    grad_proj = jnp.concatenate([query_grad, pair_grads], axis=1).astype(jnp.bfloat16)
    grad_norm = jnp.dot(grad_proj, input_weight.T, preferred_element_type=jnp.float32)
    result = norm_backward(grad_norm, normed, inverse, norm_gain)
    return result[None]


def solution(mesh):
    in_specs = (
        P(("groups", "weight"), "seq", None),
        P(("groups", "weight"), "seq", None),
        P(),
        P(),
        P("weight", None),
        P("weight", None),
        P(),
        P(),
        P(),
        P(),
    )
    out_specs = P(("groups", "weight"), "seq", None)
    fits = mesh.shape["seq"] == 4 and mesh.shape["weight"] == 4
    plan = local_middle if fits else local
    return jax.shard_map(plan, mesh=mesh, in_specs=in_specs, out_specs=out_specs, check_vma=False)
```

```python
import functools
import math

import jax
import jax.numpy as jnp
from jax import lax
from jax.experimental import pallas as pl
from jax.experimental.pallas import tpu as pltpu
from jax.sharding import PartitionSpec as P

HEADS = 12
HEAD_DIM = 64
QBLOCK = 128
HD = 768
HALF = HD // 2
EPSILON = 1e-06
VMEM = pltpu.VMEM
SMEM = pltpu.SMEM


def half_index():
    return lax.axis_index("seq") * 2 // lax.axis_size("seq")


def cost(micros):
    return pl.CostEstimate(flops=int(micros * 1.0e9), bytes_accessed=int(micros * 3.0e6), transcendentals=0)


def spec(memory_space=VMEM):
    return pl.BlockSpec(memory_space=memory_space)


def norm_rows(rows):
    mean_value = jnp.mean(rows, axis=-1, keepdims=True)
    centered = rows - mean_value
    variance = jnp.mean(centered * centered, axis=-1, keepdims=True)
    inverse = lax.rsqrt(variance + EPSILON)
    return centered * inverse, inverse


def row_vector(ref):
    return ref[...].reshape(1, ref.shape[0])


def scale_block(codes, scale):
    return (codes.astype(jnp.float32) * scale).astype(jnp.bfloat16)


def first_kernel(
    tokens_ref, gain_ref, shift_ref, scales_ref, codes_ref, grad_ref, layer_ref, out_scales_ref, out_codes_ref,
    weight_out, near_out, far_out,
    tokens, gain, shift, scales, codes, grad, layer, out_scales, out_codes, scaled, weight, sems
):
    half = half_index()
    other = 1 - half
    blocks = HALF // QBLOCK

    def copy(source, target, at):
        started = pltpu.make_async_copy(source, target, sems.at[at])
        started.start()
        return started

    def columns(part):
        return codes_ref.at[:, pl.ds(pl.multiple_of(part * HD + half * HALF, QBLOCK), HALF)]

    def rows(which):
        return out_codes_ref.at[pl.ds(pl.multiple_of(which * HALF, QBLOCK), HALF), :]

    scales_copy = copy(scales_ref, scales, 0)
    codes_copies = [copy(columns(part), codes.at[part], 1 + part) for part in range(3)]
    tokens_copies = [
        copy(tokens_ref, tokens, 4), copy(gain_ref, gain, 5), copy(shift_ref, shift, 6)
    ]
    grad_copies = [
        copy(grad_ref, grad, 7), copy(layer_ref, layer, 8), copy(out_scales_ref, out_scales, 9)
    ]
    out_copies = [copy(rows(other), out_codes.at[0], 10), copy(rows(half), out_codes.at[1], 11)]

    scales_copy.wait()
    for part in range(3):
        codes_copies[part].wait()
        for r in range(codes_ref.shape[0] // QBLOCK):
            for c in range(blocks):
                scale = scales[r, (part * HD) // QBLOCK + half * blocks + c]
                lines = slice(r * QBLOCK, (r + 1) * QBLOCK)
                weight_out[lines, part * HALF + c * QBLOCK : part * HALF + (c + 1) * QBLOCK] = scale_block(
                    codes[part, lines, c * QBLOCK : (c + 1) * QBLOCK], scale
                )

    for started in tokens_copies:
        started.wait()
    width = tokens.shape[2]
    gain_row = row_vector(gain)
    shift_row = row_vector(shift)
    for r in range(0, tokens.shape[1], 16):
        normed, _ = norm_rows(tokens[0, r : r + 16, :].astype(jnp.float32))
        norm_out = (normed * gain_row + shift_row).astype(jnp.bfloat16)
        near_out[r : r + 16, :width] = norm_out
        far_out[r : r + 16, :width] = norm_out

    for started in grad_copies:
        started.wait()
    scaled[...] = (grad[0].astype(jnp.float32) * row_vector(layer)).astype(jnp.bfloat16)
    for i, (out_ref, which) in enumerate(((far_out, other), (near_out, half))):
        out_copies[i].wait()
        for r in range(blocks):
            lines = slice(r * QBLOCK, (r + 1) * QBLOCK)
            for c in range(width // QBLOCK):
                at = slice(c * QBLOCK, (c + 1) * QBLOCK)
                weight[lines, at] = scale_block(out_codes[i, lines, at], out_scales[which * blocks + r, c])
        out_ref[:, width:] = dot_last(scaled[...], weight[...]).astype(jnp.bfloat16)


def first_step(tokens, gain, shift, scales, codes, grad, layer_scale, out_scales, out_codes):
    lines, width = tokens.shape[1:]
    depth = codes.shape[0]
    both = jax.ShapeDtypeStruct((lines, width + HALF), jnp.bfloat16)
    return pl.pallas_call(
        first_kernel,
        out_shape=(jax.ShapeDtypeStruct((depth, 3 * HALF), jnp.bfloat16), both, both),
        in_specs=[spec(pltpu.HBM)] * 9,
        out_specs=(spec(),) * 3,
        scratch_shapes=[
            VMEM(tokens.shape, tokens.dtype),
            VMEM(gain.shape, gain.dtype),
            VMEM(shift.shape, shift.dtype),
            SMEM(scales.shape, scales.dtype),
            VMEM((3, depth, HALF), codes.dtype),
            VMEM(grad.shape, grad.dtype),
            VMEM(layer_scale.shape, layer_scale.dtype),
            SMEM(out_scales.shape, out_scales.dtype),
            VMEM((2, HALF, width), out_codes.dtype),
            VMEM((lines, width), jnp.bfloat16),
            VMEM((HALF, width), jnp.bfloat16),
            pltpu.SemaphoreType.DMA((12,)),
        ],
        compiler_params=pltpu.CompilerParams(vmem_limit_bytes=60 * 2**20),
        cost_estimate=cost(3),
        name="first_weights_and_rows",
    )(tokens, gain, shift, scales, codes, grad, layer_scale, out_scales, out_codes)


def far_kernel(scales_ref, codes_ref, after_ref, weight_out, scales, codes, sems):
    other = 1 - half_index()
    blocks = HALF // QBLOCK
    copies = [pltpu.make_async_copy(scales_ref, scales, sems.at[3])]
    for part in range(3):
        at = pl.ds(pl.multiple_of(part * HD + other * HALF, QBLOCK), HALF)
        copies.append(pltpu.make_async_copy(codes_ref.at[:, at], codes.at[part], sems.at[part]))
    for started in copies:
        started.start()
    for started in copies:
        started.wait()
    for part in range(3):
        for r in range(codes_ref.shape[0] // QBLOCK):
            for c in range(blocks):
                scale = scales[r, (part * HD) // QBLOCK + other * blocks + c]
                lines = slice(r * QBLOCK, (r + 1) * QBLOCK)
                weight_out[lines, part * HALF + c * QBLOCK : part * HALF + (c + 1) * QBLOCK] = scale_block(
                    codes[part, lines, c * QBLOCK : (c + 1) * QBLOCK], scale
                )


def far_step(scales, codes, after):
    depth = codes.shape[0]
    return pl.pallas_call(
        far_kernel,
        out_shape=jax.ShapeDtypeStruct((depth, 3 * HALF), jnp.bfloat16),
        in_specs=[spec(pltpu.HBM), spec(pltpu.HBM), spec()],
        out_specs=spec(),
        scratch_shapes=[
            SMEM(scales.shape, scales.dtype),
            VMEM((3, depth, HALF), codes.dtype),
            pltpu.SemaphoreType.DMA((4,)),
        ],
        compiler_params=pltpu.CompilerParams(vmem_limit_bytes=16 * 2**20),
        cost_estimate=cost(0.01),
        name="far_weight",
    )(scales, codes, after)


def dot_last(a, b):
    return lax.dot_general(a, b, (((1,), (1,)), ((), ())), preferred_element_type=jnp.float32)


def dot_plain(a, b):
    return jnp.dot(a, b, preferred_element_type=jnp.float32)


def norm_columns(norms, picks, depth):
    mine = lax.axis_index("weight")
    return jnp.concatenate(
        [
            jnp.concatenate(
                [norm_ref[:, pl.ds(pl.multiple_of((mine ^ j) * depth, QBLOCK), depth)] for j in picks],
                axis=1,
            )
            for norm_ref in norms
        ],
        axis=0,
    )


def project_kernel(first, *refs):
    norms, weights, bias_ref, proj = refs[0:2], refs[2:7], refs[7], refs[-1]
    half = half_index()
    rows = norm_columns(norms, range(4), weights[0].shape[0])
    bias = row_vector(bias_ref)
    for part in range(3):
        at = slice(part * HALF, (part + 1) * HALF)
        shift = jnp.where(
            half == 0,
            bias[:, part * HD : part * HD + HALF],
            bias[:, part * HD + HALF : (part + 1) * HD],
        )
        columns = jnp.concatenate([w[:, at] for w in weights], axis=0)
        value = (dot_plain(rows, columns) + shift).astype(jnp.bfloat16)
        if part == 0:
            value = value * jnp.bfloat16(HEAD_DIM**-0.5)
        proj[first : first + rows.shape[0], at] = value


def project_step(norms, weights, bias, *before):
    tokens = norms[0].shape[0]
    first = 2 * tokens * len(before)
    return pl.pallas_call(
        functools.partial(project_kernel, first),
        out_shape=jax.ShapeDtypeStruct((4 * tokens, 3 * HALF), jnp.bfloat16),
        in_specs=[spec()] * (8 + len(before)),
        out_specs=spec(),
        input_output_aliases={8: 0} if before else {},
        compiler_params=pltpu.CompilerParams(vmem_limit_bytes=24 * 2**20),
        cost_estimate=cost(0.01),
        name="projection",
    )(*norms, *weights, bias, *before)


PAIR = 2 * HEAD_DIM


def attention_kernel(pairs, held, *refs):
    proj, grads, before, outs = refs[0], refs[1:5], refs[5:-4], refs[-4:]
    total = proj.shape[0]
    tokens = grads[0].shape[0]
    low = lax.broadcasted_iota(jnp.int32, (total, PAIR), 1) < HEAD_DIM
    zero = jnp.zeros((total, PAIR), jnp.bfloat16)
    for place, t in enumerate(pairs):
        query = proj[:, t * PAIR : (t + 1) * PAIR]
        key = proj[:, HALF + t * PAIR : HALF + (t + 1) * PAIR]
        value = proj[:, 2 * HALF + t * PAIR : 2 * HALF + (t + 1) * PAIR]
        grad = jnp.concatenate(
            [g[:, g.shape[1] - HALF + t * PAIR : g.shape[1] - HALF + (t + 1) * PAIR] for g in grads], axis=0
        )
        key_t = key.T
        key_grad = value_grad = None
        query_grad = []
        for side in range(2):
            mask = low if side == 0 else ~low
            scores = dot_last(jnp.where(mask, key, zero), query)
            dprob = dot_last(jnp.where(mask, value, zero), grad)
            expo = jnp.exp(scores - jnp.max(scores, axis=0, keepdims=True))
            scale = 1.0 / jnp.sum(expo, axis=0, keepdims=True)
            delta = jnp.sum(expo * dprob, axis=0, keepdims=True) * scale
            prob = expo * scale
            dscore = (prob * (dprob - delta)).astype(jnp.bfloat16)
            key_part = dot_plain(dscore, jnp.where(mask, query, zero))
            value_part = dot_plain(prob.astype(jnp.bfloat16), jnp.where(mask, grad, zero))
            key_grad = key_part if side == 0 else key_grad + key_part
            value_grad = value_part if side == 0 else value_grad + value_part
            query_grad.append(dot_plain(key_t[side * HEAD_DIM : (side + 1) * HEAD_DIM], dscore))
        query_grad = jnp.concatenate(query_grad, axis=0).T * HEAD_DIM**-0.5
        for part, piece in enumerate((query_grad, key_grad, value_grad)):
            piece = piece.astype(jnp.bfloat16)
            for i, out in enumerate(outs):
                whole = out.shape[1] == 3 * HALF
                first = part * HALF + t * PAIR if whole else (part * len(pairs) + place) * PAIR
                out[:, first : first + PAIR] = piece[i * tokens : (i + 1) * tokens]
    for old, out in zip(before[:3] if held else (), outs):
        for part in range(3):
            out[:, part * HALF : part * HALF + held] = old[:, part * held : (part + 1) * held]


def attention_step(proj, grads, pairs, before=(), after=()):
    tokens = grads[0].shape[0]
    widths = [3 * len(pairs) * PAIR] * 4
    for i in range(len(before)):
        widths[i] = 3 * HALF
    held = before[0].shape[1] // 3 if before else 0
    return pl.pallas_call(
        functools.partial(attention_kernel, pairs, held),
        out_shape=tuple(jax.ShapeDtypeStruct((tokens, width), jnp.bfloat16) for width in widths),
        in_specs=[spec()] * (5 + len(before) + len(after)),
        out_specs=(spec(),) * 4,
        compiler_params=pltpu.CompilerParams(vmem_limit_bytes=24 * 2**20),
        cost_estimate=cost(12),
        name="attention",
    )(proj, *grads, *before, *after)


def join_halves(weights):
    return [w[...] for w in weights[:3]] + [jnp.concatenate([w[...] for w in weights[3:]], axis=0)]


def join_skip(first, second):
    wide, narrow = first.shape[1] // 3, second.shape[1] // 3
    pieces = []
    for part in range(3):
        pieces += [first[:, part * wide : (part + 1) * wide], second[:, part * narrow : (part + 1) * narrow]]
    return jnp.concatenate(pieces, axis=1)


def on_middle():
    place = lax.axis_index("seq")
    return (place == 1) | (place == 2)


def early_kernel(*refs):
    near_w, far_w = join_halves(refs[0:5]), {0: refs[5], 2: refs[6]}
    own_ref, skip_first, skip_second, tokens_ref, sums, normed_out, inverse_out = refs[7:]
    middle = on_middle()
    mine = lax.axis_index("weight")
    depth = far_w[0].shape[0]

    def fill(value, weights, far):
        for j in range(4):
            at = pl.ds(pl.multiple_of((mine ^ j) * depth, QBLOCK), depth)
            if not far or j in weights:
                sums[:, at] = dot_last(value, weights[j][...] if far else weights[j])
            else:
                sums[:, at] = jnp.zeros((value.shape[0], depth), jnp.float32)

    pl.when(middle)(lambda: fill(own_ref[...], near_w, False))
    pl.when(jnp.logical_not(middle))(lambda: fill(join_skip(skip_first, skip_second), far_w, True))
    for r in range(0, tokens_ref.shape[1], 16):
        normed, inverse = norm_rows(tokens_ref[0, r : r + 16, :].astype(jnp.float32))
        normed_out[r : r + 16, :] = normed
        inverse_out[r : r + 16, :] = jnp.broadcast_to(inverse, (16, QBLOCK))


def early_step(near_w, far_w, own, skips, tokens):
    rows, width = tokens.shape[1:]
    full = jax.ShapeDtypeStruct((rows, width), jnp.float32)
    return pl.pallas_call(
        early_kernel,
        out_shape=(full, full, jax.ShapeDtypeStruct((rows, QBLOCK), jnp.float32)),
        in_specs=[spec()] * 11,
        out_specs=(spec(),) * 3,
        compiler_params=pltpu.CompilerParams(vmem_limit_bytes=24 * 2**20),
        cost_estimate=cost(50),
        name="grad_norm_part",
    )(*near_w, *far_w, own, *skips, tokens)


def pair_part_kernel(pair, skip_first, skip_second, sums, out_ref):
    mine = lax.axis_index("weight")
    depth = pair.shape[0] // 2
    out_ref[...] = sums[...]

    @pl.when(jnp.logical_not(on_middle()))
    def _():
        for i, j in enumerate((1, 3)):
            at = pl.ds(pl.multiple_of((mine ^ j) * depth, QBLOCK), depth)
            out_ref[:, at] = sums[:, at] + dot_last(
                join_skip(skip_first, skip_second), pair[i * depth : (i + 1) * depth]
            )


def pair_part_step(pair, skips, sums):
    return pl.pallas_call(
        pair_part_kernel,
        out_shape=jax.ShapeDtypeStruct(sums.shape, sums.dtype),
        in_specs=[spec()] * 4,
        out_specs=spec(),
        compiler_params=pltpu.CompilerParams(vmem_limit_bytes=24 * 2**20),
        cost_estimate=cost(0.01),
        name="pair_part",
    )(pair, *skips, sums)


def last_kernel(*refs):
    near_w, pair = join_halves(refs[0:5]), refs[7]
    back_ref, cross_ref, sums, normed_ref, inverse_ref, gain_ref, out_ref, grad_norm = refs[8:]
    middle = on_middle()
    mine = lax.axis_index("weight")
    depth = refs[5].shape[0]
    far_w = (refs[5], pair.at[:depth], refs[6], pair.at[depth:])

    def fill(value_ref, weights, far):
        value = value_ref[...]
        for j in range(4):
            at = pl.ds(pl.multiple_of((mine ^ j) * depth, QBLOCK), depth)
            grad_norm[:, at] = sums[:, at] + dot_last(value, weights[j][...] if far else weights[j])

    pl.when(middle)(lambda: fill(cross_ref, far_w, True))
    pl.when(jnp.logical_not(middle))(lambda: fill(back_ref, near_w, False))
    gain = row_vector(gain_ref)
    for r in range(0, normed_ref.shape[0], 16):
        normed = normed_ref[r : r + 16, :]
        grad_hat = grad_norm[r : r + 16, :] * gain
        first_mean = jnp.mean(grad_hat, axis=-1, keepdims=True)
        second_mean = jnp.mean(grad_hat * normed, axis=-1, keepdims=True)
        out_ref[0, r : r + 16, :] = inverse_ref[r : r + 16, :1] * (grad_hat - first_mean - normed * second_mean)


def last_step(near_w, far_w, back, cross, sums, normed, inverse, gain):
    return pl.pallas_call(
        last_kernel,
        out_shape=jax.ShapeDtypeStruct((1, *normed.shape), jnp.float32),
        in_specs=[spec()] * 14,
        out_specs=spec(),
        scratch_shapes=[VMEM(normed.shape, jnp.float32)],
        compiler_params=pltpu.CompilerParams(vmem_limit_bytes=24 * 2**20),
        cost_estimate=cost(2),
        name="input_grad",
    )(*near_w, *far_w, back, cross, sums, normed, inverse, gain)


def split_kernel(value_ref, upper_ref, lower_ref):
    middle = upper_ref.shape[0]
    upper_ref[...] = value_ref[:middle]
    lower_ref[...] = value_ref[middle:]


def split_step(value):
    half = jax.ShapeDtypeStruct((value.shape[0] // 2, value.shape[1]), value.dtype)
    return pl.pallas_call(
        split_kernel,
        out_shape=(half, half),
        in_specs=[spec()],
        out_specs=(spec(), spec()),
        compiler_params=pltpu.CompilerParams(vmem_limit_bytes=16 * 2**20),
        cost_estimate=cost(0.01),
        name="split_rows",
    )(value)


def pair_kernel(first_ref, second_ref, after_ref, out_ref):
    middle = first_ref.shape[0]
    out_ref[:middle] = first_ref[...]
    out_ref[middle:] = second_ref[...]


def pair_step(first, second, after):
    return pl.pallas_call(
        pair_kernel,
        out_shape=jax.ShapeDtypeStruct((2 * first.shape[0], first.shape[1]), first.dtype),
        in_specs=[spec()] * 3,
        out_specs=spec(),
        compiler_params=pltpu.CompilerParams(vmem_limit_bytes=16 * 2**20),
        cost_estimate=cost(0.01),
        name="chip_weight",
    )(first, second, after)


END_TO_MIDDLE = [(0, 1), (3, 2)]
MIDDLE = [(1, 2), (2, 1)]
END_TO_FAR = [(0, 2), (3, 1)]
MIDDLE_TO_END = [(1, 0), (2, 3)]
FAR_TO_END = [(1, 3), (2, 0)]


def flip(bit):
    return [(i, i ^ bit) for i in range(4)]


def local_middle(
    tokens,
    upstream_grad,
    norm_gain,
    norm_bias,
    input_codes,
    input_scales,
    input_bias,
    output_codes,
    output_scales,
    layer_scale,
):
    near, both_near, both_other = first_step(
        tokens, norm_gain, norm_bias, input_scales, input_codes, upstream_grad, layer_scale, output_scales, output_codes
    )
    both_mid = lax.ppermute(both_other, "seq", MIDDLE)
    both_far = lax.ppermute(both_other, "seq", END_TO_FAR)
    both_end = lax.ppermute(both_near, "seq", END_TO_MIDDLE)
    near_across = lax.ppermute(near, "weight", flip(2))
    near_beside = lax.ppermute(near, "weight", flip(1))
    near_diagonal = [lax.ppermute(w, "weight", flip(1)) for w in split_step(near_across)]
    far = far_step(input_scales, input_codes, near_across)
    far_across = lax.ppermute(far, "weight", flip(2))
    rows = (both_near, both_end, both_mid, both_far)
    near_w = (near, near_beside, near_across, *near_diagonal)
    proj = project_step(rows[:2], near_w, input_bias)
    proj = project_step(rows[2:], near_w, input_bias, proj)
    grads = (both_near, both_end, both_mid, both_far)
    *kept, skip_first = attention_step(proj, grads, (0, 1), after=(far,))
    skip_first = lax.ppermute(skip_first, "seq", FAR_TO_END)
    own, end, mid, skip_second = attention_step(proj, grads, (2,), kept)
    skip_second = lax.ppermute(skip_second, "seq", FAR_TO_END)
    cross = lax.ppermute(mid, "seq", MIDDLE)
    back = lax.ppermute(end, "seq", MIDDLE_TO_END)
    far_pair = lax.ppermute(pair_step(far, far_across, skip_second), "weight", flip(1))
    far_w = (far, far_across)
    skips = (skip_first, skip_second)
    sums, normed, inverse = early_step(near_w, far_w, own, skips, tokens)
    sums = pair_part_step(far_pair, skips, sums)
    return last_step(near_w, (*far_w, far_pair), back, cross, sums, normed, inverse, norm_gain)


def dequantize(codes, scales):
    expanded = jnp.repeat(jnp.repeat(scales, QBLOCK, axis=0), QBLOCK, axis=1)
    return (codes.astype(jnp.float32) * expanded).astype(jnp.bfloat16)


def normalize(rows, gain, shift):
    mean_value = jnp.mean(rows, axis=-1, keepdims=True)
    centered = rows - mean_value
    variance = jnp.mean(centered * centered, axis=-1, keepdims=True)
    inverse = lax.rsqrt(variance + 1e-06)
    normed = centered * inverse
    return (normed, inverse, (normed * gain + shift).astype(jnp.bfloat16))


def norm_backward(grad_norm, normed, inverse, gain):
    grad_hat = grad_norm * gain
    first_mean = jnp.mean(grad_hat, axis=-1, keepdims=True)
    second_mean = jnp.mean(grad_hat * normed, axis=-1, keepdims=True)
    return inverse * (grad_hat - first_mean - normed * second_mean)


def score_block(queries, head_grads, pair_block):
    row_count = pair_block.shape[0]
    keys_blk = pair_block[:, :HD].reshape(row_count, HEADS, HEAD_DIM)
    values_blk = pair_block[:, HD:].reshape(row_count, HEADS, HEAD_DIM)
    scores = jnp.einsum(
        "qhd,khd->hqk", queries, keys_blk, preferred_element_type=jnp.float32
    ) * HEAD_DIM ** (-0.5)
    dprob = jnp.einsum("qhd,khd->hqk", head_grads, values_blk, preferred_element_type=jnp.float32)
    return (keys_blk, scores, dprob)


def update_stats(statistics, queries, head_grads, pair_rows):
    sub_size = math.gcd(pair_rows.shape[0], 512)

    def visit_block(block_index, running):
        run_max, run_total, run_mix = running
        pair_block = lax.dynamic_slice_in_dim(pair_rows, block_index * sub_size, sub_size, 0)
        keys_blk, scores, dprob = score_block(queries, head_grads, pair_block)
        new_max = jnp.maximum(run_max, jnp.max(scores, axis=-1))
        factor = jnp.exp(run_max - new_max)
        expo = jnp.exp(scores - new_max[..., None])
        return (
            new_max,
            run_total * factor + jnp.sum(expo, axis=-1),
            run_mix * factor + jnp.sum(expo * dprob, axis=-1),
        )

    return lax.fori_loop(0, pair_rows.shape[0] // sub_size, visit_block, statistics)


def block_backward(queries, head_grads, pair_block, log_total, row_delta):
    keys_blk, scores, dprob = score_block(queries, head_grads, pair_block)
    weights = jnp.exp(scores - log_total[..., None])
    prob_weights = weights.astype(jnp.bfloat16)
    dscore = (weights * (dprob - row_delta[..., None])).astype(jnp.bfloat16)
    return (keys_blk, prob_weights, dscore)


def key_terms_from(queries, head_grads, prob_weights, dscore):
    key_part = jnp.einsum(
        "hqk,qhd->khd", dscore, queries, preferred_element_type=jnp.float32
    ) * HEAD_DIM ** (-0.5)
    value_part = jnp.einsum(
        "hqk,qhd->khd", prob_weights, head_grads, preferred_element_type=jnp.float32
    )
    row_count = key_part.shape[0]
    return jnp.concatenate(
        [key_part.reshape(row_count, HD), value_part.reshape(row_count, HD)], axis=1
    )


def query_side(queries, head_grads, keys_values, local_rows):
    seq_rows = local_rows * lax.axis_size("seq")
    start_stats = (
        jnp.full((HEADS, local_rows), -1e30, jnp.float32),
        jnp.zeros((HEADS, local_rows), jnp.float32),
        jnp.zeros((HEADS, local_rows), jnp.float32),
    )
    all_pairs = lax.all_gather(keys_values, "seq", axis=0, tiled=True)
    statistics = update_stats(start_stats, queries, head_grads, all_pairs)
    row_max, row_total, row_mix = statistics
    log_total = row_max + jnp.log(row_total)
    row_delta = row_mix / row_total
    sub_size = math.gcd(seq_rows, 512)
    block_count = seq_rows // sub_size
    empty_query = jnp.zeros((local_rows, HEADS, HEAD_DIM), jnp.float32)

    def backward_step(block_index, running):
        query_grad, buffer = running
        pair_block = lax.dynamic_slice_in_dim(all_pairs, block_index * sub_size, sub_size, 0)
        keys_blk, prob_weights, dscore = block_backward(
            queries, head_grads, pair_block, log_total, row_delta
        )
        query_grad = query_grad + jnp.einsum(
            "hqk,khd->qhd", dscore, keys_blk, preferred_element_type=jnp.float32
        )
        block_terms = key_terms_from(queries, head_grads, prob_weights, dscore)
        buffer = lax.dynamic_update_slice_in_dim(buffer, block_terms, block_index * sub_size, 0)
        return (query_grad, buffer)

    empty_terms = jnp.zeros((seq_rows, 2 * HD), jnp.float32)
    query_grad, buffer = lax.fori_loop(0, block_count, backward_step, (empty_query, empty_terms))
    pair_grads = lax.psum_scatter(
        buffer.astype(jnp.bfloat16), "seq", scatter_dimension=0, tiled=True
    ).astype(jnp.float32)
    return (query_grad, pair_grads)


def local(
    tokens,
    upstream_grad,
    norm_gain,
    norm_bias,
    input_codes,
    input_scales,
    input_bias,
    output_codes,
    output_scales,
    layer_scale,
):
    all_codes, all_scales = (
        lax.all_gather(input_codes.astype(jnp.float32), "weight", axis=0, tiled=True).astype(
            input_codes.dtype
        ),
        lax.all_gather(input_scales, "weight", axis=0, tiled=True),
    )
    input_weight = dequantize(all_codes, all_scales)
    output_weight = dequantize(output_codes, output_scales)
    normed, inverse, norm_out = normalize(tokens[0].astype(jnp.float32), norm_gain, norm_bias)
    projected = (
        jnp.dot(norm_out, input_weight, preferred_element_type=jnp.float32) + input_bias
    ).astype(jnp.bfloat16)
    local_rows = projected.shape[0]
    queries = projected[:, :HD].reshape(local_rows, HEADS, HEAD_DIM)
    keys_values = projected[:, HD:]
    scaled_grad = (upstream_grad[0].astype(jnp.float32) * layer_scale).astype(jnp.bfloat16)
    head_grads = jnp.dot(scaled_grad, output_weight.T, preferred_element_type=jnp.float32).astype(
        jnp.bfloat16
    )
    head_grads = head_grads.reshape(local_rows, HEADS, HEAD_DIM)
    query_grad, pair_grads = query_side(queries, head_grads, keys_values, local_rows)
    query_grad = (query_grad * HEAD_DIM ** (-0.5)).reshape(local_rows, HD)
    grad_proj = jnp.concatenate([query_grad, pair_grads], axis=1).astype(jnp.bfloat16)
    grad_norm = jnp.dot(grad_proj, input_weight.T, preferred_element_type=jnp.float32)
    result = norm_backward(grad_norm, normed, inverse, norm_gain)
    return result[None]


def solution(mesh):
    in_specs = (
        P(("groups", "weight"), "seq", None),
        P(("groups", "weight"), "seq", None),
        P(),
        P(),
        P("weight", None),
        P("weight", None),
        P(),
        P(),
        P(),
        P(),
    )
    out_specs = P(("groups", "weight"), "seq", None)
    fits = mesh.shape["seq"] == 4 and mesh.shape["weight"] == 4
    plan = local_middle if fits else local
    return jax.shard_map(plan, mesh=mesh, in_specs=in_specs, out_specs=out_specs, check_vma=False)
```

```python
import functools
import math

import jax
import jax.numpy as jnp
from jax import lax
from jax.experimental import pallas as pl
from jax.experimental.pallas import tpu as pltpu
from jax.sharding import PartitionSpec as P

HEADS = 12
HEAD_DIM = 64
QBLOCK = 128
HD = 768
HALF = HD // 2
EPSILON = 1e-06
VMEM = pltpu.VMEM
SMEM = pltpu.SMEM


def half_index():
    return lax.axis_index("seq") * 2 // lax.axis_size("seq")


def cost(micros):
    return pl.CostEstimate(flops=int(micros * 1.0e9), bytes_accessed=int(micros * 3.0e6), transcendentals=0)


def spec(memory_space=VMEM):
    return pl.BlockSpec(memory_space=memory_space)


def norm_rows(rows):
    mean_value = jnp.mean(rows, axis=-1, keepdims=True)
    centered = rows - mean_value
    variance = jnp.mean(centered * centered, axis=-1, keepdims=True)
    inverse = lax.rsqrt(variance + EPSILON)
    return centered * inverse, inverse


def row_vector(ref):
    return ref[...].reshape(1, ref.shape[0])


def scale_block(codes, scale):
    return (codes.astype(jnp.float32) * scale).astype(jnp.bfloat16)


def first_kernel(
    tokens_ref, gain_ref, shift_ref, scales_ref, codes_ref, grad_ref, layer_ref, out_scales_ref, out_codes_ref,
    weight_out, near_out, far_out,
    tokens, gain, shift, scales, codes, grad, layer, out_scales, out_codes, scaled, weight, far, sems
):
    half = half_index()
    other = 1 - half
    blocks = HALF // QBLOCK

    def copy(source, target, at):
        started = pltpu.make_async_copy(source, target, sems.at[at])
        started.start()
        return started

    def columns(part):
        return codes_ref.at[:, pl.ds(pl.multiple_of(part * HD + half * HALF, QBLOCK), HALF)]

    def rows(which):
        return out_codes_ref.at[pl.ds(pl.multiple_of(which * HALF, QBLOCK), HALF), :]

    scales_copy = copy(scales_ref, scales, 0)
    codes_copies = [copy(columns(part), codes.at[part], 1 + part) for part in range(3)]
    tokens_copies = [
        copy(tokens_ref, tokens, 4), copy(gain_ref, gain, 5), copy(shift_ref, shift, 6)
    ]
    grad_copies = [
        copy(grad_ref, grad, 7), copy(layer_ref, layer, 8), copy(out_scales_ref, out_scales, 9)
    ]
    out_copies = [copy(rows(other), out_codes.at[0], 10), copy(rows(half), out_codes.at[1], 11)]

    scales_copy.wait()
    for part in range(3):
        codes_copies[part].wait()
        for r in range(codes_ref.shape[0] // QBLOCK):
            for c in range(blocks):
                scale = scales[r, (part * HD) // QBLOCK + half * blocks + c]
                lines = slice(r * QBLOCK, (r + 1) * QBLOCK)
                weight_out[lines, part * HALF + c * QBLOCK : part * HALF + (c + 1) * QBLOCK] = scale_block(
                    codes[part, lines, c * QBLOCK : (c + 1) * QBLOCK], scale
                )

    for started in tokens_copies:
        started.wait()
    width = tokens.shape[2]
    gain_row = row_vector(gain)
    shift_row = row_vector(shift)
    for r in range(0, tokens.shape[1], 16):
        normed, _ = norm_rows(tokens[0, r : r + 16, :].astype(jnp.float32))
        norm_out = (normed * gain_row + shift_row).astype(jnp.bfloat16)
        near_out[r : r + 16, :width] = norm_out
        far[r : r + 16, :width] = norm_out

    for started in grad_copies:
        started.wait()
    scaled[...] = (grad[0].astype(jnp.float32) * row_vector(layer)).astype(jnp.bfloat16)
    for i, (out_ref, which) in enumerate(((far, other), (near_out, half))):
        out_copies[i].wait()
        for r in range(blocks):
            lines = slice(r * QBLOCK, (r + 1) * QBLOCK)
            for c in range(width // QBLOCK):
                at = slice(c * QBLOCK, (c + 1) * QBLOCK)
                weight[lines, at] = scale_block(out_codes[i, lines, at], out_scales[which * blocks + r, c])
        out_ref[:, width:] = dot_last(scaled[...], weight[...]).astype(jnp.bfloat16)
        if out_ref is far:
            far_copy = copy(far, far_out, 12)
    far_copy.wait()


def first_step(tokens, gain, shift, scales, codes, grad, layer_scale, out_scales, out_codes):
    lines, width = tokens.shape[1:]
    depth = codes.shape[0]
    return pl.pallas_call(
        first_kernel,
        out_shape=(
            VMEM((depth, 3 * HALF), jnp.bfloat16),
            VMEM((lines, width + HALF), jnp.bfloat16),
            jax.ShapeDtypeStruct((lines, width + HALF), jnp.bfloat16),
        ),
        in_specs=[spec(pltpu.HBM)] * 9,
        out_specs=(spec(), spec(), spec(pltpu.HBM)),
        scratch_shapes=[
            VMEM(tokens.shape, tokens.dtype),
            VMEM(gain.shape, gain.dtype),
            VMEM(shift.shape, shift.dtype),
            SMEM(scales.shape, scales.dtype),
            VMEM((3, depth, HALF), codes.dtype),
            VMEM(grad.shape, grad.dtype),
            VMEM(layer_scale.shape, layer_scale.dtype),
            SMEM(out_scales.shape, out_scales.dtype),
            VMEM((2, HALF, width), out_codes.dtype),
            VMEM((lines, width), jnp.bfloat16),
            VMEM((HALF, width), jnp.bfloat16),
            VMEM((lines, width + HALF), jnp.bfloat16),
            pltpu.SemaphoreType.DMA((13,)),
        ],
        compiler_params=pltpu.CompilerParams(vmem_limit_bytes=60 * 2**20),
        cost_estimate=cost(3),
        name="first_weights_and_rows",
    )(tokens, gain, shift, scales, codes, grad, layer_scale, out_scales, out_codes)


def far_kernel(scales_ref, codes_ref, after_ref, weight_out, scales, codes, sems):
    other = 1 - half_index()
    blocks = HALF // QBLOCK
    copies = [pltpu.make_async_copy(scales_ref, scales, sems.at[3])]
    for part in range(3):
        at = pl.ds(pl.multiple_of(part * HD + other * HALF, QBLOCK), HALF)
        copies.append(pltpu.make_async_copy(codes_ref.at[:, at], codes.at[part], sems.at[part]))
    for started in copies:
        started.start()
    for started in copies:
        started.wait()
    for part in range(3):
        for r in range(codes_ref.shape[0] // QBLOCK):
            for c in range(blocks):
                scale = scales[r, (part * HD) // QBLOCK + other * blocks + c]
                lines = slice(r * QBLOCK, (r + 1) * QBLOCK)
                weight_out[lines, part * HALF + c * QBLOCK : part * HALF + (c + 1) * QBLOCK] = scale_block(
                    codes[part, lines, c * QBLOCK : (c + 1) * QBLOCK], scale
                )


def far_step(scales, codes, after):
    depth = codes.shape[0]
    return pl.pallas_call(
        far_kernel,
        out_shape=jax.ShapeDtypeStruct((depth, 3 * HALF), jnp.bfloat16),
        in_specs=[spec(pltpu.HBM), spec(pltpu.HBM), spec()],
        out_specs=spec(),
        scratch_shapes=[
            SMEM(scales.shape, scales.dtype),
            VMEM((3, depth, HALF), codes.dtype),
            pltpu.SemaphoreType.DMA((4,)),
        ],
        compiler_params=pltpu.CompilerParams(vmem_limit_bytes=16 * 2**20),
        cost_estimate=cost(0.01),
        name="far_weight",
    )(scales, codes, after)


def dot_last(a, b):
    return lax.dot_general(a, b, (((1,), (1,)), ((), ())), preferred_element_type=jnp.float32)


def dot_plain(a, b):
    return jnp.dot(a, b, preferred_element_type=jnp.float32)


def norm_columns(norms, picks, depth):
    mine = lax.axis_index("weight")
    return jnp.concatenate(
        [
            jnp.concatenate(
                [norm_ref[:, pl.ds(pl.multiple_of((mine ^ j) * depth, QBLOCK), depth)] for j in picks],
                axis=1,
            )
            for norm_ref in norms
        ],
        axis=0,
    )


def project_kernel(first, *refs):
    norms, weights, bias_ref, proj = refs[0:2], refs[2:7], refs[7], refs[-1]
    half = half_index()
    rows = norm_columns(norms, range(4), weights[0].shape[0])
    bias = row_vector(bias_ref)
    for part in range(3):
        at = slice(part * HALF, (part + 1) * HALF)
        shift = jnp.where(
            half == 0,
            bias[:, part * HD : part * HD + HALF],
            bias[:, part * HD + HALF : (part + 1) * HD],
        )
        columns = jnp.concatenate([w[:, at] for w in weights], axis=0)
        value = (dot_plain(rows, columns) + shift).astype(jnp.bfloat16)
        if part == 0:
            value = value * jnp.bfloat16(HEAD_DIM**-0.5)
        proj[first : first + rows.shape[0], at] = value


def project_step(norms, weights, bias, *before):
    tokens = norms[0].shape[0]
    first = 2 * tokens * len(before)
    return pl.pallas_call(
        functools.partial(project_kernel, first),
        out_shape=jax.ShapeDtypeStruct((4 * tokens, 3 * HALF), jnp.bfloat16),
        in_specs=[spec()] * (8 + len(before)),
        out_specs=spec(),
        input_output_aliases={8: 0} if before else {},
        compiler_params=pltpu.CompilerParams(vmem_limit_bytes=24 * 2**20),
        cost_estimate=cost(0.01),
        name="projection",
    )(*norms, *weights, bias, *before)


PAIR = 2 * HEAD_DIM


def soft_part(scores, dprob):
    expo = jnp.exp(scores - jnp.max(scores, axis=0, keepdims=True))
    scale = 1.0 / jnp.sum(expo, axis=0, keepdims=True)
    delta = jnp.sum(expo * dprob, axis=0, keepdims=True) * scale
    prob = (expo * scale).astype(jnp.bfloat16)
    return prob, prob * (dprob - delta).astype(jnp.bfloat16)


def attention_kernel(pairs, held, *refs):
    proj, grads, before, outs = refs[0], refs[1:5], refs[5:-4], refs[-4:]
    total = proj.shape[0]
    tokens = grads[0].shape[0]
    low = lax.broadcasted_iota(jnp.int32, (total, PAIR), 1) < HEAD_DIM
    zero = jnp.zeros((total, PAIR), jnp.bfloat16)

    def load(t):
        query, key, value = (proj[:, part * HALF + t * PAIR : part * HALF + (t + 1) * PAIR] for part in range(3))
        grad = jnp.concatenate(
            [g[:, g.shape[1] - HALF + t * PAIR : g.shape[1] - HALF + (t + 1) * PAIR] for g in grads], axis=0
        )
        return query, key, value, grad

    def mask(side, value):
        return jnp.where(low, value, zero) if side == 0 else jnp.where(low, zero, value)

    def before_soft(t, side):
        query, key, value, grad = load(t)
        return dot_last(mask(side, key), query), dot_last(mask(side, value), grad)

    def after_soft(t, side, prob, dscore):
        query, key, _, grad = load(t)
        key_t = key.T[side * HEAD_DIM : (side + 1) * HEAD_DIM]
        return (
            dot_plain(key_t, dscore),
            dot_plain(dscore, mask(side, query)),
            dot_plain(prob, mask(side, grad)),
        )

    def store(t, first, second):
        place = pairs.index(t)
        query_grad = jnp.concatenate([first[0], second[0]], axis=0).T * HEAD_DIM**-0.5
        for part, piece in enumerate((query_grad, first[1] + second[1], first[2] + second[2])):
            piece = piece.astype(jnp.bfloat16)
            for i, out in enumerate(outs):
                whole = out.shape[1] == 3 * HALF
                at = part * HALF + t * PAIR if whole else (part * len(pairs) + place) * PAIR
                out[:, at : at + PAIR] = piece[i * tokens : (i + 1) * tokens]

    heads = [(t, side) for t in pairs for side in range(2)]
    done = {}

    def finish(t, side, *soft):
        done[t, side] = after_soft(t, side, *soft)
        if side == 1:
            store(t, done[t, 0], done[t, 1])

    ready, behind = before_soft(*heads[0]), None
    for i, head in enumerate(heads):
        now = ready
        if i + 1 < len(heads):
            ready = before_soft(*heads[i + 1])
        if behind is not None:
            finish(*behind)
        behind = (*head, *soft_part(*now))
    finish(*behind)
    for old, out in zip(before[:3] if held else (), outs):
        for part in range(3):
            out[:, part * HALF : part * HALF + held] = old[:, part * held : (part + 1) * held]


def attention_step(proj, grads, pairs, before=(), after=()):
    tokens = grads[0].shape[0]
    widths = [3 * len(pairs) * PAIR] * 4
    for i in range(len(before)):
        widths[i] = 3 * HALF
    held = before[0].shape[1] // 3 if before else 0
    return pl.pallas_call(
        functools.partial(attention_kernel, pairs, held),
        out_shape=tuple(jax.ShapeDtypeStruct((tokens, width), jnp.bfloat16) for width in widths),
        in_specs=[spec()] * (5 + len(before) + len(after)),
        out_specs=(spec(),) * 4,
        compiler_params=pltpu.CompilerParams(vmem_limit_bytes=24 * 2**20),
        cost_estimate=cost(12),
        name="attention",
    )(proj, *grads, *before, *after)


def join_halves(weights):
    return [w[...] for w in weights[:3]] + [jnp.concatenate([w[...] for w in weights[3:]], axis=0)]


def join_skip(first, second):
    wide, narrow = first.shape[1] // 3, second.shape[1] // 3
    pieces = []
    for part in range(3):
        pieces += [first[:, part * wide : (part + 1) * wide], second[:, part * narrow : (part + 1) * narrow]]
    return jnp.concatenate(pieces, axis=1)


def on_middle():
    place = lax.axis_index("seq")
    return (place == 1) | (place == 2)


def early_kernel(*refs):
    near_w, far_w = join_halves(refs[0:5]), {0: refs[5], 2: refs[6]}
    own_ref, skip_first, skip_second, tokens_ref, sums, normed_out, inverse_out = refs[7:]
    middle = on_middle()
    mine = lax.axis_index("weight")
    depth = far_w[0].shape[0]

    def fill(value, weights, far):
        for j in range(4):
            at = pl.ds(pl.multiple_of((mine ^ j) * depth, QBLOCK), depth)
            if not far or j in weights:
                sums[:, at] = dot_last(value, weights[j][...] if far else weights[j])
            else:
                sums[:, at] = jnp.zeros((value.shape[0], depth), jnp.float32)

    pl.when(middle)(lambda: fill(own_ref[...], near_w, False))
    pl.when(jnp.logical_not(middle))(lambda: fill(join_skip(skip_first, skip_second), far_w, True))
    for r in range(0, tokens_ref.shape[1], 16):
        normed, inverse = norm_rows(tokens_ref[0, r : r + 16, :].astype(jnp.float32))
        normed_out[r : r + 16, :] = normed
        inverse_out[r : r + 16, :] = jnp.broadcast_to(inverse, (16, QBLOCK))


def early_step(near_w, far_w, own, skips, tokens):
    rows, width = tokens.shape[1:]
    full = jax.ShapeDtypeStruct((rows, width), jnp.float32)
    return pl.pallas_call(
        early_kernel,
        out_shape=(full, full, jax.ShapeDtypeStruct((rows, QBLOCK), jnp.float32)),
        in_specs=[spec()] * 11,
        out_specs=(spec(),) * 3,
        compiler_params=pltpu.CompilerParams(vmem_limit_bytes=24 * 2**20),
        cost_estimate=cost(50),
        name="grad_norm_part",
    )(*near_w, *far_w, own, *skips, tokens)


def pair_part_kernel(pair, skip_first, skip_second, sums, out_ref):
    mine = lax.axis_index("weight")
    depth = pair.shape[0] // 2
    out_ref[...] = sums[...]

    @pl.when(jnp.logical_not(on_middle()))
    def _():
        for i, j in enumerate((1, 3)):
            at = pl.ds(pl.multiple_of((mine ^ j) * depth, QBLOCK), depth)
            out_ref[:, at] = sums[:, at] + dot_last(
                join_skip(skip_first, skip_second), pair[i * depth : (i + 1) * depth]
            )


def pair_part_step(pair, skips, sums):
    return pl.pallas_call(
        pair_part_kernel,
        out_shape=jax.ShapeDtypeStruct(sums.shape, sums.dtype),
        in_specs=[spec()] * 4,
        out_specs=spec(),
        compiler_params=pltpu.CompilerParams(vmem_limit_bytes=24 * 2**20),
        cost_estimate=cost(0.01),
        name="pair_part",
    )(pair, *skips, sums)


def last_kernel(*refs):
    near_w, pair = join_halves(refs[0:5]), refs[7]
    back_ref, cross_ref, sums, normed_ref, inverse_ref, gain_ref, out_ref, grad_norm = refs[8:]
    middle = on_middle()
    mine = lax.axis_index("weight")
    depth = refs[5].shape[0]
    far_w = (refs[5], pair.at[:depth], refs[6], pair.at[depth:])

    def fill(value_ref, weights, far):
        value = value_ref[...]
        for j in range(4):
            at = pl.ds(pl.multiple_of((mine ^ j) * depth, QBLOCK), depth)
            grad_norm[:, at] = sums[:, at] + dot_last(value, weights[j][...] if far else weights[j])

    pl.when(middle)(lambda: fill(cross_ref, far_w, True))
    pl.when(jnp.logical_not(middle))(lambda: fill(back_ref, near_w, False))
    gain = row_vector(gain_ref)
    for r in range(0, normed_ref.shape[0], 16):
        normed = normed_ref[r : r + 16, :]
        grad_hat = grad_norm[r : r + 16, :] * gain
        first_mean = jnp.mean(grad_hat, axis=-1, keepdims=True)
        second_mean = jnp.mean(grad_hat * normed, axis=-1, keepdims=True)
        out_ref[0, r : r + 16, :] = inverse_ref[r : r + 16, :1] * (grad_hat - first_mean - normed * second_mean)


def last_step(near_w, far_w, back, cross, sums, normed, inverse, gain):
    return pl.pallas_call(
        last_kernel,
        out_shape=jax.ShapeDtypeStruct((1, *normed.shape), jnp.float32),
        in_specs=[spec()] * 14,
        out_specs=spec(),
        scratch_shapes=[VMEM(normed.shape, jnp.float32)],
        compiler_params=pltpu.CompilerParams(vmem_limit_bytes=24 * 2**20),
        cost_estimate=cost(2),
        name="input_grad",
    )(*near_w, *far_w, back, cross, sums, normed, inverse, gain)


def split_kernel(value_ref, upper_ref, lower_ref):
    middle = upper_ref.shape[0]
    upper_ref[...] = value_ref[:middle]
    lower_ref[...] = value_ref[middle:]


def split_step(value):
    half = jax.ShapeDtypeStruct((value.shape[0] // 2, value.shape[1]), value.dtype)
    return pl.pallas_call(
        split_kernel,
        out_shape=(half, half),
        in_specs=[spec()],
        out_specs=(spec(), spec()),
        compiler_params=pltpu.CompilerParams(vmem_limit_bytes=16 * 2**20),
        cost_estimate=cost(0.01),
        name="split_rows",
    )(value)


def pair_kernel(first_ref, second_ref, after_ref, out_ref):
    middle = first_ref.shape[0]
    out_ref[:middle] = first_ref[...]
    out_ref[middle:] = second_ref[...]


def pair_step(first, second, after):
    return pl.pallas_call(
        pair_kernel,
        out_shape=jax.ShapeDtypeStruct((2 * first.shape[0], first.shape[1]), first.dtype),
        in_specs=[spec()] * 3,
        out_specs=spec(),
        compiler_params=pltpu.CompilerParams(vmem_limit_bytes=16 * 2**20),
        cost_estimate=cost(0.01),
        name="chip_weight",
    )(first, second, after)


END_TO_MIDDLE = [(0, 1), (3, 2)]
MIDDLE = [(1, 2), (2, 1)]
END_TO_FAR = [(0, 2), (3, 1)]
MIDDLE_TO_END = [(1, 0), (2, 3)]
FAR_TO_END = [(1, 3), (2, 0)]


def flip(bit):
    return [(i, i ^ bit) for i in range(4)]


def local_middle(
    tokens,
    upstream_grad,
    norm_gain,
    norm_bias,
    input_codes,
    input_scales,
    input_bias,
    output_codes,
    output_scales,
    layer_scale,
):
    near, both_near, both_other = first_step(
        tokens, norm_gain, norm_bias, input_scales, input_codes, upstream_grad, layer_scale, output_scales, output_codes
    )
    both_mid = lax.ppermute(both_other, "seq", MIDDLE)
    both_far = lax.ppermute(both_other, "seq", END_TO_FAR)
    both_end = lax.ppermute(both_near, "seq", END_TO_MIDDLE)
    near_across = lax.ppermute(near, "weight", flip(2))
    near_beside = lax.ppermute(near, "weight", flip(1))
    near_diagonal = [lax.ppermute(w, "weight", flip(1)) for w in split_step(near_across)]
    far = far_step(input_scales, input_codes, near_across)
    far_across = lax.ppermute(far, "weight", flip(2))
    rows = (both_near, both_end, both_mid, both_far)
    near_w = (near, near_beside, near_across, *near_diagonal)
    proj = project_step(rows[:2], near_w, input_bias)
    proj = project_step(rows[2:], near_w, input_bias, proj)
    grads = (both_near, both_end, both_mid, both_far)
    *kept, skip_first = attention_step(proj, grads, (0, 1), after=(far,))
    skip_first = lax.ppermute(skip_first, "seq", FAR_TO_END)
    own, end, mid, skip_second = attention_step(proj, grads, (2,), kept)
    skip_second = lax.ppermute(skip_second, "seq", FAR_TO_END)
    cross = lax.ppermute(mid, "seq", MIDDLE)
    back = lax.ppermute(end, "seq", MIDDLE_TO_END)
    far_pair = lax.ppermute(pair_step(far, far_across, skip_second), "weight", flip(1))
    far_w = (far, far_across)
    skips = (skip_first, skip_second)
    sums, normed, inverse = early_step(near_w, far_w, own, skips, tokens)
    sums = pair_part_step(far_pair, skips, sums)
    return last_step(near_w, (*far_w, far_pair), back, cross, sums, normed, inverse, norm_gain)


def dequantize(codes, scales):
    expanded = jnp.repeat(jnp.repeat(scales, QBLOCK, axis=0), QBLOCK, axis=1)
    return (codes.astype(jnp.float32) * expanded).astype(jnp.bfloat16)


def normalize(rows, gain, shift):
    mean_value = jnp.mean(rows, axis=-1, keepdims=True)
    centered = rows - mean_value
    variance = jnp.mean(centered * centered, axis=-1, keepdims=True)
    inverse = lax.rsqrt(variance + 1e-06)
    normed = centered * inverse
    return (normed, inverse, (normed * gain + shift).astype(jnp.bfloat16))


def norm_backward(grad_norm, normed, inverse, gain):
    grad_hat = grad_norm * gain
    first_mean = jnp.mean(grad_hat, axis=-1, keepdims=True)
    second_mean = jnp.mean(grad_hat * normed, axis=-1, keepdims=True)
    return inverse * (grad_hat - first_mean - normed * second_mean)


def score_block(queries, head_grads, pair_block):
    row_count = pair_block.shape[0]
    keys_blk = pair_block[:, :HD].reshape(row_count, HEADS, HEAD_DIM)
    values_blk = pair_block[:, HD:].reshape(row_count, HEADS, HEAD_DIM)
    scores = jnp.einsum(
        "qhd,khd->hqk", queries, keys_blk, preferred_element_type=jnp.float32
    ) * HEAD_DIM ** (-0.5)
    dprob = jnp.einsum("qhd,khd->hqk", head_grads, values_blk, preferred_element_type=jnp.float32)
    return (keys_blk, scores, dprob)


def update_stats(statistics, queries, head_grads, pair_rows):
    sub_size = math.gcd(pair_rows.shape[0], 512)

    def visit_block(block_index, running):
        run_max, run_total, run_mix = running
        pair_block = lax.dynamic_slice_in_dim(pair_rows, block_index * sub_size, sub_size, 0)
        keys_blk, scores, dprob = score_block(queries, head_grads, pair_block)
        new_max = jnp.maximum(run_max, jnp.max(scores, axis=-1))
        factor = jnp.exp(run_max - new_max)
        expo = jnp.exp(scores - new_max[..., None])
        return (
            new_max,
            run_total * factor + jnp.sum(expo, axis=-1),
            run_mix * factor + jnp.sum(expo * dprob, axis=-1),
        )

    return lax.fori_loop(0, pair_rows.shape[0] // sub_size, visit_block, statistics)


def block_backward(queries, head_grads, pair_block, log_total, row_delta):
    keys_blk, scores, dprob = score_block(queries, head_grads, pair_block)
    weights = jnp.exp(scores - log_total[..., None])
    prob_weights = weights.astype(jnp.bfloat16)
    dscore = (weights * (dprob - row_delta[..., None])).astype(jnp.bfloat16)
    return (keys_blk, prob_weights, dscore)


def key_terms_from(queries, head_grads, prob_weights, dscore):
    key_part = jnp.einsum(
        "hqk,qhd->khd", dscore, queries, preferred_element_type=jnp.float32
    ) * HEAD_DIM ** (-0.5)
    value_part = jnp.einsum(
        "hqk,qhd->khd", prob_weights, head_grads, preferred_element_type=jnp.float32
    )
    row_count = key_part.shape[0]
    return jnp.concatenate(
        [key_part.reshape(row_count, HD), value_part.reshape(row_count, HD)], axis=1
    )


def query_side(queries, head_grads, keys_values, local_rows):
    seq_rows = local_rows * lax.axis_size("seq")
    start_stats = (
        jnp.full((HEADS, local_rows), -1e30, jnp.float32),
        jnp.zeros((HEADS, local_rows), jnp.float32),
        jnp.zeros((HEADS, local_rows), jnp.float32),
    )
    all_pairs = lax.all_gather(keys_values, "seq", axis=0, tiled=True)
    statistics = update_stats(start_stats, queries, head_grads, all_pairs)
    row_max, row_total, row_mix = statistics
    log_total = row_max + jnp.log(row_total)
    row_delta = row_mix / row_total
    sub_size = math.gcd(seq_rows, 512)
    block_count = seq_rows // sub_size
    empty_query = jnp.zeros((local_rows, HEADS, HEAD_DIM), jnp.float32)

    def backward_step(block_index, running):
        query_grad, buffer = running
        pair_block = lax.dynamic_slice_in_dim(all_pairs, block_index * sub_size, sub_size, 0)
        keys_blk, prob_weights, dscore = block_backward(
            queries, head_grads, pair_block, log_total, row_delta
        )
        query_grad = query_grad + jnp.einsum(
            "hqk,khd->qhd", dscore, keys_blk, preferred_element_type=jnp.float32
        )
        block_terms = key_terms_from(queries, head_grads, prob_weights, dscore)
        buffer = lax.dynamic_update_slice_in_dim(buffer, block_terms, block_index * sub_size, 0)
        return (query_grad, buffer)

    empty_terms = jnp.zeros((seq_rows, 2 * HD), jnp.float32)
    query_grad, buffer = lax.fori_loop(0, block_count, backward_step, (empty_query, empty_terms))
    pair_grads = lax.psum_scatter(
        buffer.astype(jnp.bfloat16), "seq", scatter_dimension=0, tiled=True
    ).astype(jnp.float32)
    return (query_grad, pair_grads)


def local(
    tokens,
    upstream_grad,
    norm_gain,
    norm_bias,
    input_codes,
    input_scales,
    input_bias,
    output_codes,
    output_scales,
    layer_scale,
):
    all_codes, all_scales = (
        lax.all_gather(input_codes.astype(jnp.float32), "weight", axis=0, tiled=True).astype(
            input_codes.dtype
        ),
        lax.all_gather(input_scales, "weight", axis=0, tiled=True),
    )
    input_weight = dequantize(all_codes, all_scales)
    output_weight = dequantize(output_codes, output_scales)
    normed, inverse, norm_out = normalize(tokens[0].astype(jnp.float32), norm_gain, norm_bias)
    projected = (
        jnp.dot(norm_out, input_weight, preferred_element_type=jnp.float32) + input_bias
    ).astype(jnp.bfloat16)
    local_rows = projected.shape[0]
    queries = projected[:, :HD].reshape(local_rows, HEADS, HEAD_DIM)
    keys_values = projected[:, HD:]
    scaled_grad = (upstream_grad[0].astype(jnp.float32) * layer_scale).astype(jnp.bfloat16)
    head_grads = jnp.dot(scaled_grad, output_weight.T, preferred_element_type=jnp.float32).astype(
        jnp.bfloat16
    )
    head_grads = head_grads.reshape(local_rows, HEADS, HEAD_DIM)
    query_grad, pair_grads = query_side(queries, head_grads, keys_values, local_rows)
    query_grad = (query_grad * HEAD_DIM ** (-0.5)).reshape(local_rows, HD)
    grad_proj = jnp.concatenate([query_grad, pair_grads], axis=1).astype(jnp.bfloat16)
    grad_norm = jnp.dot(grad_proj, input_weight.T, preferred_element_type=jnp.float32)
    result = norm_backward(grad_norm, normed, inverse, norm_gain)
    return result[None]


def solution(mesh):
    in_specs = (
        P(("groups", "weight"), "seq", None),
        P(("groups", "weight"), "seq", None),
        P(),
        P(),
        P("weight", None),
        P("weight", None),
        P(),
        P(),
        P(),
        P(),
    )
    out_specs = P(("groups", "weight"), "seq", None)
    fits = mesh.shape["seq"] == 4 and mesh.shape["weight"] == 4
    plan = local_middle if fits else local
    return jax.shard_map(plan, mesh=mesh, in_specs=in_specs, out_specs=out_specs, check_vma=False)
```

```python
import functools
import math

import jax
import jax.numpy as jnp
from jax import lax
from jax.experimental import pallas as pl
from jax.experimental.pallas import tpu as pltpu
from jax.sharding import PartitionSpec as P

HEADS = 12
HEAD_DIM = 64
QBLOCK = 128
HD = 768
HALF = HD // 2
ROWS_OUT = 32
EPSILON = 1e-06
VMEM = pltpu.VMEM
SMEM = pltpu.SMEM


def half_index():
    return lax.axis_index("seq") * 2 // lax.axis_size("seq")


def cost(micros):
    return pl.CostEstimate(flops=int(micros * 1.0e9), bytes_accessed=int(micros * 3.0e6), transcendentals=0)


def spec(memory_space=VMEM):
    return pl.BlockSpec(memory_space=memory_space)


def norm_rows(rows):
    mean_value = jnp.mean(rows, axis=-1, keepdims=True)
    centered = rows - mean_value
    variance = jnp.mean(centered * centered, axis=-1, keepdims=True)
    inverse = lax.rsqrt(variance + EPSILON)
    return centered * inverse, inverse


def row_vector(ref):
    return ref[...].reshape(1, ref.shape[0])


def scale_block(codes, scale):
    return (codes.astype(jnp.float32) * scale).astype(jnp.bfloat16)


def first_kernel(
    tokens_ref, gain_ref, shift_ref, scales_ref, codes_ref, grad_ref, layer_ref, out_scales_ref, out_codes_ref,
    weight_out, near_out, far_out,
    tokens, gain, shift, scales, codes, grad, layer, out_scales, out_codes, scaled, weight, far, sems
):
    half = half_index()
    other = 1 - half
    blocks = HALF // QBLOCK

    def copy(source, target, at):
        started = pltpu.make_async_copy(source, target, sems.at[at])
        started.start()
        return started

    def columns(part):
        return codes_ref.at[:, pl.ds(pl.multiple_of(part * HD + half * HALF, QBLOCK), HALF)]

    def rows(which):
        return out_codes_ref.at[pl.ds(pl.multiple_of(which * HALF, QBLOCK), HALF), :]

    scales_copy = copy(scales_ref, scales, 0)
    codes_copies = [copy(columns(part), codes.at[part], 1 + part) for part in range(3)]
    tokens_copies = [
        copy(tokens_ref, tokens, 4), copy(gain_ref, gain, 5), copy(shift_ref, shift, 6)
    ]
    grad_copies = [
        copy(grad_ref, grad, 7), copy(layer_ref, layer, 8), copy(out_scales_ref, out_scales, 9)
    ]
    out_copies = [copy(rows(other), out_codes.at[0], 10), copy(rows(half), out_codes.at[1], 11)]

    scales_copy.wait()
    for part in range(3):
        codes_copies[part].wait()
        for r in range(codes_ref.shape[0] // QBLOCK):
            for c in range(blocks):
                scale = scales[r, (part * HD) // QBLOCK + half * blocks + c]
                lines = slice(r * QBLOCK, (r + 1) * QBLOCK)
                weight_out[lines, part * HALF + c * QBLOCK : part * HALF + (c + 1) * QBLOCK] = scale_block(
                    codes[part, lines, c * QBLOCK : (c + 1) * QBLOCK], scale
                )

    for started in tokens_copies:
        started.wait()
    width = tokens.shape[2]
    gain_row = row_vector(gain)
    shift_row = row_vector(shift)
    for r in range(0, tokens.shape[1], 16):
        normed, _ = norm_rows(tokens[0, r : r + 16, :].astype(jnp.float32))
        norm_out = (normed * gain_row + shift_row).astype(jnp.bfloat16)
        near_out[r : r + 16, :width] = norm_out
        far[r : r + 16, :width] = norm_out

    for started in grad_copies:
        started.wait()
    scaled[...] = (grad[0].astype(jnp.float32) * row_vector(layer)).astype(jnp.bfloat16)
    for i, (out_ref, which) in enumerate(((far, other), (near_out, half))):
        out_copies[i].wait()
        for r in range(blocks):
            lines = slice(r * QBLOCK, (r + 1) * QBLOCK)
            for c in range(width // QBLOCK):
                at = slice(c * QBLOCK, (c + 1) * QBLOCK)
                weight[lines, at] = scale_block(out_codes[i, lines, at], out_scales[which * blocks + r, c])
        out_ref[:, width:] = dot_last(scaled[...], weight[...]).astype(jnp.bfloat16)
        if out_ref is far:
            far_copy = copy(far, far_out, 12)
    far_copy.wait()


def first_step(tokens, gain, shift, scales, codes, grad, layer_scale, out_scales, out_codes):
    lines, width = tokens.shape[1:]
    depth = codes.shape[0]
    return pl.pallas_call(
        first_kernel,
        out_shape=(
            VMEM((depth, 3 * HALF), jnp.bfloat16),
            VMEM((lines, width + HALF), jnp.bfloat16),
            jax.ShapeDtypeStruct((lines, width + HALF), jnp.bfloat16),
        ),
        in_specs=[spec(pltpu.HBM)] * 9,
        out_specs=(spec(), spec(), spec(pltpu.HBM)),
        scratch_shapes=[
            VMEM(tokens.shape, tokens.dtype),
            VMEM(gain.shape, gain.dtype),
            VMEM(shift.shape, shift.dtype),
            SMEM(scales.shape, scales.dtype),
            VMEM((3, depth, HALF), codes.dtype),
            VMEM(grad.shape, grad.dtype),
            VMEM(layer_scale.shape, layer_scale.dtype),
            SMEM(out_scales.shape, out_scales.dtype),
            VMEM((2, HALF, width), out_codes.dtype),
            VMEM((lines, width), jnp.bfloat16),
            VMEM((HALF, width), jnp.bfloat16),
            VMEM((lines, width + HALF), jnp.bfloat16),
            pltpu.SemaphoreType.DMA((13,)),
        ],
        compiler_params=pltpu.CompilerParams(vmem_limit_bytes=60 * 2**20),
        cost_estimate=cost(3),
        name="first_weights_and_rows",
    )(tokens, gain, shift, scales, codes, grad, layer_scale, out_scales, out_codes)


def far_kernel(scales_ref, codes_ref, after_ref, weight_out, scales, codes, sems):
    other = 1 - half_index()
    blocks = HALF // QBLOCK
    copies = [pltpu.make_async_copy(scales_ref, scales, sems.at[3])]
    for part in range(3):
        at = pl.ds(pl.multiple_of(part * HD + other * HALF, QBLOCK), HALF)
        copies.append(pltpu.make_async_copy(codes_ref.at[:, at], codes.at[part], sems.at[part]))
    for started in copies:
        started.start()
    for started in copies:
        started.wait()
    for part in range(3):
        for r in range(codes_ref.shape[0] // QBLOCK):
            for c in range(blocks):
                scale = scales[r, (part * HD) // QBLOCK + other * blocks + c]
                lines = slice(r * QBLOCK, (r + 1) * QBLOCK)
                weight_out[lines, part * HALF + c * QBLOCK : part * HALF + (c + 1) * QBLOCK] = scale_block(
                    codes[part, lines, c * QBLOCK : (c + 1) * QBLOCK], scale
                )


def far_step(scales, codes, after):
    depth = codes.shape[0]
    return pl.pallas_call(
        far_kernel,
        out_shape=jax.ShapeDtypeStruct((depth, 3 * HALF), jnp.bfloat16),
        in_specs=[spec(pltpu.HBM), spec(pltpu.HBM), spec()],
        out_specs=spec(),
        scratch_shapes=[
            SMEM(scales.shape, scales.dtype),
            VMEM((3, depth, HALF), codes.dtype),
            pltpu.SemaphoreType.DMA((4,)),
        ],
        compiler_params=pltpu.CompilerParams(vmem_limit_bytes=16 * 2**20),
        cost_estimate=cost(0.01),
        name="far_weight",
    )(scales, codes, after)


def dot_last(a, b):
    return lax.dot_general(a, b, (((1,), (1,)), ((), ())), preferred_element_type=jnp.float32)


def dot_plain(a, b):
    return jnp.dot(a, b, preferred_element_type=jnp.float32)


def norm_columns(norms, picks, depth):
    mine = lax.axis_index("weight")
    return jnp.concatenate(
        [
            jnp.concatenate(
                [norm_ref[:, pl.ds(pl.multiple_of((mine ^ j) * depth, QBLOCK), depth)] for j in picks],
                axis=1,
            )
            for norm_ref in norms
        ],
        axis=0,
    )


def project_part(norms, weights, bias_ref, proj, first, part):
    half = half_index()
    rows = norm_columns(norms, range(4), weights[0].shape[0])
    bias = row_vector(bias_ref)
    at = slice(part * HALF, (part + 1) * HALF)
    shift = jnp.where(
        half == 0,
        bias[:, part * HD : part * HD + HALF],
        bias[:, part * HD + HALF : (part + 1) * HD],
    )
    columns = jnp.concatenate([w[:, at] for w in weights], axis=0)
    value = (dot_plain(rows, columns) + shift).astype(jnp.bfloat16)
    if part == 0:
        value = value * jnp.bfloat16(HEAD_DIM**-0.5)
    proj[first : first + rows.shape[0], at] = value


def project_kernel(*refs):
    for part in range(3):
        project_part(refs[0:2], refs[2:7], refs[7], refs[8], 0, part)


def project_step(norms, weights, bias):
    tokens = norms[0].shape[0]
    return pl.pallas_call(
        project_kernel,
        out_shape=jax.ShapeDtypeStruct((4 * tokens, 3 * HALF), jnp.bfloat16),
        in_specs=[spec()] * 8,
        out_specs=spec(),
        compiler_params=pltpu.CompilerParams(vmem_limit_bytes=24 * 2**20),
        cost_estimate=cost(0.01),
        name="projection",
    )(*norms, *weights, bias)


PAIR = 2 * HEAD_DIM


def soft_part(scores, dprob):
    expo = jnp.exp(scores - jnp.max(scores, axis=0, keepdims=True))
    scale = 1.0 / jnp.sum(expo, axis=0, keepdims=True)
    delta = jnp.sum(expo * dprob, axis=0, keepdims=True) * scale
    prob = (expo * scale).astype(jnp.bfloat16)
    return prob, prob * (dprob - delta).astype(jnp.bfloat16)


def attention_kernel(pairs, held, *refs):
    proj, grads, before, outs = refs[0], refs[1:5], refs[5:-4], refs[-4:]
    attention(pairs, held, proj, grads, before, outs)


def project_attention_kernel(pairs, *refs):
    norms, weights, bias_ref, proj_in, grads = refs[0:2], refs[2:7], refs[7], refs[8], refs[9:13]
    proj, outs = refs[-5], refs[-4:]
    tokens = norms[0].shape[0]
    proj[: 2 * tokens] = proj_in[: 2 * tokens]

    def project(part):
        project_part(norms, weights, bias_ref, proj, 2 * tokens, part)

    project(0)
    project(1)
    attention(pairs, 0, proj, grads, (), outs, lambda: project(2))


def attention(pairs, held, proj, grads, before, outs, between=None):
    total = proj.shape[0]
    tokens = grads[0].shape[0]
    low = lax.broadcasted_iota(jnp.int32, (total, PAIR), 1) < HEAD_DIM
    zero = jnp.zeros((total, PAIR), jnp.bfloat16)

    def load(t):
        query, key, value = (proj[:, part * HALF + t * PAIR : part * HALF + (t + 1) * PAIR] for part in range(3))
        grad = jnp.concatenate(
            [g[:, g.shape[1] - HALF + t * PAIR : g.shape[1] - HALF + (t + 1) * PAIR] for g in grads], axis=0
        )
        return query, key, value, grad

    def mask(side, value):
        return jnp.where(low, value, zero) if side == 0 else jnp.where(low, zero, value)

    def before_soft(t, side, between=None):
        query, key, value, grad = load(t)
        scores = dot_last(mask(side, key), query)
        if between is not None:
            between()
            value = load(t)[2]
        return scores, dot_last(mask(side, value), grad)

    def after_soft(t, side, prob, dscore):
        query, key, _, grad = load(t)
        key_t = key.T[side * HEAD_DIM : (side + 1) * HEAD_DIM]
        return (
            dot_plain(key_t, dscore),
            dot_plain(dscore, mask(side, query)),
            dot_plain(prob, mask(side, grad)),
        )

    def store(t, first, second):
        place = pairs.index(t)
        query_grad = jnp.concatenate([first[0], second[0]], axis=0).T * HEAD_DIM**-0.5
        for part, piece in enumerate((query_grad, first[1] + second[1], first[2] + second[2])):
            piece = piece.astype(jnp.bfloat16)
            for i, out in enumerate(outs):
                whole = out.shape[1] == 3 * HALF
                at = part * HALF + t * PAIR if whole else (part * len(pairs) + place) * PAIR
                out[:, at : at + PAIR] = piece[i * tokens : (i + 1) * tokens]

    heads = [(t, side) for t in pairs for side in range(2)]
    done = {}

    def finish(t, side, *soft):
        done[t, side] = after_soft(t, side, *soft)
        if side == 1:
            store(t, done[t, 0], done[t, 1])

    ready, behind = before_soft(*heads[0], between), None
    for i, head in enumerate(heads):
        now = ready
        if i + 1 < len(heads):
            ready = before_soft(*heads[i + 1])
        if behind is not None:
            finish(*behind)
        behind = (*head, *soft_part(*now))
    finish(*behind)
    for old, out in zip(before[:3] if held else (), outs):
        for part in range(3):
            out[:, part * HALF : part * HALF + held] = old[:, part * held : (part + 1) * held]


def project_attention_step(norms, weights, bias, proj, grads, pairs, after):
    tokens = grads[0].shape[0]
    out = jax.ShapeDtypeStruct((tokens, 3 * len(pairs) * PAIR), jnp.bfloat16)
    return pl.pallas_call(
        functools.partial(project_attention_kernel, pairs),
        out_shape=(jax.ShapeDtypeStruct(proj.shape, proj.dtype),) + (out,) * 4,
        in_specs=[spec()] * 14,
        out_specs=(spec(),) * 5,
        input_output_aliases={8: 0},
        compiler_params=pltpu.CompilerParams(vmem_limit_bytes=24 * 2**20),
        cost_estimate=cost(12),
        name="projection_attention",
    )(*norms, *weights, bias, proj, *grads, after)


def attention_step(proj, grads, pairs, before):
    tokens = grads[0].shape[0]
    widths = [3 * len(pairs) * PAIR] * 4
    for i in range(len(before)):
        widths[i] = 3 * HALF
    held = before[0].shape[1] // 3 if before else 0
    return pl.pallas_call(
        functools.partial(attention_kernel, pairs, held),
        out_shape=tuple(jax.ShapeDtypeStruct((tokens, width), jnp.bfloat16) for width in widths),
        in_specs=[spec()] * (5 + len(before)),
        out_specs=(spec(),) * 4,
        compiler_params=pltpu.CompilerParams(vmem_limit_bytes=24 * 2**20),
        cost_estimate=cost(12),
        name="attention",
    )(proj, *grads, *before)


def near_shard(refs, j):
    return refs[j][...] if j < 3 else jnp.concatenate([ref[...] for ref in refs[3:5]], axis=0)


def join_skip(first, second):
    wide, narrow = first.shape[1] // 3, second.shape[1] // 3
    pieces = []
    for part in range(3):
        pieces += [first[:, part * wide : (part + 1) * wide], second[:, part * narrow : (part + 1) * narrow]]
    return jnp.concatenate(pieces, axis=1)


def on_middle():
    place = lax.axis_index("seq")
    return (place == 1) | (place == 2)


def early_kernel(*refs):
    near_w, far_w = refs[0:5], {0: refs[5], 2: refs[6]}
    own_ref, skip_first, skip_second, tokens_ref, sums, normed_out, inverse_out = refs[7:]
    middle = on_middle()
    mine = lax.axis_index("weight")
    depth = far_w[0].shape[0]

    def fill(value, weights, far):
        for j in range(4):
            at = pl.ds(pl.multiple_of((mine ^ j) * depth, QBLOCK), depth)
            if not far or j in weights:
                sums[:, at] = dot_last(value, weights[j][...] if far else near_shard(weights, j))
            else:
                sums[:, at] = jnp.zeros((value.shape[0], depth), jnp.float32)

    pl.when(middle)(lambda: fill(own_ref[...], near_w, False))
    pl.when(jnp.logical_not(middle))(lambda: fill(join_skip(skip_first, skip_second), far_w, True))
    for r in range(0, tokens_ref.shape[1], 16):
        normed, inverse = norm_rows(tokens_ref[0, r : r + 16, :].astype(jnp.float32))
        normed_out[r : r + 16, :] = normed
        inverse_out[r : r + 16, :] = jnp.broadcast_to(inverse, (16, QBLOCK))


def early_step(near_w, far_w, own, skips, tokens):
    rows, width = tokens.shape[1:]
    full = jax.ShapeDtypeStruct((rows, width), jnp.float32)
    return pl.pallas_call(
        early_kernel,
        out_shape=(full, full, jax.ShapeDtypeStruct((rows, QBLOCK), jnp.float32)),
        in_specs=[spec()] * 11,
        out_specs=(spec(),) * 3,
        compiler_params=pltpu.CompilerParams(vmem_limit_bytes=24 * 2**20),
        cost_estimate=cost(50),
        name="grad_norm_part",
    )(*near_w, *far_w, own, *skips, tokens)


def pair_part_kernel(pair, skip_first, skip_second, sums, out_ref):
    mine = lax.axis_index("weight")
    depth = pair.shape[0] // 2
    out_ref[...] = sums[...]

    @pl.when(jnp.logical_not(on_middle()))
    def _():
        for i, j in enumerate((1, 3)):
            at = pl.ds(pl.multiple_of((mine ^ j) * depth, QBLOCK), depth)
            out_ref[:, at] = sums[:, at] + dot_last(
                join_skip(skip_first, skip_second), pair[i * depth : (i + 1) * depth]
            )


def pair_part_step(pair, skips, sums):
    return pl.pallas_call(
        pair_part_kernel,
        out_shape=jax.ShapeDtypeStruct(sums.shape, sums.dtype),
        in_specs=[spec()] * 4,
        out_specs=spec(),
        compiler_params=pltpu.CompilerParams(vmem_limit_bytes=24 * 2**20),
        cost_estimate=cost(0.01),
        name="pair_part",
    )(pair, *skips, sums)


def last_kernel(*refs):
    near_w, pair = refs[0:5], refs[7]
    back_ref, cross_ref, sums, normed_ref, inverse_ref, gain_ref, out_ref = refs[8:15]
    gain, grad_hat, first_sum, second_sum, result, sems = refs[15:]
    middle = on_middle()
    mine = lax.axis_index("weight")
    depth = refs[5].shape[0]
    far_w = (refs[5], pair.at[:depth], refs[6], pair.at[depth:])
    gain[...] = row_vector(gain_ref)

    def fill(value_ref, weight_of):
        value = value_ref[...]
        first = second = jnp.zeros(first_sum.shape, jnp.float32)
        for j in range(4):
            at = pl.ds(pl.multiple_of((mine ^ j) * depth, QBLOCK), depth)
            hat = (sums[:, at] + dot_last(value, weight_of(j))) * gain[:, at]
            grad_hat[:, at] = hat
            mixed = hat * normed_ref[:, at]
            for c in range(0, depth, QBLOCK):
                first += hat[:, c : c + QBLOCK]
                second += mixed[:, c : c + QBLOCK]
        first_sum[...] = first
        second_sum[...] = second

    pl.when(middle)(lambda: fill(cross_ref, lambda j: far_w[j][...]))
    pl.when(jnp.logical_not(middle))(lambda: fill(back_ref, lambda j: near_shard(near_w, j)))
    rows, width = normed_ref.shape
    copies = []
    for i, first in enumerate(range(0, rows, ROWS_OUT)):
        for r in range(first, first + ROWS_OUT, 8):
            at = slice(r, r + 8)
            first_mean = jnp.sum(first_sum[at, :], axis=-1, keepdims=True) * (1.0 / width)
            second_mean = jnp.sum(second_sum[at, :], axis=-1, keepdims=True) * (1.0 / width)
            result[at, :] = inverse_ref[at, :1] * (
                grad_hat[at, :] - first_mean - normed_ref[at, :] * second_mean
            )
        lines = pl.ds(first, ROWS_OUT)
        copies.append(pltpu.make_async_copy(result.at[lines, :], out_ref.at[0, lines, :], sems.at[i]))
        copies[-1].start()
    for copy in copies:
        copy.wait()


def last_step(near_w, far_w, back, cross, sums, normed, inverse, gain):
    return pl.pallas_call(
        last_kernel,
        out_shape=jax.ShapeDtypeStruct((1, *normed.shape), jnp.float32),
        in_specs=[spec()] * 14,
        out_specs=spec(pltpu.HBM),
        scratch_shapes=[
            VMEM((1, normed.shape[1]), jnp.float32),
            VMEM(normed.shape, jnp.float32),
            VMEM((normed.shape[0], QBLOCK), jnp.float32),
            VMEM((normed.shape[0], QBLOCK), jnp.float32),
            VMEM(normed.shape, jnp.float32),
            pltpu.SemaphoreType.DMA((normed.shape[0] // ROWS_OUT,)),
        ],
        compiler_params=pltpu.CompilerParams(vmem_limit_bytes=24 * 2**20),
        cost_estimate=cost(2),
        name="input_grad",
    )(*near_w, *far_w, back, cross, sums, normed, inverse, gain)


def split_kernel(value_ref, upper_ref, lower_ref):
    middle = upper_ref.shape[0]
    upper_ref[...] = value_ref[:middle]
    lower_ref[...] = value_ref[middle:]


def split_step(value):
    half = jax.ShapeDtypeStruct((value.shape[0] // 2, value.shape[1]), value.dtype)
    return pl.pallas_call(
        split_kernel,
        out_shape=(half, half),
        in_specs=[spec()],
        out_specs=(spec(), spec()),
        compiler_params=pltpu.CompilerParams(vmem_limit_bytes=16 * 2**20),
        cost_estimate=cost(0.01),
        name="split_rows",
    )(value)


def pair_kernel(first_ref, second_ref, after_ref, out_ref):
    middle = first_ref.shape[0]
    out_ref[:middle] = first_ref[...]
    out_ref[middle:] = second_ref[...]


def pair_step(first, second, after):
    return pl.pallas_call(
        pair_kernel,
        out_shape=jax.ShapeDtypeStruct((2 * first.shape[0], first.shape[1]), first.dtype),
        in_specs=[spec()] * 3,
        out_specs=spec(),
        compiler_params=pltpu.CompilerParams(vmem_limit_bytes=16 * 2**20),
        cost_estimate=cost(0.01),
        name="chip_weight",
    )(first, second, after)


END_TO_MIDDLE = [(0, 1), (3, 2)]
MIDDLE = [(1, 2), (2, 1)]
END_TO_FAR = [(0, 2), (3, 1)]
MIDDLE_TO_END = [(1, 0), (2, 3)]
FAR_TO_END = [(1, 3), (2, 0)]


def flip(bit):
    return [(i, i ^ bit) for i in range(4)]


def local_middle(
    tokens,
    upstream_grad,
    norm_gain,
    norm_bias,
    input_codes,
    input_scales,
    input_bias,
    output_codes,
    output_scales,
    layer_scale,
):
    near, both_near, both_other = first_step(
        tokens, norm_gain, norm_bias, input_scales, input_codes, upstream_grad, layer_scale, output_scales, output_codes
    )
    both_mid = lax.ppermute(both_other, "seq", MIDDLE)
    both_far = lax.ppermute(both_other, "seq", END_TO_FAR)
    both_end = lax.ppermute(both_near, "seq", END_TO_MIDDLE)
    near_across = lax.ppermute(near, "weight", flip(2))
    near_beside = lax.ppermute(near, "weight", flip(1))
    near_diagonal = [lax.ppermute(w, "weight", flip(1)) for w in split_step(near_across)]
    far = far_step(input_scales, input_codes, near_across)
    far_across = lax.ppermute(far, "weight", flip(2))
    rows = (both_near, both_end, both_mid, both_far)
    near_w = (near, near_beside, near_across, *near_diagonal)
    proj = project_step(rows[:2], near_w, input_bias)
    grads = (both_near, both_end, both_mid, both_far)
    proj, *kept, skip_first = project_attention_step(
        rows[2:], near_w, input_bias, proj, grads, (0, 1), far
    )
    skip_first = lax.ppermute(skip_first, "seq", FAR_TO_END)
    own, end, mid, skip_second = attention_step(proj, grads, (2,), kept)
    skip_second = lax.ppermute(skip_second, "seq", FAR_TO_END)
    cross = lax.ppermute(mid, "seq", MIDDLE)
    back = lax.ppermute(end, "seq", MIDDLE_TO_END)
    far_pair = lax.ppermute(pair_step(far, far_across, skip_second), "weight", flip(1))
    far_w = (far, far_across)
    skips = (skip_first, skip_second)
    sums, normed, inverse = early_step(near_w, far_w, own, skips, tokens)
    sums = pair_part_step(far_pair, skips, sums)
    return last_step(near_w, (*far_w, far_pair), back, cross, sums, normed, inverse, norm_gain)


def dequantize(codes, scales):
    expanded = jnp.repeat(jnp.repeat(scales, QBLOCK, axis=0), QBLOCK, axis=1)
    return (codes.astype(jnp.float32) * expanded).astype(jnp.bfloat16)


def normalize(rows, gain, shift):
    mean_value = jnp.mean(rows, axis=-1, keepdims=True)
    centered = rows - mean_value
    variance = jnp.mean(centered * centered, axis=-1, keepdims=True)
    inverse = lax.rsqrt(variance + 1e-06)
    normed = centered * inverse
    return (normed, inverse, (normed * gain + shift).astype(jnp.bfloat16))


def norm_backward(grad_norm, normed, inverse, gain):
    grad_hat = grad_norm * gain
    first_mean = jnp.mean(grad_hat, axis=-1, keepdims=True)
    second_mean = jnp.mean(grad_hat * normed, axis=-1, keepdims=True)
    return inverse * (grad_hat - first_mean - normed * second_mean)


def score_block(queries, head_grads, pair_block):
    row_count = pair_block.shape[0]
    keys_blk = pair_block[:, :HD].reshape(row_count, HEADS, HEAD_DIM)
    values_blk = pair_block[:, HD:].reshape(row_count, HEADS, HEAD_DIM)
    scores = jnp.einsum(
        "qhd,khd->hqk", queries, keys_blk, preferred_element_type=jnp.float32
    ) * HEAD_DIM ** (-0.5)
    dprob = jnp.einsum("qhd,khd->hqk", head_grads, values_blk, preferred_element_type=jnp.float32)
    return (keys_blk, scores, dprob)


def update_stats(statistics, queries, head_grads, pair_rows):
    sub_size = math.gcd(pair_rows.shape[0], 512)

    def visit_block(block_index, running):
        run_max, run_total, run_mix = running
        pair_block = lax.dynamic_slice_in_dim(pair_rows, block_index * sub_size, sub_size, 0)
        keys_blk, scores, dprob = score_block(queries, head_grads, pair_block)
        new_max = jnp.maximum(run_max, jnp.max(scores, axis=-1))
        factor = jnp.exp(run_max - new_max)
        expo = jnp.exp(scores - new_max[..., None])
        return (
            new_max,
            run_total * factor + jnp.sum(expo, axis=-1),
            run_mix * factor + jnp.sum(expo * dprob, axis=-1),
        )

    return lax.fori_loop(0, pair_rows.shape[0] // sub_size, visit_block, statistics)


def block_backward(queries, head_grads, pair_block, log_total, row_delta):
    keys_blk, scores, dprob = score_block(queries, head_grads, pair_block)
    weights = jnp.exp(scores - log_total[..., None])
    prob_weights = weights.astype(jnp.bfloat16)
    dscore = (weights * (dprob - row_delta[..., None])).astype(jnp.bfloat16)
    return (keys_blk, prob_weights, dscore)


def key_terms_from(queries, head_grads, prob_weights, dscore):
    key_part = jnp.einsum(
        "hqk,qhd->khd", dscore, queries, preferred_element_type=jnp.float32
    ) * HEAD_DIM ** (-0.5)
    value_part = jnp.einsum(
        "hqk,qhd->khd", prob_weights, head_grads, preferred_element_type=jnp.float32
    )
    row_count = key_part.shape[0]
    return jnp.concatenate(
        [key_part.reshape(row_count, HD), value_part.reshape(row_count, HD)], axis=1
    )


def query_side(queries, head_grads, keys_values, local_rows):
    seq_rows = local_rows * lax.axis_size("seq")
    start_stats = (
        jnp.full((HEADS, local_rows), -1e30, jnp.float32),
        jnp.zeros((HEADS, local_rows), jnp.float32),
        jnp.zeros((HEADS, local_rows), jnp.float32),
    )
    all_pairs = lax.all_gather(keys_values, "seq", axis=0, tiled=True)
    statistics = update_stats(start_stats, queries, head_grads, all_pairs)
    row_max, row_total, row_mix = statistics
    log_total = row_max + jnp.log(row_total)
    row_delta = row_mix / row_total
    sub_size = math.gcd(seq_rows, 512)
    block_count = seq_rows // sub_size
    empty_query = jnp.zeros((local_rows, HEADS, HEAD_DIM), jnp.float32)

    def backward_step(block_index, running):
        query_grad, buffer = running
        pair_block = lax.dynamic_slice_in_dim(all_pairs, block_index * sub_size, sub_size, 0)
        keys_blk, prob_weights, dscore = block_backward(
            queries, head_grads, pair_block, log_total, row_delta
        )
        query_grad = query_grad + jnp.einsum(
            "hqk,khd->qhd", dscore, keys_blk, preferred_element_type=jnp.float32
        )
        block_terms = key_terms_from(queries, head_grads, prob_weights, dscore)
        buffer = lax.dynamic_update_slice_in_dim(buffer, block_terms, block_index * sub_size, 0)
        return (query_grad, buffer)

    empty_terms = jnp.zeros((seq_rows, 2 * HD), jnp.float32)
    query_grad, buffer = lax.fori_loop(0, block_count, backward_step, (empty_query, empty_terms))
    pair_grads = lax.psum_scatter(
        buffer.astype(jnp.bfloat16), "seq", scatter_dimension=0, tiled=True
    ).astype(jnp.float32)
    return (query_grad, pair_grads)


def local(
    tokens,
    upstream_grad,
    norm_gain,
    norm_bias,
    input_codes,
    input_scales,
    input_bias,
    output_codes,
    output_scales,
    layer_scale,
):
    all_codes, all_scales = (
        lax.all_gather(input_codes.astype(jnp.float32), "weight", axis=0, tiled=True).astype(
            input_codes.dtype
        ),
        lax.all_gather(input_scales, "weight", axis=0, tiled=True),
    )
    input_weight = dequantize(all_codes, all_scales)
    output_weight = dequantize(output_codes, output_scales)
    normed, inverse, norm_out = normalize(tokens[0].astype(jnp.float32), norm_gain, norm_bias)
    projected = (
        jnp.dot(norm_out, input_weight, preferred_element_type=jnp.float32) + input_bias
    ).astype(jnp.bfloat16)
    local_rows = projected.shape[0]
    queries = projected[:, :HD].reshape(local_rows, HEADS, HEAD_DIM)
    keys_values = projected[:, HD:]
    scaled_grad = (upstream_grad[0].astype(jnp.float32) * layer_scale).astype(jnp.bfloat16)
    head_grads = jnp.dot(scaled_grad, output_weight.T, preferred_element_type=jnp.float32).astype(
        jnp.bfloat16
    )
    head_grads = head_grads.reshape(local_rows, HEADS, HEAD_DIM)
    query_grad, pair_grads = query_side(queries, head_grads, keys_values, local_rows)
    query_grad = (query_grad * HEAD_DIM ** (-0.5)).reshape(local_rows, HD)
    grad_proj = jnp.concatenate([query_grad, pair_grads], axis=1).astype(jnp.bfloat16)
    grad_norm = jnp.dot(grad_proj, input_weight.T, preferred_element_type=jnp.float32)
    result = norm_backward(grad_norm, normed, inverse, norm_gain)
    return result[None]


def solution(mesh):
    in_specs = (
        P(("groups", "weight"), "seq", None),
        P(("groups", "weight"), "seq", None),
        P(),
        P(),
        P("weight", None),
        P("weight", None),
        P(),
        P(),
        P(),
        P(),
    )
    out_specs = P(("groups", "weight"), "seq", None)
    fits = mesh.shape["seq"] == 4 and mesh.shape["weight"] == 4
    plan = local_middle if fits else local
    return jax.shard_map(plan, mesh=mesh, in_specs=in_specs, out_specs=out_specs, check_vma=False)
```

```python
import functools
import math

import jax
import jax.numpy as jnp
from jax import lax
from jax.experimental import pallas as pl
from jax.experimental.pallas import tpu as pltpu
from jax.sharding import PartitionSpec as P

HEADS = 12
HEAD_DIM = 64
QBLOCK = 128
HD = 768
HALF = HD // 2
ROWS_OUT = 32
EPSILON = 1e-06
VMEM = pltpu.VMEM
SMEM = pltpu.SMEM


def half_index():
    return lax.axis_index("seq") * 2 // lax.axis_size("seq")


def cost(micros):
    return pl.CostEstimate(flops=int(micros * 1.0e9), bytes_accessed=int(micros * 3.0e6), transcendentals=0)


def spec(memory_space=VMEM):
    return pl.BlockSpec(memory_space=memory_space)


def norm_rows(rows):
    mean_value = jnp.mean(rows, axis=-1, keepdims=True)
    centered = rows - mean_value
    variance = jnp.mean(centered * centered, axis=-1, keepdims=True)
    inverse = lax.rsqrt(variance + EPSILON)
    return centered * inverse, inverse


def row_vector(ref):
    return ref[...].reshape(1, ref.shape[0])


def scale_block(codes, scale):
    return (codes.astype(jnp.float32) * scale).astype(jnp.bfloat16)


def first_kernel(
    tokens_ref, gain_ref, shift_ref, scales_ref, codes_ref, grad_ref, layer_ref, out_scales_ref, out_codes_ref,
    weight_out, near_out, far_out,
    tokens, gain, shift, scales, codes, grad, layer, out_scales, out_codes, scaled, weight, far, sems
):
    half = half_index()
    other = 1 - half
    blocks = HALF // QBLOCK

    def copy(source, target, at):
        started = pltpu.make_async_copy(source, target, sems.at[at])
        started.start()
        return started

    def columns(part):
        return codes_ref.at[:, pl.ds(pl.multiple_of(part * HD + half * HALF, QBLOCK), HALF)]

    def rows(which):
        return out_codes_ref.at[pl.ds(pl.multiple_of(which * HALF, QBLOCK), HALF), :]

    scales_copy = copy(scales_ref, scales, 0)
    codes_copies = [copy(columns(part), codes.at[part], 1 + part) for part in range(3)]
    tokens_copies = [
        copy(tokens_ref, tokens, 4), copy(gain_ref, gain, 5), copy(shift_ref, shift, 6)
    ]
    grad_copies = [
        copy(grad_ref, grad, 7), copy(layer_ref, layer, 8), copy(out_scales_ref, out_scales, 9)
    ]
    out_copies = [copy(rows(other), out_codes.at[0], 10), copy(rows(half), out_codes.at[1], 11)]

    scales_copy.wait()
    for part in range(3):
        codes_copies[part].wait()
        for r in range(codes_ref.shape[0] // QBLOCK):
            for c in range(blocks):
                scale = scales[r, (part * HD) // QBLOCK + half * blocks + c]
                lines = slice(r * QBLOCK, (r + 1) * QBLOCK)
                weight_out[lines, part * HALF + c * QBLOCK : part * HALF + (c + 1) * QBLOCK] = scale_block(
                    codes[part, lines, c * QBLOCK : (c + 1) * QBLOCK], scale
                )

    for started in tokens_copies:
        started.wait()
    width = tokens.shape[2]
    gain_row = row_vector(gain)
    shift_row = row_vector(shift)
    for r in range(0, tokens.shape[1], 16):
        normed, _ = norm_rows(tokens[0, r : r + 16, :].astype(jnp.float32))
        norm_out = (normed * gain_row + shift_row).astype(jnp.bfloat16)
        near_out[r : r + 16, :width] = norm_out
        far[r : r + 16, :width] = norm_out

    for started in grad_copies:
        started.wait()
    scaled[...] = (grad[0].astype(jnp.float32) * row_vector(layer)).astype(jnp.bfloat16)
    for i, (out_ref, which) in enumerate(((far, other), (near_out, half))):
        out_copies[i].wait()
        for r in range(blocks):
            lines = slice(r * QBLOCK, (r + 1) * QBLOCK)
            for c in range(width // QBLOCK):
                at = slice(c * QBLOCK, (c + 1) * QBLOCK)
                weight[lines, at] = scale_block(out_codes[i, lines, at], out_scales[which * blocks + r, c])
        out_ref[:, width:] = dot_last(scaled[...], weight[...]).astype(jnp.bfloat16)
        if out_ref is far:
            far_copy = copy(far, far_out, 12)
    far_copy.wait()


def first_step(tokens, gain, shift, scales, codes, grad, layer_scale, out_scales, out_codes):
    lines, width = tokens.shape[1:]
    depth = codes.shape[0]
    return pl.pallas_call(
        first_kernel,
        out_shape=(
            VMEM((depth, 3 * HALF), jnp.bfloat16),
            VMEM((lines, width + HALF), jnp.bfloat16),
            jax.ShapeDtypeStruct((lines, width + HALF), jnp.bfloat16),
        ),
        in_specs=[spec(pltpu.HBM)] * 9,
        out_specs=(spec(), spec(), spec(pltpu.HBM)),
        scratch_shapes=[
            VMEM(tokens.shape, tokens.dtype),
            VMEM(gain.shape, gain.dtype),
            VMEM(shift.shape, shift.dtype),
            SMEM(scales.shape, scales.dtype),
            VMEM((3, depth, HALF), codes.dtype),
            VMEM(grad.shape, grad.dtype),
            VMEM(layer_scale.shape, layer_scale.dtype),
            SMEM(out_scales.shape, out_scales.dtype),
            VMEM((2, HALF, width), out_codes.dtype),
            VMEM((lines, width), jnp.bfloat16),
            VMEM((HALF, width), jnp.bfloat16),
            VMEM((lines, width + HALF), jnp.bfloat16),
            pltpu.SemaphoreType.DMA((13,)),
        ],
        compiler_params=pltpu.CompilerParams(vmem_limit_bytes=60 * 2**20),
        cost_estimate=cost(3),
        name="first_weights_and_rows",
    )(tokens, gain, shift, scales, codes, grad, layer_scale, out_scales, out_codes)


def far_kernel(scales_ref, codes_ref, after_ref, weight_out, scales, codes, sems):
    other = 1 - half_index()
    blocks = HALF // QBLOCK
    copies = [pltpu.make_async_copy(scales_ref, scales, sems.at[3])]
    for part in range(3):
        at = pl.ds(pl.multiple_of(part * HD + other * HALF, QBLOCK), HALF)
        copies.append(pltpu.make_async_copy(codes_ref.at[:, at], codes.at[part], sems.at[part]))
    for started in copies:
        started.start()
    for started in copies:
        started.wait()
    for part in range(3):
        for r in range(codes_ref.shape[0] // QBLOCK):
            for c in range(blocks):
                scale = scales[r, (part * HD) // QBLOCK + other * blocks + c]
                lines = slice(r * QBLOCK, (r + 1) * QBLOCK)
                weight_out[lines, part * HALF + c * QBLOCK : part * HALF + (c + 1) * QBLOCK] = scale_block(
                    codes[part, lines, c * QBLOCK : (c + 1) * QBLOCK], scale
                )


def far_step(scales, codes, after):
    depth = codes.shape[0]
    return pl.pallas_call(
        far_kernel,
        out_shape=jax.ShapeDtypeStruct((depth, 3 * HALF), jnp.bfloat16),
        in_specs=[spec(pltpu.HBM), spec(pltpu.HBM), spec()],
        out_specs=spec(),
        scratch_shapes=[
            SMEM(scales.shape, scales.dtype),
            VMEM((3, depth, HALF), codes.dtype),
            pltpu.SemaphoreType.DMA((4,)),
        ],
        compiler_params=pltpu.CompilerParams(vmem_limit_bytes=16 * 2**20),
        cost_estimate=cost(0.01),
        name="far_weight",
    )(scales, codes, after)


def dot_last(a, b):
    return lax.dot_general(a, b, (((1,), (1,)), ((), ())), preferred_element_type=jnp.float32)


def dot_plain(a, b):
    return jnp.dot(a, b, preferred_element_type=jnp.float32)


def norm_columns(norms, picks, depth):
    mine = lax.axis_index("weight")
    return jnp.concatenate(
        [
            jnp.concatenate(
                [norm_ref[:, pl.ds(pl.multiple_of((mine ^ j) * depth, QBLOCK), depth)] for j in picks],
                axis=1,
            )
            for norm_ref in norms
        ],
        axis=0,
    )


def project_part(norms, weights, bias_ref, proj, first, part):
    half = half_index()
    rows = norm_columns(norms, range(4), weights[0].shape[0])
    bias = row_vector(bias_ref)
    at = slice(part * HALF, (part + 1) * HALF)
    shift = jnp.where(
        half == 0,
        bias[:, part * HD : part * HD + HALF],
        bias[:, part * HD + HALF : (part + 1) * HD],
    )
    columns = jnp.concatenate([w[:, at] for w in weights], axis=0)
    value = (dot_plain(rows, columns) + shift).astype(jnp.bfloat16)
    if part == 0:
        value = value * jnp.bfloat16(HEAD_DIM**-0.5)
    proj[first : first + rows.shape[0], at] = value


def project_kernel(*refs):
    for part in range(3):
        project_part(refs[0:2], refs[2:7], refs[7], refs[8], 0, part)


def project_step(norms, weights, bias):
    tokens = norms[0].shape[0]
    return pl.pallas_call(
        project_kernel,
        out_shape=jax.ShapeDtypeStruct((4 * tokens, 3 * HALF), jnp.bfloat16),
        in_specs=[spec()] * 8,
        out_specs=spec(),
        compiler_params=pltpu.CompilerParams(vmem_limit_bytes=24 * 2**20),
        cost_estimate=cost(0.01),
        name="projection",
    )(*norms, *weights, bias)


PAIR = 2 * HEAD_DIM


def soft_part(scores, dprob):
    expo = jnp.exp(scores - jnp.max(scores, axis=0, keepdims=True))
    scale = 1.0 / jnp.sum(expo, axis=0, keepdims=True)
    delta = jnp.sum(expo * dprob, axis=0, keepdims=True) * scale
    prob = (expo * scale).astype(jnp.bfloat16)
    return prob, prob * (dprob - delta).astype(jnp.bfloat16)


def attention_kernel(pairs, held, *refs):
    proj, grads, before, outs = refs[0], refs[1:5], refs[5:-4], refs[-4:]
    attention(pairs, held, proj, grads, before, outs)


def project_attention_kernel(pairs, *refs):
    norms, weights, bias_ref, proj_in, grads = refs[0:2], refs[2:7], refs[7], refs[8], refs[9:13]
    proj, outs = refs[-5], refs[-4:]
    tokens = norms[0].shape[0]
    proj[: 2 * tokens] = proj_in[: 2 * tokens]

    def project(part):
        project_part(norms, weights, bias_ref, proj, 2 * tokens, part)

    project(0)
    project(1)
    attention(pairs, 0, proj, grads, (), outs, lambda: project(2))


def attention(pairs, held, proj, grads, before, outs, between=None):
    total = proj.shape[0]
    tokens = grads[0].shape[0]
    low = lax.broadcasted_iota(jnp.int32, (total, PAIR), 1) < HEAD_DIM
    zero = jnp.zeros((total, PAIR), jnp.bfloat16)

    def load(t):
        query, key, value = (proj[:, part * HALF + t * PAIR : part * HALF + (t + 1) * PAIR] for part in range(3))
        grad = jnp.concatenate(
            [g[:, g.shape[1] - HALF + t * PAIR : g.shape[1] - HALF + (t + 1) * PAIR] for g in grads], axis=0
        )
        return query, key, value, grad

    def mask(side, value):
        return jnp.where(low, value, zero) if side == 0 else jnp.where(low, zero, value)

    def before_soft(t, side, between=None):
        query, key, value, grad = load(t)
        scores = dot_last(mask(side, key), query)
        if between is not None:
            between()
            value = load(t)[2]
        return scores, dot_last(mask(side, value), grad)

    def after_soft(t, side, prob, dscore):
        query, key, _, grad = load(t)
        key_t = key.T[side * HEAD_DIM : (side + 1) * HEAD_DIM]
        return (
            dot_plain(key_t, dscore),
            dot_plain(dscore, mask(side, query)),
            dot_plain(prob, mask(side, grad)),
        )

    def store(t, first, second):
        place = pairs.index(t)
        query_grad = jnp.concatenate([first[0], second[0]], axis=0).T * HEAD_DIM**-0.5
        for part, piece in enumerate((query_grad, first[1] + second[1], first[2] + second[2])):
            piece = piece.astype(jnp.bfloat16)
            for i, out in enumerate(outs):
                whole = out.shape[1] == 3 * HALF
                at = part * HALF + t * PAIR if whole else (part * len(pairs) + place) * PAIR
                out[:, at : at + PAIR] = piece[i * tokens : (i + 1) * tokens]

    heads = [(t, side) for t in pairs for side in range(2)]
    done = {}

    def finish(t, side, *soft):
        done[t, side] = after_soft(t, side, *soft)
        if side == 1:
            store(t, done[t, 0], done[t, 1])

    ready, behind = before_soft(*heads[0], between), None
    for i, head in enumerate(heads):
        now = ready
        if i + 1 < len(heads):
            ready = before_soft(*heads[i + 1])
        if behind is not None:
            finish(*behind)
        behind = (*head, *soft_part(*now))
    finish(*behind)
    for old, out in zip(before, outs[0:3:2]):
        for part in range(3):
            out[:, part * HALF : part * HALF + held] = old[:, part * held : (part + 1) * held]


def project_attention_step(norms, weights, bias, proj, grads, pairs, after):
    tokens = grads[0].shape[0]
    out = jax.ShapeDtypeStruct((tokens, 3 * len(pairs) * PAIR), jnp.bfloat16)
    return pl.pallas_call(
        functools.partial(project_attention_kernel, pairs),
        out_shape=(jax.ShapeDtypeStruct(proj.shape, proj.dtype),) + (out,) * 4,
        in_specs=[spec()] * 14,
        out_specs=(spec(),) * 5,
        input_output_aliases={8: 0},
        compiler_params=pltpu.CompilerParams(vmem_limit_bytes=24 * 2**20),
        cost_estimate=cost(12),
        name="projection_attention",
    )(*norms, *weights, bias, proj, *grads, after)


def attention_step(proj, grads, pairs, before):
    tokens = grads[0].shape[0]
    widths = [3 * len(pairs) * PAIR] * 4
    for i in range(len(before)):
        widths[2 * i] = 3 * HALF
    held = before[0].shape[1] // 3 if before else 0
    return pl.pallas_call(
        functools.partial(attention_kernel, pairs, held),
        out_shape=tuple(jax.ShapeDtypeStruct((tokens, width), jnp.bfloat16) for width in widths),
        in_specs=[spec()] * (5 + len(before)),
        out_specs=(spec(),) * 4,
        compiler_params=pltpu.CompilerParams(vmem_limit_bytes=24 * 2**20),
        cost_estimate=cost(12),
        name="attention",
    )(proj, *grads, *before)


def near_shard(refs, j, pairs=None):
    def columns(ref):
        if pairs is None:
            return ref[...]
        first, last = pairs[0] * PAIR, (pairs[-1] + 1) * PAIR
        return jnp.concatenate([ref[:, part * HALF + first : part * HALF + last] for part in range(3)], axis=1)

    return columns(refs[j]) if j < 3 else jnp.concatenate([columns(ref) for ref in refs[3:5]], axis=0)


def join_skip(first, second):
    wide, narrow = first.shape[1] // 3, second.shape[1] // 3
    pieces = []
    for part in range(3):
        pieces += [first[:, part * wide : (part + 1) * wide], second[:, part * narrow : (part + 1) * narrow]]
    return jnp.concatenate(pieces, axis=1)


def on_middle():
    place = lax.axis_index("seq")
    return (place == 1) | (place == 2)


def early_kernel(*refs):
    near_w, far_w = refs[0:5], {0: refs[5], 2: refs[6]}
    own_ref, skip_first, skip_second, tokens_ref, sums, normed_out, inverse_out = refs[7:]
    middle = on_middle()
    mine = lax.axis_index("weight")
    depth = far_w[0].shape[0]

    def fill(value, weights, far):
        for j in range(4):
            at = pl.ds(pl.multiple_of((mine ^ j) * depth, QBLOCK), depth)
            if not far or j in weights:
                sums[:, at] = dot_last(value, weights[j][...] if far else near_shard(weights, j))
            else:
                sums[:, at] = jnp.zeros((value.shape[0], depth), jnp.float32)

    pl.when(middle)(lambda: fill(own_ref[...], near_w, False))
    pl.when(jnp.logical_not(middle))(lambda: fill(join_skip(skip_first, skip_second), far_w, True))
    for r in range(0, tokens_ref.shape[1], 16):
        normed, inverse = norm_rows(tokens_ref[0, r : r + 16, :].astype(jnp.float32))
        normed_out[r : r + 16, :] = normed
        inverse_out[r : r + 16, :] = jnp.broadcast_to(inverse, (16, QBLOCK))


def early_step(near_w, far_w, own, skips, tokens):
    rows, width = tokens.shape[1:]
    full = jax.ShapeDtypeStruct((rows, width), jnp.float32)
    return pl.pallas_call(
        early_kernel,
        out_shape=(full, full, jax.ShapeDtypeStruct((rows, QBLOCK), jnp.float32)),
        in_specs=[spec()] * 11,
        out_specs=(spec(),) * 3,
        compiler_params=pltpu.CompilerParams(vmem_limit_bytes=24 * 2**20),
        cost_estimate=cost(50),
        name="grad_norm_part",
    )(*near_w, *far_w, own, *skips, tokens)


def pair_part_kernel(*refs):
    near_w = refs[0:5]
    pair, skip_first, skip_second, back_first, sums, out_ref = refs[5:]
    mine = lax.axis_index("weight")
    depth = pair.shape[0] // 2
    out_ref[...] = sums[...]

    @pl.when(jnp.logical_not(on_middle()))
    def _():
        skip = join_skip(skip_first, skip_second)
        for j in range(4):
            at = pl.ds(pl.multiple_of((mine ^ j) * depth, QBLOCK), depth)
            total = sums[:, at] + dot_last(back_first[...], near_shard(near_w, j, EARLY))
            if j % 2 == 1:
                total += dot_last(skip, pair[j // 2 * depth : (j // 2 + 1) * depth])
            out_ref[:, at] = total


def pair_part_step(near_w, pair, skips, back_first, sums):
    return pl.pallas_call(
        pair_part_kernel,
        out_shape=jax.ShapeDtypeStruct(sums.shape, sums.dtype),
        in_specs=[spec()] * 10,
        out_specs=spec(),
        compiler_params=pltpu.CompilerParams(vmem_limit_bytes=24 * 2**20),
        cost_estimate=cost(0.01),
        name="pair_part",
    )(*near_w, pair, *skips, back_first, sums)


def last_kernel(*refs):
    near_w, pair = refs[0:5], refs[7]
    sums, back_ref, cross_ref, normed_ref, inverse_ref, gain_ref, out_ref = refs[8:15]
    gain, grad_hat, first_sum, second_sum, result, sems = refs[15:]
    middle = on_middle()
    mine = lax.axis_index("weight")
    depth = refs[5].shape[0]
    far_w = (refs[5], pair.at[:depth], refs[6], pair.at[depth:])
    gain[...] = row_vector(gain_ref)

    def fill(value_ref, weight_of):
        value = value_ref[...]
        first = second = jnp.zeros(first_sum.shape, jnp.float32)
        for j in range(4):
            at = pl.ds(pl.multiple_of((mine ^ j) * depth, QBLOCK), depth)
            hat = (sums[:, at] + dot_last(value, weight_of(j))) * gain[:, at]
            grad_hat[:, at] = hat
            mixed = hat * normed_ref[:, at]
            for c in range(0, depth, QBLOCK):
                first += hat[:, c : c + QBLOCK]
                second += mixed[:, c : c + QBLOCK]
        first_sum[...] = first
        second_sum[...] = second

    pl.when(middle)(lambda: fill(cross_ref, lambda j: far_w[j][...]))
    pl.when(jnp.logical_not(middle))(lambda: fill(back_ref, lambda j: near_shard(near_w, j, LATE)))
    rows, width = normed_ref.shape
    copies = []
    for i, first in enumerate(range(0, rows, ROWS_OUT)):
        for r in range(first, first + ROWS_OUT, 8):
            at = slice(r, r + 8)
            first_mean = jnp.sum(first_sum[at, :], axis=-1, keepdims=True) * (1.0 / width)
            second_mean = jnp.sum(second_sum[at, :], axis=-1, keepdims=True) * (1.0 / width)
            result[at, :] = inverse_ref[at, :1] * (
                grad_hat[at, :] - first_mean - normed_ref[at, :] * second_mean
            )
        lines = pl.ds(first, ROWS_OUT)
        copies.append(pltpu.make_async_copy(result.at[lines, :], out_ref.at[0, lines, :], sems.at[i]))
        copies[-1].start()
    for copy in copies:
        copy.wait()


def last_step(near_w, far_w, back, cross, sums, normed, inverse, gain):
    return pl.pallas_call(
        last_kernel,
        out_shape=jax.ShapeDtypeStruct((1, *normed.shape), jnp.float32),
        in_specs=[spec()] * 14,
        out_specs=spec(pltpu.HBM),
        scratch_shapes=[
            VMEM((1, normed.shape[1]), jnp.float32),
            VMEM(normed.shape, jnp.float32),
            VMEM((normed.shape[0], QBLOCK), jnp.float32),
            VMEM((normed.shape[0], QBLOCK), jnp.float32),
            VMEM(normed.shape, jnp.float32),
            pltpu.SemaphoreType.DMA((normed.shape[0] // ROWS_OUT,)),
        ],
        compiler_params=pltpu.CompilerParams(vmem_limit_bytes=24 * 2**20),
        cost_estimate=cost(2),
        name="input_grad",
    )(*near_w, *far_w, sums, back, cross, normed, inverse, gain)


def split_kernel(value_ref, upper_ref, lower_ref):
    middle = upper_ref.shape[0]
    upper_ref[...] = value_ref[:middle]
    lower_ref[...] = value_ref[middle:]


def split_step(value):
    half = jax.ShapeDtypeStruct((value.shape[0] // 2, value.shape[1]), value.dtype)
    return pl.pallas_call(
        split_kernel,
        out_shape=(half, half),
        in_specs=[spec()],
        out_specs=(spec(), spec()),
        compiler_params=pltpu.CompilerParams(vmem_limit_bytes=16 * 2**20),
        cost_estimate=cost(0.01),
        name="split_rows",
    )(value)


def pair_kernel(first_ref, second_ref, after_ref, out_ref):
    middle = first_ref.shape[0]
    out_ref[:middle] = first_ref[...]
    out_ref[middle:] = second_ref[...]


def pair_step(first, second, after):
    return pl.pallas_call(
        pair_kernel,
        out_shape=jax.ShapeDtypeStruct((2 * first.shape[0], first.shape[1]), first.dtype),
        in_specs=[spec()] * 3,
        out_specs=spec(),
        compiler_params=pltpu.CompilerParams(vmem_limit_bytes=16 * 2**20),
        cost_estimate=cost(0.01),
        name="chip_weight",
    )(first, second, after)


EARLY = (0, 1)
LATE = (2,)
END_TO_MIDDLE = [(0, 1), (3, 2)]
MIDDLE = [(1, 2), (2, 1)]
END_TO_FAR = [(0, 2), (3, 1)]
MIDDLE_TO_END = [(1, 0), (2, 3)]
FAR_TO_END = [(1, 3), (2, 0)]


def flip(bit):
    return [(i, i ^ bit) for i in range(4)]


def local_middle(
    tokens,
    upstream_grad,
    norm_gain,
    norm_bias,
    input_codes,
    input_scales,
    input_bias,
    output_codes,
    output_scales,
    layer_scale,
):
    near, both_near, both_other = first_step(
        tokens, norm_gain, norm_bias, input_scales, input_codes, upstream_grad, layer_scale, output_scales, output_codes
    )
    both_mid = lax.ppermute(both_other, "seq", MIDDLE)
    both_far = lax.ppermute(both_other, "seq", END_TO_FAR)
    both_end = lax.ppermute(both_near, "seq", END_TO_MIDDLE)
    near_across = lax.ppermute(near, "weight", flip(2))
    near_beside = lax.ppermute(near, "weight", flip(1))
    near_diagonal = [lax.ppermute(w, "weight", flip(1)) for w in split_step(near_across)]
    far = far_step(input_scales, input_codes, near_across)
    far_across = lax.ppermute(far, "weight", flip(2))
    rows = (both_near, both_end, both_mid, both_far)
    near_w = (near, near_beside, near_across, *near_diagonal)
    proj = project_step(rows[:2], near_w, input_bias)
    grads = (both_near, both_end, both_mid, both_far)
    proj, own, end, mid, skip_first = project_attention_step(
        rows[2:], near_w, input_bias, proj, grads, EARLY, far
    )
    back_first = lax.ppermute(end, "seq", MIDDLE_TO_END)
    skip_first = lax.ppermute(skip_first, "seq", FAR_TO_END)
    own, end, mid, skip_second = attention_step(proj, grads, LATE, (own, mid))
    skip_second = lax.ppermute(skip_second, "seq", FAR_TO_END)
    cross = lax.ppermute(mid, "seq", MIDDLE)
    back = lax.ppermute(end, "seq", MIDDLE_TO_END)
    far_pair = lax.ppermute(pair_step(far, far_across, skip_second), "weight", flip(1))
    far_w = (far, far_across)
    skips = (skip_first, skip_second)
    sums, normed, inverse = early_step(near_w, far_w, own, skips, tokens)
    sums = pair_part_step(near_w, far_pair, skips, back_first, sums)
    return last_step(near_w, (*far_w, far_pair), back, cross, sums, normed, inverse, norm_gain)


def dequantize(codes, scales):
    expanded = jnp.repeat(jnp.repeat(scales, QBLOCK, axis=0), QBLOCK, axis=1)
    return (codes.astype(jnp.float32) * expanded).astype(jnp.bfloat16)


def normalize(rows, gain, shift):
    mean_value = jnp.mean(rows, axis=-1, keepdims=True)
    centered = rows - mean_value
    variance = jnp.mean(centered * centered, axis=-1, keepdims=True)
    inverse = lax.rsqrt(variance + 1e-06)
    normed = centered * inverse
    return (normed, inverse, (normed * gain + shift).astype(jnp.bfloat16))


def norm_backward(grad_norm, normed, inverse, gain):
    grad_hat = grad_norm * gain
    first_mean = jnp.mean(grad_hat, axis=-1, keepdims=True)
    second_mean = jnp.mean(grad_hat * normed, axis=-1, keepdims=True)
    return inverse * (grad_hat - first_mean - normed * second_mean)


def score_block(queries, head_grads, pair_block):
    row_count = pair_block.shape[0]
    keys_blk = pair_block[:, :HD].reshape(row_count, HEADS, HEAD_DIM)
    values_blk = pair_block[:, HD:].reshape(row_count, HEADS, HEAD_DIM)
    scores = jnp.einsum(
        "qhd,khd->hqk", queries, keys_blk, preferred_element_type=jnp.float32
    ) * HEAD_DIM ** (-0.5)
    dprob = jnp.einsum("qhd,khd->hqk", head_grads, values_blk, preferred_element_type=jnp.float32)
    return (keys_blk, scores, dprob)


def update_stats(statistics, queries, head_grads, pair_rows):
    sub_size = math.gcd(pair_rows.shape[0], 512)

    def visit_block(block_index, running):
        run_max, run_total, run_mix = running
        pair_block = lax.dynamic_slice_in_dim(pair_rows, block_index * sub_size, sub_size, 0)
        keys_blk, scores, dprob = score_block(queries, head_grads, pair_block)
        new_max = jnp.maximum(run_max, jnp.max(scores, axis=-1))
        factor = jnp.exp(run_max - new_max)
        expo = jnp.exp(scores - new_max[..., None])
        return (
            new_max,
            run_total * factor + jnp.sum(expo, axis=-1),
            run_mix * factor + jnp.sum(expo * dprob, axis=-1),
        )

    return lax.fori_loop(0, pair_rows.shape[0] // sub_size, visit_block, statistics)


def block_backward(queries, head_grads, pair_block, log_total, row_delta):
    keys_blk, scores, dprob = score_block(queries, head_grads, pair_block)
    weights = jnp.exp(scores - log_total[..., None])
    prob_weights = weights.astype(jnp.bfloat16)
    dscore = (weights * (dprob - row_delta[..., None])).astype(jnp.bfloat16)
    return (keys_blk, prob_weights, dscore)


def key_terms_from(queries, head_grads, prob_weights, dscore):
    key_part = jnp.einsum(
        "hqk,qhd->khd", dscore, queries, preferred_element_type=jnp.float32
    ) * HEAD_DIM ** (-0.5)
    value_part = jnp.einsum(
        "hqk,qhd->khd", prob_weights, head_grads, preferred_element_type=jnp.float32
    )
    row_count = key_part.shape[0]
    return jnp.concatenate(
        [key_part.reshape(row_count, HD), value_part.reshape(row_count, HD)], axis=1
    )


def query_side(queries, head_grads, keys_values, local_rows):
    seq_rows = local_rows * lax.axis_size("seq")
    start_stats = (
        jnp.full((HEADS, local_rows), -1e30, jnp.float32),
        jnp.zeros((HEADS, local_rows), jnp.float32),
        jnp.zeros((HEADS, local_rows), jnp.float32),
    )
    all_pairs = lax.all_gather(keys_values, "seq", axis=0, tiled=True)
    statistics = update_stats(start_stats, queries, head_grads, all_pairs)
    row_max, row_total, row_mix = statistics
    log_total = row_max + jnp.log(row_total)
    row_delta = row_mix / row_total
    sub_size = math.gcd(seq_rows, 512)
    block_count = seq_rows // sub_size
    empty_query = jnp.zeros((local_rows, HEADS, HEAD_DIM), jnp.float32)

    def backward_step(block_index, running):
        query_grad, buffer = running
        pair_block = lax.dynamic_slice_in_dim(all_pairs, block_index * sub_size, sub_size, 0)
        keys_blk, prob_weights, dscore = block_backward(
            queries, head_grads, pair_block, log_total, row_delta
        )
        query_grad = query_grad + jnp.einsum(
            "hqk,khd->qhd", dscore, keys_blk, preferred_element_type=jnp.float32
        )
        block_terms = key_terms_from(queries, head_grads, prob_weights, dscore)
        buffer = lax.dynamic_update_slice_in_dim(buffer, block_terms, block_index * sub_size, 0)
        return (query_grad, buffer)

    empty_terms = jnp.zeros((seq_rows, 2 * HD), jnp.float32)
    query_grad, buffer = lax.fori_loop(0, block_count, backward_step, (empty_query, empty_terms))
    pair_grads = lax.psum_scatter(
        buffer.astype(jnp.bfloat16), "seq", scatter_dimension=0, tiled=True
    ).astype(jnp.float32)
    return (query_grad, pair_grads)


def local(
    tokens,
    upstream_grad,
    norm_gain,
    norm_bias,
    input_codes,
    input_scales,
    input_bias,
    output_codes,
    output_scales,
    layer_scale,
):
    all_codes, all_scales = (
        lax.all_gather(input_codes.astype(jnp.float32), "weight", axis=0, tiled=True).astype(
            input_codes.dtype
        ),
        lax.all_gather(input_scales, "weight", axis=0, tiled=True),
    )
    input_weight = dequantize(all_codes, all_scales)
    output_weight = dequantize(output_codes, output_scales)
    normed, inverse, norm_out = normalize(tokens[0].astype(jnp.float32), norm_gain, norm_bias)
    projected = (
        jnp.dot(norm_out, input_weight, preferred_element_type=jnp.float32) + input_bias
    ).astype(jnp.bfloat16)
    local_rows = projected.shape[0]
    queries = projected[:, :HD].reshape(local_rows, HEADS, HEAD_DIM)
    keys_values = projected[:, HD:]
    scaled_grad = (upstream_grad[0].astype(jnp.float32) * layer_scale).astype(jnp.bfloat16)
    head_grads = jnp.dot(scaled_grad, output_weight.T, preferred_element_type=jnp.float32).astype(
        jnp.bfloat16
    )
    head_grads = head_grads.reshape(local_rows, HEADS, HEAD_DIM)
    query_grad, pair_grads = query_side(queries, head_grads, keys_values, local_rows)
    query_grad = (query_grad * HEAD_DIM ** (-0.5)).reshape(local_rows, HD)
    grad_proj = jnp.concatenate([query_grad, pair_grads], axis=1).astype(jnp.bfloat16)
    grad_norm = jnp.dot(grad_proj, input_weight.T, preferred_element_type=jnp.float32)
    result = norm_backward(grad_norm, normed, inverse, norm_gain)
    return result[None]


def solution(mesh):
    in_specs = (
        P(("groups", "weight"), "seq", None),
        P(("groups", "weight"), "seq", None),
        P(),
        P(),
        P("weight", None),
        P("weight", None),
        P(),
        P(),
        P(),
        P(),
    )
    out_specs = P(("groups", "weight"), "seq", None)
    fits = mesh.shape["seq"] == 4 and mesh.shape["weight"] == 4
    plan = local_middle if fits else local
    return jax.shard_map(plan, mesh=mesh, in_specs=in_specs, out_specs=out_specs, check_vma=False)
```

```python
import functools
import math

import jax
import jax.numpy as jnp
from jax import lax
from jax.experimental import pallas as pl
from jax.experimental.pallas import tpu as pltpu
from jax.sharding import PartitionSpec as P

HEADS = 12
HEAD_DIM = 64
QBLOCK = 128
HD = 768
HALF = HD // 2
ROWS_OUT = 32
EPSILON = 1e-06
VMEM = pltpu.VMEM
SMEM = pltpu.SMEM


def half_index():
    return lax.axis_index("seq") * 2 // lax.axis_size("seq")


def cost(micros):
    return pl.CostEstimate(flops=int(micros * 1.0e9), bytes_accessed=int(micros * 3.0e6), transcendentals=0)


def spec(memory_space=VMEM):
    return pl.BlockSpec(memory_space=memory_space)


def norm_rows(rows):
    mean_value = jnp.mean(rows, axis=-1, keepdims=True)
    centered = rows - mean_value
    variance = jnp.mean(centered * centered, axis=-1, keepdims=True)
    inverse = lax.rsqrt(variance + EPSILON)
    return centered * inverse, inverse


def row_vector(ref):
    return ref[...].reshape(1, ref.shape[0])


def scale_block(codes, scale):
    return (codes.astype(jnp.float32) * scale).astype(jnp.bfloat16)


def first_kernel(
    tokens_ref, gain_ref, shift_ref, scales_ref, codes_ref, grad_ref, layer_ref, out_scales_ref, out_codes_ref,
    weight_out, near_out, far_out,
    tokens, gain, shift, scales, codes, grad, layer, out_scales, out_codes, scaled, weight, far, sems
):
    half = half_index()
    other = 1 - half
    blocks = HALF // QBLOCK

    def copy(source, target, at):
        started = pltpu.make_async_copy(source, target, sems.at[at])
        started.start()
        return started

    def columns(part):
        return codes_ref.at[:, pl.ds(pl.multiple_of(part * HD + half * HALF, QBLOCK), HALF)]

    def rows(which):
        return out_codes_ref.at[pl.ds(pl.multiple_of(which * HALF, QBLOCK), HALF), :]

    scales_copy = copy(scales_ref, scales, 0)
    codes_copies = [copy(columns(part), codes.at[part], 1 + part) for part in range(3)]
    tokens_copies = [
        copy(tokens_ref, tokens, 4), copy(gain_ref, gain, 5), copy(shift_ref, shift, 6)
    ]
    grad_copies = [
        copy(grad_ref, grad, 7), copy(layer_ref, layer, 8), copy(out_scales_ref, out_scales, 9)
    ]
    out_copies = [copy(rows(other), out_codes.at[0], 10), copy(rows(half), out_codes.at[1], 11)]

    scales_copy.wait()
    for part in range(3):
        codes_copies[part].wait()
        for r in range(codes_ref.shape[0] // QBLOCK):
            for c in range(blocks):
                scale = scales[r, (part * HD) // QBLOCK + half * blocks + c]
                lines = slice(r * QBLOCK, (r + 1) * QBLOCK)
                weight_out[lines, part * HALF + c * QBLOCK : part * HALF + (c + 1) * QBLOCK] = scale_block(
                    codes[part, lines, c * QBLOCK : (c + 1) * QBLOCK], scale
                )

    for started in tokens_copies:
        started.wait()
    width = tokens.shape[2]
    gain_row = row_vector(gain)
    shift_row = row_vector(shift)
    for r in range(0, tokens.shape[1], 16):
        normed, _ = norm_rows(tokens[0, r : r + 16, :].astype(jnp.float32))
        norm_out = (normed * gain_row + shift_row).astype(jnp.bfloat16)
        near_out[r : r + 16, :width] = norm_out
        far[r : r + 16, :width] = norm_out

    for started in grad_copies:
        started.wait()
    scaled[...] = (grad[0].astype(jnp.float32) * row_vector(layer)).astype(jnp.bfloat16)
    for i, (out_ref, which) in enumerate(((far, other), (near_out, half))):
        out_copies[i].wait()
        for r in range(blocks):
            lines = slice(r * QBLOCK, (r + 1) * QBLOCK)
            for c in range(width // QBLOCK):
                at = slice(c * QBLOCK, (c + 1) * QBLOCK)
                weight[lines, at] = scale_block(out_codes[i, lines, at], out_scales[which * blocks + r, c])
        out_ref[:, width:] = dot_last(scaled[...], weight[...]).astype(jnp.bfloat16)
        if out_ref is far:
            far_copy = copy(far, far_out, 12)
    far_copy.wait()


def first_step(tokens, gain, shift, scales, codes, grad, layer_scale, out_scales, out_codes):
    lines, width = tokens.shape[1:]
    depth = codes.shape[0]
    return pl.pallas_call(
        first_kernel,
        out_shape=(
            VMEM((depth, 3 * HALF), jnp.bfloat16),
            VMEM((lines, width + HALF), jnp.bfloat16),
            jax.ShapeDtypeStruct((lines, width + HALF), jnp.bfloat16),
        ),
        in_specs=[spec(pltpu.HBM)] * 9,
        out_specs=(spec(), spec(), spec(pltpu.HBM)),
        scratch_shapes=[
            VMEM(tokens.shape, tokens.dtype),
            VMEM(gain.shape, gain.dtype),
            VMEM(shift.shape, shift.dtype),
            SMEM(scales.shape, scales.dtype),
            VMEM((3, depth, HALF), codes.dtype),
            VMEM(grad.shape, grad.dtype),
            VMEM(layer_scale.shape, layer_scale.dtype),
            SMEM(out_scales.shape, out_scales.dtype),
            VMEM((2, HALF, width), out_codes.dtype),
            VMEM((lines, width), jnp.bfloat16),
            VMEM((HALF, width), jnp.bfloat16),
            VMEM((lines, width + HALF), jnp.bfloat16),
            pltpu.SemaphoreType.DMA((13,)),
        ],
        compiler_params=pltpu.CompilerParams(vmem_limit_bytes=60 * 2**20),
        cost_estimate=cost(3),
        name="first_weights_and_rows",
    )(tokens, gain, shift, scales, codes, grad, layer_scale, out_scales, out_codes)


def far_kernel(scales_ref, codes_ref, after_ref, weight_out, scales, codes, sems):
    other = 1 - half_index()
    blocks = HALF // QBLOCK
    copies = [pltpu.make_async_copy(scales_ref, scales, sems.at[3])]
    for part in range(3):
        at = pl.ds(pl.multiple_of(part * HD + other * HALF, QBLOCK), HALF)
        copies.append(pltpu.make_async_copy(codes_ref.at[:, at], codes.at[part], sems.at[part]))
    for started in copies:
        started.start()
    for started in copies:
        started.wait()
    for part in range(3):
        for r in range(codes_ref.shape[0] // QBLOCK):
            for c in range(blocks):
                scale = scales[r, (part * HD) // QBLOCK + other * blocks + c]
                lines = slice(r * QBLOCK, (r + 1) * QBLOCK)
                weight_out[lines, part * HALF + c * QBLOCK : part * HALF + (c + 1) * QBLOCK] = scale_block(
                    codes[part, lines, c * QBLOCK : (c + 1) * QBLOCK], scale
                )


def far_step(scales, codes, after):
    depth = codes.shape[0]
    return pl.pallas_call(
        far_kernel,
        out_shape=jax.ShapeDtypeStruct((depth, 3 * HALF), jnp.bfloat16),
        in_specs=[spec(pltpu.HBM), spec(pltpu.HBM), spec()],
        out_specs=spec(),
        scratch_shapes=[
            SMEM(scales.shape, scales.dtype),
            VMEM((3, depth, HALF), codes.dtype),
            pltpu.SemaphoreType.DMA((4,)),
        ],
        compiler_params=pltpu.CompilerParams(vmem_limit_bytes=16 * 2**20),
        cost_estimate=cost(0.01),
        name="far_weight",
    )(scales, codes, after)


def dot_last(a, b):
    return lax.dot_general(a, b, (((1,), (1,)), ((), ())), preferred_element_type=jnp.float32)


def dot_plain(a, b):
    return jnp.dot(a, b, preferred_element_type=jnp.float32)


def norm_columns(norms, picks, depth):
    mine = lax.axis_index("weight")
    return jnp.concatenate(
        [
            jnp.concatenate(
                [norm_ref[:, pl.ds(pl.multiple_of((mine ^ j) * depth, QBLOCK), depth)] for j in picks],
                axis=1,
            )
            for norm_ref in norms
        ],
        axis=0,
    )


def project_part(norms, weights, bias_ref, proj, first, part):
    half = half_index()
    rows = norm_columns(norms, range(4), weights[0].shape[0])
    bias = row_vector(bias_ref)
    at = slice(part * HALF, (part + 1) * HALF)
    shift = jnp.where(
        half == 0,
        bias[:, part * HD : part * HD + HALF],
        bias[:, part * HD + HALF : (part + 1) * HD],
    )
    columns = jnp.concatenate([w[:, at] for w in weights], axis=0)
    value = (dot_plain(rows, columns) + shift).astype(jnp.bfloat16)
    if part == 0:
        value = value * jnp.bfloat16(HEAD_DIM**-0.5)
    proj[first : first + rows.shape[0], at] = value


def project_kernel(*refs):
    for part in range(3):
        project_part(refs[0:2], refs[2:7], refs[7], refs[8], 0, part)


def project_step(norms, weights, bias):
    tokens = norms[0].shape[0]
    return pl.pallas_call(
        project_kernel,
        out_shape=jax.ShapeDtypeStruct((4 * tokens, 3 * HALF), jnp.bfloat16),
        in_specs=[spec()] * 8,
        out_specs=spec(),
        compiler_params=pltpu.CompilerParams(vmem_limit_bytes=24 * 2**20),
        cost_estimate=cost(0.01),
        name="projection",
    )(*norms, *weights, bias)


PAIR = 2 * HEAD_DIM


def soft_part(scores, dprob):
    expo = jnp.exp(scores - jnp.max(scores, axis=0, keepdims=True))
    scale = 1.0 / jnp.sum(expo, axis=0, keepdims=True)
    delta = jnp.sum(expo * dprob, axis=0, keepdims=True) * scale
    prob = (expo * scale).astype(jnp.bfloat16)
    return prob, prob * (dprob - delta).astype(jnp.bfloat16)


def attention_kernel(pairs, held, *refs):
    proj, grads, before, outs = refs[0], refs[1:5], refs[5:-4], refs[-4:]
    attention(pairs, held, proj, grads, before, outs)


def project_attention_kernel(pairs, *refs):
    norms, weights, bias_ref, proj_in, grads = refs[0:2], refs[2:7], refs[7], refs[8], refs[9:13]
    proj, outs = refs[-5], refs[-4:]
    tokens = norms[0].shape[0]
    proj[: 2 * tokens] = proj_in[: 2 * tokens]

    def project(part):
        project_part(norms, weights, bias_ref, proj, 2 * tokens, part)

    project(0)
    project(1)
    attention(pairs, 0, proj, grads, (), outs, lambda: project(2))


def attention(pairs, held, proj, grads, before, outs, between=None):
    total = proj.shape[0]
    tokens = grads[0].shape[0]
    low = lax.broadcasted_iota(jnp.int32, (total, PAIR), 1) < HEAD_DIM
    zero = jnp.zeros((total, PAIR), jnp.bfloat16)

    def load(t):
        query, key, value = (proj[:, part * HALF + t * PAIR : part * HALF + (t + 1) * PAIR] for part in range(3))
        grad = jnp.concatenate(
            [g[:, g.shape[1] - HALF + t * PAIR : g.shape[1] - HALF + (t + 1) * PAIR] for g in grads], axis=0
        )
        return query, key, value, grad

    def mask(side, value):
        return jnp.where(low, value, zero) if side == 0 else jnp.where(low, zero, value)

    def before_soft(t, side, between=None):
        query, key, value, grad = load(t)
        scores = dot_last(mask(side, key), query)
        if between is not None:
            between()
            value = load(t)[2]
        return scores, dot_last(mask(side, value), grad)

    def after_soft(t, side, prob, dscore):
        query, key, _, grad = load(t)
        key_t = key.T[side * HEAD_DIM : (side + 1) * HEAD_DIM]
        return (
            dot_plain(key_t, dscore),
            dot_plain(dscore, mask(side, query)),
            dot_plain(prob, mask(side, grad)),
        )

    def store(t, first, second):
        place = pairs.index(t)
        query_grad = jnp.concatenate([first[0], second[0]], axis=0).T * HEAD_DIM**-0.5
        for part, piece in enumerate((query_grad, first[1] + second[1], first[2] + second[2])):
            piece = piece.astype(jnp.bfloat16)
            for i, out in enumerate(outs):
                whole = out.shape[1] == 3 * HALF
                at = part * HALF + t * PAIR if whole else (part * len(pairs) + place) * PAIR
                out[:, at : at + PAIR] = piece[i * tokens : (i + 1) * tokens]

    heads = [(t, side) for t in pairs for side in range(2)]
    done = {}

    def finish(t, side, *soft):
        done[t, side] = after_soft(t, side, *soft)
        if side == 1:
            store(t, done[t, 0], done[t, 1])

    ready, behind = before_soft(*heads[0], between), None
    for i, head in enumerate(heads):
        now = ready
        if i + 1 < len(heads):
            ready = before_soft(*heads[i + 1])
        if behind is not None:
            finish(*behind)
        behind = (*head, *soft_part(*now))
    finish(*behind)
    for old, out in zip(before, outs[0:3:2]):
        for part in range(3):
            out[:, part * HALF : part * HALF + held] = old[:, part * held : (part + 1) * held]


def project_attention_step(norms, weights, bias, proj, grads, pairs, after):
    tokens = grads[0].shape[0]
    out = jax.ShapeDtypeStruct((tokens, 3 * len(pairs) * PAIR), jnp.bfloat16)
    return pl.pallas_call(
        functools.partial(project_attention_kernel, pairs),
        out_shape=(jax.ShapeDtypeStruct(proj.shape, proj.dtype),) + (out,) * 4,
        in_specs=[spec()] * 14,
        out_specs=(spec(),) * 5,
        input_output_aliases={8: 0},
        compiler_params=pltpu.CompilerParams(vmem_limit_bytes=24 * 2**20),
        cost_estimate=cost(12),
        name="projection_attention",
    )(*norms, *weights, bias, proj, *grads, after)


def attention_step(proj, grads, pairs, before):
    tokens = grads[0].shape[0]
    widths = [3 * len(pairs) * PAIR] * 4
    for i in range(len(before)):
        widths[2 * i] = 3 * HALF
    held = before[0].shape[1] // 3 if before else 0
    return pl.pallas_call(
        functools.partial(attention_kernel, pairs, held),
        out_shape=tuple(jax.ShapeDtypeStruct((tokens, width), jnp.bfloat16) for width in widths),
        in_specs=[spec()] * (5 + len(before)),
        out_specs=(spec(),) * 4,
        compiler_params=pltpu.CompilerParams(vmem_limit_bytes=24 * 2**20),
        cost_estimate=cost(12),
        name="attention",
    )(proj, *grads, *before)


def near_shard(refs, j, pairs=None):
    def columns(ref):
        if pairs is None:
            return ref[...]
        first, last = pairs[0] * PAIR, (pairs[-1] + 1) * PAIR
        return jnp.concatenate([ref[:, part * HALF + first : part * HALF + last] for part in range(3)], axis=1)

    return columns(refs[j]) if j < 3 else jnp.concatenate([columns(ref) for ref in refs[3:5]], axis=0)


def join_skip(first, second):
    wide, narrow = first.shape[1] // 3, second.shape[1] // 3
    pieces = []
    for part in range(3):
        pieces += [first[:, part * wide : (part + 1) * wide], second[:, part * narrow : (part + 1) * narrow]]
    return jnp.concatenate(pieces, axis=1)


def on_middle():
    place = lax.axis_index("seq")
    return (place == 1) | (place == 2)


def early_kernel(*refs):
    near_w, far_w = refs[0:5], {0: refs[5], 2: refs[6]}
    own_ref, skip_first, skip_second, tokens_ref, sums, normed_out, inverse_out = refs[7:]
    middle = on_middle()
    mine = lax.axis_index("weight")
    depth = far_w[0].shape[0]

    def fill(value, weights, far):
        for j in range(4):
            at = pl.ds(pl.multiple_of((mine ^ j) * depth, QBLOCK), depth)
            if not far or j in weights:
                sums[:, at] = dot_last(value, weights[j][...] if far else near_shard(weights, j))
            else:
                sums[:, at] = jnp.zeros((value.shape[0], depth), jnp.float32)

    pl.when(middle)(lambda: fill(own_ref[...], near_w, False))
    pl.when(jnp.logical_not(middle))(lambda: fill(join_skip(skip_first, skip_second), far_w, True))
    for r in range(0, tokens_ref.shape[1], 16):
        normed, inverse = norm_rows(tokens_ref[0, r : r + 16, :].astype(jnp.float32))
        normed_out[r : r + 16, :] = normed
        inverse_out[r : r + 16, :] = jnp.broadcast_to(inverse, (16, QBLOCK))


def early_step(near_w, far_w, own, skips, tokens):
    rows, width = tokens.shape[1:]
    full = jax.ShapeDtypeStruct((rows, width), jnp.float32)
    return pl.pallas_call(
        early_kernel,
        out_shape=(full, full, jax.ShapeDtypeStruct((rows, QBLOCK), jnp.float32)),
        in_specs=[spec()] * 11,
        out_specs=(spec(),) * 3,
        compiler_params=pltpu.CompilerParams(vmem_limit_bytes=24 * 2**20),
        cost_estimate=cost(0.01),
        name="grad_norm_part",
    )(*near_w, *far_w, own, *skips, tokens)


def back_part_kernel(*refs):
    near_w, back_first, sums, out_ref = refs[0:5], refs[5], refs[6], refs[7]
    depth = near_w[0].shape[0]
    mine = lax.axis_index("weight")
    out_ref[...] = sums[...]

    @pl.when(jnp.logical_not(on_middle()))
    def _():
        back = back_first[...]
        for j in range(4):
            at = pl.ds(pl.multiple_of((mine ^ j) * depth, QBLOCK), depth)
            out_ref[:, at] = sums[:, at] + dot_last(back, near_shard(near_w, j, EARLY))


def back_part_step(near_w, back_first, sums):
    return pl.pallas_call(
        back_part_kernel,
        out_shape=jax.ShapeDtypeStruct(sums.shape, sums.dtype),
        in_specs=[spec()] * 7,
        out_specs=spec(),
        compiler_params=pltpu.CompilerParams(vmem_limit_bytes=24 * 2**20),
        cost_estimate=cost(50),
        name="back_part",
    )(*near_w, back_first, sums)


def pair_part_kernel(pair, skip_first, skip_second, sums, out_ref):
    mine = lax.axis_index("weight")
    depth = pair.shape[0] // 2
    out_ref[...] = sums[...]

    @pl.when(jnp.logical_not(on_middle()))
    def _():
        skip = join_skip(skip_first, skip_second)
        for i, j in enumerate((1, 3)):
            at = pl.ds(pl.multiple_of((mine ^ j) * depth, QBLOCK), depth)
            out_ref[:, at] = sums[:, at] + dot_last(skip, pair[i * depth : (i + 1) * depth])


def pair_part_step(pair, skips, sums):
    return pl.pallas_call(
        pair_part_kernel,
        out_shape=jax.ShapeDtypeStruct(sums.shape, sums.dtype),
        in_specs=[spec()] * 4,
        out_specs=spec(),
        compiler_params=pltpu.CompilerParams(vmem_limit_bytes=24 * 2**20),
        cost_estimate=cost(0.01),
        name="pair_part",
    )(pair, *skips, sums)


def last_kernel(*refs):
    near_w, pair = refs[0:5], refs[7]
    sums, cross_ref, back_ref, normed_ref, inverse_ref, gain_ref, out_ref = refs[8:15]
    gain, grad_hat, first_sum, second_sum, result, sems = refs[15:]
    middle = on_middle()
    mine = lax.axis_index("weight")
    depth = refs[5].shape[0]
    far_w = (refs[5], pair.at[:depth], refs[6], pair.at[depth:])
    gain[...] = row_vector(gain_ref)

    def fill(value_ref, weight_of):
        value = value_ref[...]
        first = second = jnp.zeros(first_sum.shape, jnp.float32)
        for j in range(4):
            at = pl.ds(pl.multiple_of((mine ^ j) * depth, QBLOCK), depth)
            hat = (sums[:, at] + dot_last(value, weight_of(j))) * gain[:, at]
            grad_hat[:, at] = hat
            mixed = hat * normed_ref[:, at]
            for c in range(0, depth, QBLOCK):
                first += hat[:, c : c + QBLOCK]
                second += mixed[:, c : c + QBLOCK]
        first_sum[...] = first
        second_sum[...] = second

    pl.when(middle)(lambda: fill(cross_ref, lambda j: far_w[j][...]))
    pl.when(jnp.logical_not(middle))(lambda: fill(back_ref, lambda j: near_shard(near_w, j, LATE)))
    rows, width = normed_ref.shape
    copies = []
    for i, first in enumerate(range(0, rows, ROWS_OUT)):
        for r in range(first, first + ROWS_OUT, 8):
            at = slice(r, r + 8)
            first_mean = jnp.sum(first_sum[at, :], axis=-1, keepdims=True) * (1.0 / width)
            second_mean = jnp.sum(second_sum[at, :], axis=-1, keepdims=True) * (1.0 / width)
            result[at, :] = inverse_ref[at, :1] * (
                grad_hat[at, :] - first_mean - normed_ref[at, :] * second_mean
            )
        lines = pl.ds(first, ROWS_OUT)
        copies.append(pltpu.make_async_copy(result.at[lines, :], out_ref.at[0, lines, :], sems.at[i]))
        copies[-1].start()
    for copy in copies:
        copy.wait()


def last_step(near_w, far_w, back, cross, sums, normed, inverse, gain):
    return pl.pallas_call(
        last_kernel,
        out_shape=jax.ShapeDtypeStruct((1, *normed.shape), jnp.float32),
        in_specs=[spec()] * 14,
        out_specs=spec(pltpu.HBM),
        scratch_shapes=[
            VMEM((1, normed.shape[1]), jnp.float32),
            VMEM(normed.shape, jnp.float32),
            VMEM((normed.shape[0], QBLOCK), jnp.float32),
            VMEM((normed.shape[0], QBLOCK), jnp.float32),
            VMEM(normed.shape, jnp.float32),
            pltpu.SemaphoreType.DMA((normed.shape[0] // ROWS_OUT,)),
        ],
        compiler_params=pltpu.CompilerParams(vmem_limit_bytes=24 * 2**20),
        cost_estimate=cost(2),
        name="input_grad",
    )(*near_w, *far_w, sums, cross, back, normed, inverse, gain)


def split_kernel(value_ref, upper_ref, lower_ref):
    middle = upper_ref.shape[0]
    upper_ref[...] = value_ref[:middle]
    lower_ref[...] = value_ref[middle:]


def split_step(value):
    half = jax.ShapeDtypeStruct((value.shape[0] // 2, value.shape[1]), value.dtype)
    return pl.pallas_call(
        split_kernel,
        out_shape=(half, half),
        in_specs=[spec()],
        out_specs=(spec(), spec()),
        compiler_params=pltpu.CompilerParams(vmem_limit_bytes=16 * 2**20),
        cost_estimate=cost(0.01),
        name="split_rows",
    )(value)


def pair_kernel(first_ref, second_ref, *refs):
    out_ref = refs[-1]
    middle = first_ref.shape[0]
    out_ref[:middle] = first_ref[...]
    out_ref[middle:] = second_ref[...]


def pair_step(first, second, *after):
    return pl.pallas_call(
        pair_kernel,
        out_shape=jax.ShapeDtypeStruct((2 * first.shape[0], first.shape[1]), first.dtype),
        in_specs=[spec()] * (2 + len(after)),
        out_specs=spec(),
        compiler_params=pltpu.CompilerParams(vmem_limit_bytes=16 * 2**20),
        cost_estimate=cost(0.01),
        name="chip_weight",
    )(first, second, *after)


EARLY = (0, 1)
LATE = (2,)
END_TO_MIDDLE = [(0, 1), (3, 2)]
MIDDLE = [(1, 2), (2, 1)]
END_TO_FAR = [(0, 2), (3, 1)]
MIDDLE_TO_END = [(1, 0), (2, 3)]
FAR_TO_END = [(1, 3), (2, 0)]


def flip(bit):
    return [(i, i ^ bit) for i in range(4)]


def local_middle(
    tokens,
    upstream_grad,
    norm_gain,
    norm_bias,
    input_codes,
    input_scales,
    input_bias,
    output_codes,
    output_scales,
    layer_scale,
):
    near, both_near, both_other = first_step(
        tokens, norm_gain, norm_bias, input_scales, input_codes, upstream_grad, layer_scale, output_scales, output_codes
    )
    both_mid = lax.ppermute(both_other, "seq", MIDDLE)
    both_far = lax.ppermute(both_other, "seq", END_TO_FAR)
    both_end = lax.ppermute(both_near, "seq", END_TO_MIDDLE)
    near_across = lax.ppermute(near, "weight", flip(2))
    near_beside = lax.ppermute(near, "weight", flip(1))
    near_diagonal = [lax.ppermute(w, "weight", flip(1)) for w in split_step(near_across)]
    far = far_step(input_scales, input_codes, near_across)
    far_across = lax.ppermute(far, "weight", flip(2))
    rows = (both_near, both_end, both_mid, both_far)
    near_w = (near, near_beside, near_across, *near_diagonal)
    proj = project_step(rows[:2], near_w, input_bias)
    grads = (both_near, both_end, both_mid, both_far)
    proj, own, end, mid, skip_first = project_attention_step(
        rows[2:], near_w, input_bias, proj, grads, EARLY, far
    )
    back_first = lax.ppermute(end, "seq", MIDDLE_TO_END)
    skip_first = lax.ppermute(skip_first, "seq", FAR_TO_END)
    own, end, mid, skip_second = attention_step(proj, grads, LATE, (own, mid))
    skip_second = lax.ppermute(skip_second, "seq", FAR_TO_END)
    cross = lax.ppermute(mid, "seq", MIDDLE)
    back = lax.ppermute(end, "seq", MIDDLE_TO_END)
    far_pair = lax.ppermute(pair_step(far, far_across, skip_first, own), "weight", flip(1))
    far_w = (far, far_across)
    skips = (skip_first, skip_second)
    sums, normed, inverse = early_step(near_w, far_w, own, skips, tokens)
    sums = back_part_step(near_w, back_first, sums)
    sums = pair_part_step(far_pair, skips, sums)
    return last_step(near_w, (*far_w, far_pair), back, cross, sums, normed, inverse, norm_gain)


def dequantize(codes, scales):
    expanded = jnp.repeat(jnp.repeat(scales, QBLOCK, axis=0), QBLOCK, axis=1)
    return (codes.astype(jnp.float32) * expanded).astype(jnp.bfloat16)


def normalize(rows, gain, shift):
    mean_value = jnp.mean(rows, axis=-1, keepdims=True)
    centered = rows - mean_value
    variance = jnp.mean(centered * centered, axis=-1, keepdims=True)
    inverse = lax.rsqrt(variance + 1e-06)
    normed = centered * inverse
    return (normed, inverse, (normed * gain + shift).astype(jnp.bfloat16))


def norm_backward(grad_norm, normed, inverse, gain):
    grad_hat = grad_norm * gain
    first_mean = jnp.mean(grad_hat, axis=-1, keepdims=True)
    second_mean = jnp.mean(grad_hat * normed, axis=-1, keepdims=True)
    return inverse * (grad_hat - first_mean - normed * second_mean)


def score_block(queries, head_grads, pair_block):
    row_count = pair_block.shape[0]
    keys_blk = pair_block[:, :HD].reshape(row_count, HEADS, HEAD_DIM)
    values_blk = pair_block[:, HD:].reshape(row_count, HEADS, HEAD_DIM)
    scores = jnp.einsum(
        "qhd,khd->hqk", queries, keys_blk, preferred_element_type=jnp.float32
    ) * HEAD_DIM ** (-0.5)
    dprob = jnp.einsum("qhd,khd->hqk", head_grads, values_blk, preferred_element_type=jnp.float32)
    return (keys_blk, scores, dprob)


def update_stats(statistics, queries, head_grads, pair_rows):
    sub_size = math.gcd(pair_rows.shape[0], 512)

    def visit_block(block_index, running):
        run_max, run_total, run_mix = running
        pair_block = lax.dynamic_slice_in_dim(pair_rows, block_index * sub_size, sub_size, 0)
        keys_blk, scores, dprob = score_block(queries, head_grads, pair_block)
        new_max = jnp.maximum(run_max, jnp.max(scores, axis=-1))
        factor = jnp.exp(run_max - new_max)
        expo = jnp.exp(scores - new_max[..., None])
        return (
            new_max,
            run_total * factor + jnp.sum(expo, axis=-1),
            run_mix * factor + jnp.sum(expo * dprob, axis=-1),
        )

    return lax.fori_loop(0, pair_rows.shape[0] // sub_size, visit_block, statistics)


def block_backward(queries, head_grads, pair_block, log_total, row_delta):
    keys_blk, scores, dprob = score_block(queries, head_grads, pair_block)
    weights = jnp.exp(scores - log_total[..., None])
    prob_weights = weights.astype(jnp.bfloat16)
    dscore = (weights * (dprob - row_delta[..., None])).astype(jnp.bfloat16)
    return (keys_blk, prob_weights, dscore)


def key_terms_from(queries, head_grads, prob_weights, dscore):
    key_part = jnp.einsum(
        "hqk,qhd->khd", dscore, queries, preferred_element_type=jnp.float32
    ) * HEAD_DIM ** (-0.5)
    value_part = jnp.einsum(
        "hqk,qhd->khd", prob_weights, head_grads, preferred_element_type=jnp.float32
    )
    row_count = key_part.shape[0]
    return jnp.concatenate(
        [key_part.reshape(row_count, HD), value_part.reshape(row_count, HD)], axis=1
    )


def query_side(queries, head_grads, keys_values, local_rows):
    seq_rows = local_rows * lax.axis_size("seq")
    start_stats = (
        jnp.full((HEADS, local_rows), -1e30, jnp.float32),
        jnp.zeros((HEADS, local_rows), jnp.float32),
        jnp.zeros((HEADS, local_rows), jnp.float32),
    )
    all_pairs = lax.all_gather(keys_values, "seq", axis=0, tiled=True)
    statistics = update_stats(start_stats, queries, head_grads, all_pairs)
    row_max, row_total, row_mix = statistics
    log_total = row_max + jnp.log(row_total)
    row_delta = row_mix / row_total
    sub_size = math.gcd(seq_rows, 512)
    block_count = seq_rows // sub_size
    empty_query = jnp.zeros((local_rows, HEADS, HEAD_DIM), jnp.float32)

    def backward_step(block_index, running):
        query_grad, buffer = running
        pair_block = lax.dynamic_slice_in_dim(all_pairs, block_index * sub_size, sub_size, 0)
        keys_blk, prob_weights, dscore = block_backward(
            queries, head_grads, pair_block, log_total, row_delta
        )
        query_grad = query_grad + jnp.einsum(
            "hqk,khd->qhd", dscore, keys_blk, preferred_element_type=jnp.float32
        )
        block_terms = key_terms_from(queries, head_grads, prob_weights, dscore)
        buffer = lax.dynamic_update_slice_in_dim(buffer, block_terms, block_index * sub_size, 0)
        return (query_grad, buffer)

    empty_terms = jnp.zeros((seq_rows, 2 * HD), jnp.float32)
    query_grad, buffer = lax.fori_loop(0, block_count, backward_step, (empty_query, empty_terms))
    pair_grads = lax.psum_scatter(
        buffer.astype(jnp.bfloat16), "seq", scatter_dimension=0, tiled=True
    ).astype(jnp.float32)
    return (query_grad, pair_grads)


def local(
    tokens,
    upstream_grad,
    norm_gain,
    norm_bias,
    input_codes,
    input_scales,
    input_bias,
    output_codes,
    output_scales,
    layer_scale,
):
    all_codes, all_scales = (
        lax.all_gather(input_codes.astype(jnp.float32), "weight", axis=0, tiled=True).astype(
            input_codes.dtype
        ),
        lax.all_gather(input_scales, "weight", axis=0, tiled=True),
    )
    input_weight = dequantize(all_codes, all_scales)
    output_weight = dequantize(output_codes, output_scales)
    normed, inverse, norm_out = normalize(tokens[0].astype(jnp.float32), norm_gain, norm_bias)
    projected = (
        jnp.dot(norm_out, input_weight, preferred_element_type=jnp.float32) + input_bias
    ).astype(jnp.bfloat16)
    local_rows = projected.shape[0]
    queries = projected[:, :HD].reshape(local_rows, HEADS, HEAD_DIM)
    keys_values = projected[:, HD:]
    scaled_grad = (upstream_grad[0].astype(jnp.float32) * layer_scale).astype(jnp.bfloat16)
    head_grads = jnp.dot(scaled_grad, output_weight.T, preferred_element_type=jnp.float32).astype(
        jnp.bfloat16
    )
    head_grads = head_grads.reshape(local_rows, HEADS, HEAD_DIM)
    query_grad, pair_grads = query_side(queries, head_grads, keys_values, local_rows)
    query_grad = (query_grad * HEAD_DIM ** (-0.5)).reshape(local_rows, HD)
    grad_proj = jnp.concatenate([query_grad, pair_grads], axis=1).astype(jnp.bfloat16)
    grad_norm = jnp.dot(grad_proj, input_weight.T, preferred_element_type=jnp.float32)
    result = norm_backward(grad_norm, normed, inverse, norm_gain)
    return result[None]


def solution(mesh):
    in_specs = (
        P(("groups", "weight"), "seq", None),
        P(("groups", "weight"), "seq", None),
        P(),
        P(),
        P("weight", None),
        P("weight", None),
        P(),
        P(),
        P(),
        P(),
    )
    out_specs = P(("groups", "weight"), "seq", None)
    fits = mesh.shape["seq"] == 4 and mesh.shape["weight"] == 4
    plan = local_middle if fits else local
    return jax.shard_map(plan, mesh=mesh, in_specs=in_specs, out_specs=out_specs, check_vma=False)
```

```python
import functools
import math

import jax
import jax.numpy as jnp
from jax import lax
from jax.experimental import pallas as pl
from jax.experimental.pallas import tpu as pltpu
from jax.sharding import PartitionSpec as P

HEADS = 12
HEAD_DIM = 64
QBLOCK = 128
HD = 768
HALF = HD // 2
ROWS_OUT = 32
EPSILON = 1e-06
VMEM = pltpu.VMEM
SMEM = pltpu.SMEM


def half_index():
    return lax.axis_index("seq") * 2 // lax.axis_size("seq")


def cost(micros):
    return pl.CostEstimate(flops=int(micros * 1.0e9), bytes_accessed=int(micros * 3.0e6), transcendentals=0)


def spec(memory_space=VMEM):
    return pl.BlockSpec(memory_space=memory_space)


def norm_rows(rows):
    mean_value = jnp.mean(rows, axis=-1, keepdims=True)
    centered = rows - mean_value
    variance = jnp.mean(centered * centered, axis=-1, keepdims=True)
    inverse = lax.rsqrt(variance + EPSILON)
    return centered * inverse, inverse


def row_vector(ref):
    return ref[...].reshape(1, ref.shape[0])


def scale_block(codes, scale):
    return (codes.astype(jnp.float32) * scale).astype(jnp.bfloat16)


def first_kernel(
    tokens_ref, gain_ref, shift_ref, scales_ref, codes_ref, grad_ref, layer_ref, out_scales_ref, out_codes_ref,
    weight_out, near_out, far_out,
    tokens, gain, shift, scales, codes, grad, layer, out_scales, out_codes, scaled, weight, far, sems
):
    half = half_index()
    other = 1 - half
    blocks = HALF // QBLOCK

    def copy(source, target, at):
        started = pltpu.make_async_copy(source, target, sems.at[at])
        started.start()
        return started

    def columns(part):
        return codes_ref.at[:, pl.ds(pl.multiple_of(part * HD + half * HALF, QBLOCK), HALF)]

    def rows(which):
        return out_codes_ref.at[pl.ds(pl.multiple_of(which * HALF, QBLOCK), HALF), :]

    tokens_copies = [
        copy(tokens_ref, tokens, 4), copy(gain_ref, gain, 5), copy(shift_ref, shift, 6)
    ]
    scales_copy = copy(scales_ref, scales, 0)
    codes_copies = [copy(columns(part), codes.at[part], 1 + part) for part in range(3)]
    grad_copies = [
        copy(grad_ref, grad, 7), copy(layer_ref, layer, 8), copy(out_scales_ref, out_scales, 9)
    ]
    out_copies = [copy(rows(other), out_codes.at[0], 10), copy(rows(half), out_codes.at[1], 11)]

    for started in tokens_copies:
        started.wait()
    width = tokens.shape[2]
    gain_row = row_vector(gain)
    shift_row = row_vector(shift)
    for r in range(0, tokens.shape[1], 16):
        normed, _ = norm_rows(tokens[0, r : r + 16, :].astype(jnp.float32))
        norm_out = (normed * gain_row + shift_row).astype(jnp.bfloat16)
        near_out[r : r + 16, :width] = norm_out
        far[r : r + 16, :width] = norm_out

    scales_copy.wait()
    for part in range(3):
        codes_copies[part].wait()
        for r in range(codes_ref.shape[0] // QBLOCK):
            for c in range(blocks):
                scale = scales[r, (part * HD) // QBLOCK + half * blocks + c]
                lines = slice(r * QBLOCK, (r + 1) * QBLOCK)
                weight_out[lines, part * HALF + c * QBLOCK : part * HALF + (c + 1) * QBLOCK] = scale_block(
                    codes[part, lines, c * QBLOCK : (c + 1) * QBLOCK], scale
                )

    for started in grad_copies:
        started.wait()
    scaled[...] = (grad[0].astype(jnp.float32) * row_vector(layer)).astype(jnp.bfloat16)
    for i, (out_ref, which) in enumerate(((far, other), (near_out, half))):
        out_copies[i].wait()
        for r in range(blocks):
            lines = slice(r * QBLOCK, (r + 1) * QBLOCK)
            for c in range(width // QBLOCK):
                at = slice(c * QBLOCK, (c + 1) * QBLOCK)
                weight[lines, at] = scale_block(out_codes[i, lines, at], out_scales[which * blocks + r, c])
        out_ref[:, width:] = dot_last(scaled[...], weight[...]).astype(jnp.bfloat16)
        if out_ref is far:
            far_copy = copy(far, far_out, 12)
    far_copy.wait()


def first_step(tokens, gain, shift, scales, codes, grad, layer_scale, out_scales, out_codes):
    lines, width = tokens.shape[1:]
    depth = codes.shape[0]
    return pl.pallas_call(
        first_kernel,
        out_shape=(
            VMEM((depth, 3 * HALF), jnp.bfloat16),
            VMEM((lines, width + HALF), jnp.bfloat16),
            jax.ShapeDtypeStruct((lines, width + HALF), jnp.bfloat16),
        ),
        in_specs=[spec(pltpu.HBM)] * 9,
        out_specs=(spec(), spec(), spec(pltpu.HBM)),
        scratch_shapes=[
            VMEM(tokens.shape, tokens.dtype),
            VMEM(gain.shape, gain.dtype),
            VMEM(shift.shape, shift.dtype),
            SMEM(scales.shape, scales.dtype),
            VMEM((3, depth, HALF), codes.dtype),
            VMEM(grad.shape, grad.dtype),
            VMEM(layer_scale.shape, layer_scale.dtype),
            SMEM(out_scales.shape, out_scales.dtype),
            VMEM((2, HALF, width), out_codes.dtype),
            VMEM((lines, width), jnp.bfloat16),
            VMEM((HALF, width), jnp.bfloat16),
            VMEM((lines, width + HALF), jnp.bfloat16),
            pltpu.SemaphoreType.DMA((13,)),
        ],
        compiler_params=pltpu.CompilerParams(vmem_limit_bytes=60 * 2**20),
        cost_estimate=cost(3),
        name="first_weights_and_rows",
    )(tokens, gain, shift, scales, codes, grad, layer_scale, out_scales, out_codes)


def far_kernel(scales_ref, codes_ref, after_ref, weight_out, scales, codes, sems):
    other = 1 - half_index()
    blocks = HALF // QBLOCK
    copies = [pltpu.make_async_copy(scales_ref, scales, sems.at[3])]
    for part in range(3):
        at = pl.ds(pl.multiple_of(part * HD + other * HALF, QBLOCK), HALF)
        copies.append(pltpu.make_async_copy(codes_ref.at[:, at], codes.at[part], sems.at[part]))
    for started in copies:
        started.start()
    for started in copies:
        started.wait()
    for part in range(3):
        for r in range(codes_ref.shape[0] // QBLOCK):
            for c in range(blocks):
                scale = scales[r, (part * HD) // QBLOCK + other * blocks + c]
                lines = slice(r * QBLOCK, (r + 1) * QBLOCK)
                weight_out[lines, part * HALF + c * QBLOCK : part * HALF + (c + 1) * QBLOCK] = scale_block(
                    codes[part, lines, c * QBLOCK : (c + 1) * QBLOCK], scale
                )


def far_step(scales, codes, after):
    depth = codes.shape[0]
    return pl.pallas_call(
        far_kernel,
        out_shape=jax.ShapeDtypeStruct((depth, 3 * HALF), jnp.bfloat16),
        in_specs=[spec(pltpu.HBM), spec(pltpu.HBM), spec()],
        out_specs=spec(),
        scratch_shapes=[
            SMEM(scales.shape, scales.dtype),
            VMEM((3, depth, HALF), codes.dtype),
            pltpu.SemaphoreType.DMA((4,)),
        ],
        compiler_params=pltpu.CompilerParams(vmem_limit_bytes=16 * 2**20),
        cost_estimate=cost(0.01),
        name="far_weight",
    )(scales, codes, after)


def dot_last(a, b):
    return lax.dot_general(a, b, (((1,), (1,)), ((), ())), preferred_element_type=jnp.float32)


def dot_plain(a, b):
    return jnp.dot(a, b, preferred_element_type=jnp.float32)


def norm_columns(norms, picks, depth):
    mine = lax.axis_index("weight")
    return jnp.concatenate(
        [
            jnp.concatenate(
                [norm_ref[:, pl.ds(pl.multiple_of((mine ^ j) * depth, QBLOCK), depth)] for j in picks],
                axis=1,
            )
            for norm_ref in norms
        ],
        axis=0,
    )


def project_part(norms, weights, bias_ref, proj, first, part):
    half = half_index()
    rows = norm_columns(norms, range(4), weights[0].shape[0])
    bias = row_vector(bias_ref)
    at = slice(part * HALF, (part + 1) * HALF)
    shift = jnp.where(
        half == 0,
        bias[:, part * HD : part * HD + HALF],
        bias[:, part * HD + HALF : (part + 1) * HD],
    )
    columns = jnp.concatenate([w[:, at] for w in weights], axis=0)
    value = (dot_plain(rows, columns) + shift).astype(jnp.bfloat16)
    if part == 0:
        value = value * jnp.bfloat16(HEAD_DIM**-0.5)
    proj[first : first + rows.shape[0], at] = value


def project_kernel(*refs):
    for part in range(3):
        project_part(refs[0:2], refs[2:7], refs[7], refs[8], 0, part)


def project_step(norms, weights, bias):
    tokens = norms[0].shape[0]
    return pl.pallas_call(
        project_kernel,
        out_shape=jax.ShapeDtypeStruct((2 * tokens, 3 * HALF), jnp.bfloat16),
        in_specs=[spec()] * 8,
        out_specs=spec(),
        compiler_params=pltpu.CompilerParams(vmem_limit_bytes=24 * 2**20),
        cost_estimate=cost(0.01),
        name="projection",
    )(*norms, *weights, bias)


PAIR = 2 * HEAD_DIM


def soft_part(scores, dprob):
    expo = jnp.exp(scores - jnp.max(scores, axis=0, keepdims=True))
    scale = 1.0 / jnp.sum(expo, axis=0, keepdims=True)
    delta = jnp.sum(expo * dprob, axis=0, keepdims=True) * scale
    prob = (expo * scale).astype(jnp.bfloat16)
    return prob, prob * (dprob - delta).astype(jnp.bfloat16)


def attention_kernel(pairs, held, *refs):
    proj, grads, before, outs = refs[0:2], refs[2:6], refs[6:-4], refs[-4:]
    attention(pairs, held, proj, grads, before, outs)


def project_attention_kernel(pairs, *refs):
    norms, weights, bias_ref, proj_in, grads = refs[0:2], refs[2:7], refs[7], refs[8], refs[9:13]
    proj, outs = refs[-5], refs[-4:]

    def project(part):
        project_part(norms, weights, bias_ref, proj, 0, part)

    project(0)
    project(1)
    attention(pairs, 0, (proj_in, proj), grads, (), outs, lambda: project(2))


def attention(pairs, held, proj, grads, before, outs, between=None):
    total = sum(ref.shape[0] for ref in proj)
    tokens = grads[0].shape[0]
    low = lax.broadcasted_iota(jnp.int32, (total, PAIR), 1) < HEAD_DIM
    zero = jnp.zeros((total, PAIR), jnp.bfloat16)

    def load(t):
        query, key, value = (
            jnp.concatenate([p[:, part * HALF + t * PAIR : part * HALF + (t + 1) * PAIR] for p in proj], axis=0)
            for part in range(3)
        )
        grad = jnp.concatenate(
            [g[:, g.shape[1] - HALF + t * PAIR : g.shape[1] - HALF + (t + 1) * PAIR] for g in grads], axis=0
        )
        return query, key, value, grad

    def mask(side, value):
        return jnp.where(low, value, zero) if side == 0 else jnp.where(low, zero, value)

    def before_soft(t, side, between=None):
        query, key, value, grad = load(t)
        scores = dot_last(mask(side, key), query)
        if between is not None:
            between()
            value = load(t)[2]
        return scores, dot_last(mask(side, value), grad)

    def after_soft(t, side, prob, dscore):
        query, key, _, grad = load(t)
        key_t = key.T[side * HEAD_DIM : (side + 1) * HEAD_DIM]
        return (
            dot_plain(key_t, dscore),
            dot_plain(dscore, mask(side, query)),
            dot_plain(prob, mask(side, grad)),
        )

    def store(t, first, second):
        place = pairs.index(t)
        query_grad = jnp.concatenate([first[0], second[0]], axis=0).T * HEAD_DIM**-0.5
        for part, piece in enumerate((query_grad, first[1] + second[1], first[2] + second[2])):
            piece = piece.astype(jnp.bfloat16)
            for i, out in enumerate(outs):
                whole = out.shape[1] == 3 * HALF
                at = part * HALF + t * PAIR if whole else (part * len(pairs) + place) * PAIR
                out[:, at : at + PAIR] = piece[i * tokens : (i + 1) * tokens]

    heads = [(t, side) for t in pairs for side in range(2)]
    done = {}

    def finish(t, side, *soft):
        done[t, side] = after_soft(t, side, *soft)
        if side == 1:
            store(t, done[t, 0], done[t, 1])

    ready, behind = before_soft(*heads[0], between), None
    for i, head in enumerate(heads):
        now = ready
        if i + 1 < len(heads):
            ready = before_soft(*heads[i + 1])
        if behind is not None:
            finish(*behind)
        behind = (*head, *soft_part(*now))
    finish(*behind)
    for old, out in zip(before, outs[0:3:2]):
        for part in range(3):
            out[:, part * HALF : part * HALF + held] = old[:, part * held : (part + 1) * held]


def project_attention_step(norms, weights, bias, proj, grads, pairs, after):
    tokens = grads[0].shape[0]
    out = jax.ShapeDtypeStruct((tokens, 3 * len(pairs) * PAIR), jnp.bfloat16)
    return pl.pallas_call(
        functools.partial(project_attention_kernel, pairs),
        out_shape=(jax.ShapeDtypeStruct(proj.shape, proj.dtype),) + (out,) * 4,
        in_specs=[spec()] * 14,
        out_specs=(spec(),) * 5,
        compiler_params=pltpu.CompilerParams(vmem_limit_bytes=24 * 2**20),
        cost_estimate=cost(12),
        name="projection_attention",
    )(*norms, *weights, bias, proj, *grads, after)


def attention_step(proj, grads, pairs, before):
    tokens = grads[0].shape[0]
    widths = [3 * len(pairs) * PAIR] * 4
    for i in range(len(before)):
        widths[2 * i] = 3 * HALF
    held = before[0].shape[1] // 3 if before else 0
    return pl.pallas_call(
        functools.partial(attention_kernel, pairs, held),
        out_shape=tuple(jax.ShapeDtypeStruct((tokens, width), jnp.bfloat16) for width in widths),
        in_specs=[spec()] * (6 + len(before)),
        out_specs=(spec(),) * 4,
        compiler_params=pltpu.CompilerParams(vmem_limit_bytes=24 * 2**20),
        cost_estimate=cost(12),
        name="attention",
    )(*proj, *grads, *before)


def near_shard(refs, j, pairs=None):
    def columns(ref):
        if pairs is None:
            return ref[...]
        first, last = pairs[0] * PAIR, (pairs[-1] + 1) * PAIR
        return jnp.concatenate([ref[:, part * HALF + first : part * HALF + last] for part in range(3)], axis=1)

    return columns(refs[j]) if j < 3 else jnp.concatenate([columns(ref) for ref in refs[3:5]], axis=0)


def join_skip(first, second):
    wide, narrow = first.shape[1] // 3, second.shape[1] // 3
    pieces = []
    for part in range(3):
        pieces += [first[:, part * wide : (part + 1) * wide], second[:, part * narrow : (part + 1) * narrow]]
    return jnp.concatenate(pieces, axis=1)


def on_middle():
    place = lax.axis_index("seq")
    return (place == 1) | (place == 2)


def early_kernel(*refs):
    near_w, far_w = refs[0:5], {0: refs[5], 2: refs[6]}
    own_ref, skip_first, skip_second, tokens_ref, sums, normed_out, inverse_out = refs[7:]
    middle = on_middle()
    mine = lax.axis_index("weight")
    depth = far_w[0].shape[0]

    def fill(value, weights, far):
        for j in range(4):
            at = pl.ds(pl.multiple_of((mine ^ j) * depth, QBLOCK), depth)
            if not far or j in weights:
                sums[:, at] = dot_last(value, weights[j][...] if far else near_shard(weights, j))
            else:
                sums[:, at] = jnp.zeros((value.shape[0], depth), jnp.float32)

    pl.when(middle)(lambda: fill(own_ref[...], near_w, False))
    pl.when(jnp.logical_not(middle))(lambda: fill(join_skip(skip_first, skip_second), far_w, True))
    for r in range(0, tokens_ref.shape[1], 16):
        normed, inverse = norm_rows(tokens_ref[0, r : r + 16, :].astype(jnp.float32))
        normed_out[r : r + 16, :] = normed
        inverse_out[r : r + 16, :] = jnp.broadcast_to(inverse, (16, QBLOCK))


def early_step(near_w, far_w, own, skips, tokens):
    rows, width = tokens.shape[1:]
    full = jax.ShapeDtypeStruct((rows, width), jnp.float32)
    return pl.pallas_call(
        early_kernel,
        out_shape=(full, full, jax.ShapeDtypeStruct((rows, QBLOCK), jnp.float32)),
        in_specs=[spec()] * 11,
        out_specs=(spec(),) * 3,
        compiler_params=pltpu.CompilerParams(vmem_limit_bytes=24 * 2**20),
        cost_estimate=cost(0.01),
        name="grad_norm_part",
    )(*near_w, *far_w, own, *skips, tokens)


def back_part_kernel(*refs):
    near_w, back_first, sums, out_ref = refs[0:5], refs[5], refs[6], refs[7]
    depth = near_w[0].shape[0]
    mine = lax.axis_index("weight")
    out_ref[...] = sums[...]

    @pl.when(jnp.logical_not(on_middle()))
    def _():
        back = back_first[...]
        for j in range(4):
            at = pl.ds(pl.multiple_of((mine ^ j) * depth, QBLOCK), depth)
            out_ref[:, at] = sums[:, at] + dot_last(back, near_shard(near_w, j, EARLY))


def back_part_step(near_w, back_first, sums):
    return pl.pallas_call(
        back_part_kernel,
        out_shape=jax.ShapeDtypeStruct(sums.shape, sums.dtype),
        in_specs=[spec()] * 7,
        out_specs=spec(),
        compiler_params=pltpu.CompilerParams(vmem_limit_bytes=24 * 2**20),
        cost_estimate=cost(50),
        name="back_part",
    )(*near_w, back_first, sums)


def pair_part_kernel(pair, skip_first, skip_second, sums, out_ref):
    mine = lax.axis_index("weight")
    depth = pair.shape[0] // 2
    out_ref[...] = sums[...]

    @pl.when(jnp.logical_not(on_middle()))
    def _():
        skip = join_skip(skip_first, skip_second)
        for i, j in enumerate((1, 3)):
            at = pl.ds(pl.multiple_of((mine ^ j) * depth, QBLOCK), depth)
            out_ref[:, at] = sums[:, at] + dot_last(skip, pair[i * depth : (i + 1) * depth])


def pair_part_step(pair, skips, sums):
    return pl.pallas_call(
        pair_part_kernel,
        out_shape=jax.ShapeDtypeStruct(sums.shape, sums.dtype),
        in_specs=[spec()] * 4,
        out_specs=spec(),
        compiler_params=pltpu.CompilerParams(vmem_limit_bytes=24 * 2**20),
        cost_estimate=cost(0.01),
        name="pair_part",
    )(pair, *skips, sums)


def last_kernel(*refs):
    near_w, pair = refs[0:5], refs[7]
    sums, cross_ref, back_ref, normed_ref, inverse_ref, gain_ref, out_ref = refs[8:15]
    gain, grad_hat, first_sum, second_sum, result, sems = refs[15:]
    middle = on_middle()
    mine = lax.axis_index("weight")
    depth = refs[5].shape[0]
    far_w = (refs[5], pair.at[:depth], refs[6], pair.at[depth:])
    gain[...] = row_vector(gain_ref)

    def fill(value_ref, weight_of):
        value = value_ref[...]
        first = second = jnp.zeros(first_sum.shape, jnp.float32)
        for j in range(4):
            at = pl.ds(pl.multiple_of((mine ^ j) * depth, QBLOCK), depth)
            hat = (sums[:, at] + dot_last(value, weight_of(j))) * gain[:, at]
            grad_hat[:, at] = hat
            mixed = hat * normed_ref[:, at]
            for c in range(0, depth, QBLOCK):
                first += hat[:, c : c + QBLOCK]
                second += mixed[:, c : c + QBLOCK]
        first_sum[...] = first
        second_sum[...] = second

    pl.when(middle)(lambda: fill(cross_ref, lambda j: far_w[j][...]))
    pl.when(jnp.logical_not(middle))(lambda: fill(back_ref, lambda j: near_shard(near_w, j, LATE)))
    rows, width = normed_ref.shape
    copies = []
    for i, first in enumerate(range(0, rows, ROWS_OUT)):
        for r in range(first, first + ROWS_OUT, 8):
            at = slice(r, r + 8)
            first_mean = jnp.sum(first_sum[at, :], axis=-1, keepdims=True) * (1.0 / width)
            second_mean = jnp.sum(second_sum[at, :], axis=-1, keepdims=True) * (1.0 / width)
            result[at, :] = inverse_ref[at, :1] * (
                grad_hat[at, :] - first_mean - normed_ref[at, :] * second_mean
            )
        lines = pl.ds(first, ROWS_OUT)
        copies.append(pltpu.make_async_copy(result.at[lines, :], out_ref.at[0, lines, :], sems.at[i]))
        copies[-1].start()
    for copy in copies:
        copy.wait()


def last_step(near_w, far_w, back, cross, sums, normed, inverse, gain):
    return pl.pallas_call(
        last_kernel,
        out_shape=jax.ShapeDtypeStruct((1, *normed.shape), jnp.float32),
        in_specs=[spec()] * 14,
        out_specs=spec(pltpu.HBM),
        scratch_shapes=[
            VMEM((1, normed.shape[1]), jnp.float32),
            VMEM(normed.shape, jnp.float32),
            VMEM((normed.shape[0], QBLOCK), jnp.float32),
            VMEM((normed.shape[0], QBLOCK), jnp.float32),
            VMEM(normed.shape, jnp.float32),
            pltpu.SemaphoreType.DMA((normed.shape[0] // ROWS_OUT,)),
        ],
        compiler_params=pltpu.CompilerParams(vmem_limit_bytes=24 * 2**20),
        cost_estimate=cost(2),
        name="input_grad",
    )(*near_w, *far_w, sums, cross, back, normed, inverse, gain)


def split_kernel(value_ref, upper_ref, lower_ref):
    middle = upper_ref.shape[0]
    upper_ref[...] = value_ref[:middle]
    lower_ref[...] = value_ref[middle:]


def split_step(value):
    half = jax.ShapeDtypeStruct((value.shape[0] // 2, value.shape[1]), value.dtype)
    return pl.pallas_call(
        split_kernel,
        out_shape=(half, half),
        in_specs=[spec()],
        out_specs=(spec(), spec()),
        compiler_params=pltpu.CompilerParams(vmem_limit_bytes=16 * 2**20),
        cost_estimate=cost(0.01),
        name="split_rows",
    )(value)


def pair_kernel(first_ref, second_ref, *refs):
    out_ref = refs[-1]
    middle = first_ref.shape[0]
    out_ref[:middle] = first_ref[...]
    out_ref[middle:] = second_ref[...]


def pair_step(first, second, *after):
    return pl.pallas_call(
        pair_kernel,
        out_shape=jax.ShapeDtypeStruct((2 * first.shape[0], first.shape[1]), first.dtype),
        in_specs=[spec()] * (2 + len(after)),
        out_specs=spec(),
        compiler_params=pltpu.CompilerParams(vmem_limit_bytes=16 * 2**20),
        cost_estimate=cost(0.01),
        name="chip_weight",
    )(first, second, *after)


EARLY = (0, 1)
LATE = (2,)
END_TO_MIDDLE = [(0, 1), (3, 2)]
MIDDLE = [(1, 2), (2, 1)]
END_TO_FAR = [(0, 2), (3, 1)]
MIDDLE_TO_END = [(1, 0), (2, 3)]
FAR_TO_END = [(1, 3), (2, 0)]


def flip(bit):
    return [(i, i ^ bit) for i in range(4)]


def local_middle(
    tokens,
    upstream_grad,
    norm_gain,
    norm_bias,
    input_codes,
    input_scales,
    input_bias,
    output_codes,
    output_scales,
    layer_scale,
):
    near, both_near, both_other = first_step(
        tokens, norm_gain, norm_bias, input_scales, input_codes, upstream_grad, layer_scale, output_scales, output_codes
    )
    both_mid = lax.ppermute(both_other, "seq", MIDDLE)
    both_far = lax.ppermute(both_other, "seq", END_TO_FAR)
    both_end = lax.ppermute(both_near, "seq", END_TO_MIDDLE)
    near_across = lax.ppermute(near, "weight", flip(2))
    near_beside = lax.ppermute(near, "weight", flip(1))
    near_diagonal = [lax.ppermute(w, "weight", flip(1)) for w in split_step(near_across)]
    far = far_step(input_scales, input_codes, near_across)
    far_across = lax.ppermute(far, "weight", flip(2))
    rows = (both_near, both_end, both_mid, both_far)
    near_w = (near, near_beside, near_across, *near_diagonal)
    proj = project_step(rows[:2], near_w, input_bias)
    grads = (both_near, both_end, both_mid, both_far)
    proj_last, own, end, mid, skip_first = project_attention_step(
        rows[2:], near_w, input_bias, proj, grads, EARLY, far
    )
    back_first = lax.ppermute(end, "seq", MIDDLE_TO_END)
    skip_first = lax.ppermute(skip_first, "seq", FAR_TO_END)
    own, end, mid, skip_second = attention_step((proj, proj_last), grads, LATE, (own, mid))
    skip_second = lax.ppermute(skip_second, "seq", FAR_TO_END)
    cross = lax.ppermute(mid, "seq", MIDDLE)
    back = lax.ppermute(end, "seq", MIDDLE_TO_END)
    far_pair = lax.ppermute(pair_step(far, far_across, skip_first, own), "weight", flip(1))
    far_w = (far, far_across)
    skips = (skip_first, skip_second)
    sums, normed, inverse = early_step(near_w, far_w, own, skips, tokens)
    sums = back_part_step(near_w, back_first, sums)
    sums = pair_part_step(far_pair, skips, sums)
    return last_step(near_w, (*far_w, far_pair), back, cross, sums, normed, inverse, norm_gain)


def dequantize(codes, scales):
    expanded = jnp.repeat(jnp.repeat(scales, QBLOCK, axis=0), QBLOCK, axis=1)
    return (codes.astype(jnp.float32) * expanded).astype(jnp.bfloat16)


def normalize(rows, gain, shift):
    mean_value = jnp.mean(rows, axis=-1, keepdims=True)
    centered = rows - mean_value
    variance = jnp.mean(centered * centered, axis=-1, keepdims=True)
    inverse = lax.rsqrt(variance + 1e-06)
    normed = centered * inverse
    return (normed, inverse, (normed * gain + shift).astype(jnp.bfloat16))


def norm_backward(grad_norm, normed, inverse, gain):
    grad_hat = grad_norm * gain
    first_mean = jnp.mean(grad_hat, axis=-1, keepdims=True)
    second_mean = jnp.mean(grad_hat * normed, axis=-1, keepdims=True)
    return inverse * (grad_hat - first_mean - normed * second_mean)


def score_block(queries, head_grads, pair_block):
    row_count = pair_block.shape[0]
    keys_blk = pair_block[:, :HD].reshape(row_count, HEADS, HEAD_DIM)
    values_blk = pair_block[:, HD:].reshape(row_count, HEADS, HEAD_DIM)
    scores = jnp.einsum(
        "qhd,khd->hqk", queries, keys_blk, preferred_element_type=jnp.float32
    ) * HEAD_DIM ** (-0.5)
    dprob = jnp.einsum("qhd,khd->hqk", head_grads, values_blk, preferred_element_type=jnp.float32)
    return (keys_blk, scores, dprob)


def update_stats(statistics, queries, head_grads, pair_rows):
    sub_size = math.gcd(pair_rows.shape[0], 512)

    def visit_block(block_index, running):
        run_max, run_total, run_mix = running
        pair_block = lax.dynamic_slice_in_dim(pair_rows, block_index * sub_size, sub_size, 0)
        keys_blk, scores, dprob = score_block(queries, head_grads, pair_block)
        new_max = jnp.maximum(run_max, jnp.max(scores, axis=-1))
        factor = jnp.exp(run_max - new_max)
        expo = jnp.exp(scores - new_max[..., None])
        return (
            new_max,
            run_total * factor + jnp.sum(expo, axis=-1),
            run_mix * factor + jnp.sum(expo * dprob, axis=-1),
        )

    return lax.fori_loop(0, pair_rows.shape[0] // sub_size, visit_block, statistics)


def block_backward(queries, head_grads, pair_block, log_total, row_delta):
    keys_blk, scores, dprob = score_block(queries, head_grads, pair_block)
    weights = jnp.exp(scores - log_total[..., None])
    prob_weights = weights.astype(jnp.bfloat16)
    dscore = (weights * (dprob - row_delta[..., None])).astype(jnp.bfloat16)
    return (keys_blk, prob_weights, dscore)


def key_terms_from(queries, head_grads, prob_weights, dscore):
    key_part = jnp.einsum(
        "hqk,qhd->khd", dscore, queries, preferred_element_type=jnp.float32
    ) * HEAD_DIM ** (-0.5)
    value_part = jnp.einsum(
        "hqk,qhd->khd", prob_weights, head_grads, preferred_element_type=jnp.float32
    )
    row_count = key_part.shape[0]
    return jnp.concatenate(
        [key_part.reshape(row_count, HD), value_part.reshape(row_count, HD)], axis=1
    )


def query_side(queries, head_grads, keys_values, local_rows):
    seq_rows = local_rows * lax.axis_size("seq")
    start_stats = (
        jnp.full((HEADS, local_rows), -1e30, jnp.float32),
        jnp.zeros((HEADS, local_rows), jnp.float32),
        jnp.zeros((HEADS, local_rows), jnp.float32),
    )
    all_pairs = lax.all_gather(keys_values, "seq", axis=0, tiled=True)
    statistics = update_stats(start_stats, queries, head_grads, all_pairs)
    row_max, row_total, row_mix = statistics
    log_total = row_max + jnp.log(row_total)
    row_delta = row_mix / row_total
    sub_size = math.gcd(seq_rows, 512)
    block_count = seq_rows // sub_size
    empty_query = jnp.zeros((local_rows, HEADS, HEAD_DIM), jnp.float32)

    def backward_step(block_index, running):
        query_grad, buffer = running
        pair_block = lax.dynamic_slice_in_dim(all_pairs, block_index * sub_size, sub_size, 0)
        keys_blk, prob_weights, dscore = block_backward(
            queries, head_grads, pair_block, log_total, row_delta
        )
        query_grad = query_grad + jnp.einsum(
            "hqk,khd->qhd", dscore, keys_blk, preferred_element_type=jnp.float32
        )
        block_terms = key_terms_from(queries, head_grads, prob_weights, dscore)
        buffer = lax.dynamic_update_slice_in_dim(buffer, block_terms, block_index * sub_size, 0)
        return (query_grad, buffer)

    empty_terms = jnp.zeros((seq_rows, 2 * HD), jnp.float32)
    query_grad, buffer = lax.fori_loop(0, block_count, backward_step, (empty_query, empty_terms))
    pair_grads = lax.psum_scatter(
        buffer.astype(jnp.bfloat16), "seq", scatter_dimension=0, tiled=True
    ).astype(jnp.float32)
    return (query_grad, pair_grads)


def local(
    tokens,
    upstream_grad,
    norm_gain,
    norm_bias,
    input_codes,
    input_scales,
    input_bias,
    output_codes,
    output_scales,
    layer_scale,
):
    all_codes, all_scales = (
        lax.all_gather(input_codes.astype(jnp.float32), "weight", axis=0, tiled=True).astype(
            input_codes.dtype
        ),
        lax.all_gather(input_scales, "weight", axis=0, tiled=True),
    )
    input_weight = dequantize(all_codes, all_scales)
    output_weight = dequantize(output_codes, output_scales)
    normed, inverse, norm_out = normalize(tokens[0].astype(jnp.float32), norm_gain, norm_bias)
    projected = (
        jnp.dot(norm_out, input_weight, preferred_element_type=jnp.float32) + input_bias
    ).astype(jnp.bfloat16)
    local_rows = projected.shape[0]
    queries = projected[:, :HD].reshape(local_rows, HEADS, HEAD_DIM)
    keys_values = projected[:, HD:]
    scaled_grad = (upstream_grad[0].astype(jnp.float32) * layer_scale).astype(jnp.bfloat16)
    head_grads = jnp.dot(scaled_grad, output_weight.T, preferred_element_type=jnp.float32).astype(
        jnp.bfloat16
    )
    head_grads = head_grads.reshape(local_rows, HEADS, HEAD_DIM)
    query_grad, pair_grads = query_side(queries, head_grads, keys_values, local_rows)
    query_grad = (query_grad * HEAD_DIM ** (-0.5)).reshape(local_rows, HD)
    grad_proj = jnp.concatenate([query_grad, pair_grads], axis=1).astype(jnp.bfloat16)
    grad_norm = jnp.dot(grad_proj, input_weight.T, preferred_element_type=jnp.float32)
    result = norm_backward(grad_norm, normed, inverse, norm_gain)
    return result[None]


def solution(mesh):
    in_specs = (
        P(("groups", "weight"), "seq", None),
        P(("groups", "weight"), "seq", None),
        P(),
        P(),
        P("weight", None),
        P("weight", None),
        P(),
        P(),
        P(),
        P(),
    )
    out_specs = P(("groups", "weight"), "seq", None)
    fits = mesh.shape["seq"] == 4 and mesh.shape["weight"] == 4
    plan = local_middle if fits else local
    return jax.shard_map(plan, mesh=mesh, in_specs=in_specs, out_specs=out_specs, check_vma=False)
```

```python
import functools
import math

import jax
import jax.numpy as jnp
from jax import lax
from jax.experimental import pallas as pl
from jax.experimental.pallas import tpu as pltpu
from jax.sharding import PartitionSpec as P

HEADS = 12
HEAD_DIM = 64
QBLOCK = 128
HD = 768
HALF = HD // 2
ROWS_OUT = 64
EPSILON = 1e-06
VMEM = pltpu.VMEM
SMEM = pltpu.SMEM


def half_index():
    return lax.axis_index("seq") * 2 // lax.axis_size("seq")


def cost(micros):
    return pl.CostEstimate(flops=int(micros * 1.0e9), bytes_accessed=int(micros * 3.0e6), transcendentals=0)


def spec(memory_space=VMEM):
    return pl.BlockSpec(memory_space=memory_space)


def norm_rows(rows):
    mean_value = jnp.mean(rows, axis=-1, keepdims=True)
    centered = rows - mean_value
    variance = jnp.mean(centered * centered, axis=-1, keepdims=True)
    inverse = lax.rsqrt(variance + EPSILON)
    return centered * inverse, inverse


def row_vector(ref):
    return ref[...].reshape(1, ref.shape[0])


def scale_block(codes, scale):
    return (codes.astype(jnp.float32) * scale).astype(jnp.bfloat16)


def first_kernel(
    tokens_ref, gain_ref, shift_ref, scales_ref, codes_ref, grad_ref, layer_ref, out_scales_ref, out_codes_ref,
    weight_out, near_out, far_out,
    tokens, gain, shift, scales, codes, grad, layer, out_scales, out_codes, scaled, weight, far, sems
):
    half = half_index()
    other = 1 - half
    blocks = HALF // QBLOCK

    def copy(source, target, at):
        started = pltpu.make_async_copy(source, target, sems.at[at])
        started.start()
        return started

    def columns(part):
        return codes_ref.at[:, pl.ds(pl.multiple_of(part * HD + half * HALF, QBLOCK), HALF)]

    def rows(which):
        return out_codes_ref.at[pl.ds(pl.multiple_of(which * HALF, QBLOCK), HALF), :]

    tokens_copies = [
        copy(tokens_ref, tokens, 4), copy(gain_ref, gain, 5), copy(shift_ref, shift, 6)
    ]
    scales_copy = copy(scales_ref, scales, 0)
    codes_copies = [copy(columns(part), codes.at[part], 1 + part) for part in range(3)]
    grad_copies = [
        copy(grad_ref, grad, 7), copy(layer_ref, layer, 8), copy(out_scales_ref, out_scales, 9)
    ]
    out_copies = [copy(rows(other), out_codes.at[0], 10), copy(rows(half), out_codes.at[1], 11)]

    for started in tokens_copies:
        started.wait()
    width = tokens.shape[2]
    gain_row = row_vector(gain)
    shift_row = row_vector(shift)
    for r in range(0, tokens.shape[1], 16):
        normed, _ = norm_rows(tokens[0, r : r + 16, :].astype(jnp.float32))
        norm_out = (normed * gain_row + shift_row).astype(jnp.bfloat16)
        near_out[r : r + 16, :width] = norm_out
        far[r : r + 16, :width] = norm_out

    scales_copy.wait()
    for part in range(3):
        codes_copies[part].wait()
        for r in range(codes_ref.shape[0] // QBLOCK):
            for c in range(blocks):
                scale = scales[r, (part * HD) // QBLOCK + half * blocks + c]
                lines = slice(r * QBLOCK, (r + 1) * QBLOCK)
                weight_out[lines, part * HALF + c * QBLOCK : part * HALF + (c + 1) * QBLOCK] = scale_block(
                    codes[part, lines, c * QBLOCK : (c + 1) * QBLOCK], scale
                )

    for started in grad_copies:
        started.wait()
    scaled[...] = (grad[0].astype(jnp.float32) * row_vector(layer)).astype(jnp.bfloat16)
    for i, (out_ref, which) in enumerate(((far, other), (near_out, half))):
        out_copies[i].wait()
        for r in range(blocks):
            lines = slice(r * QBLOCK, (r + 1) * QBLOCK)
            for c in range(width // QBLOCK):
                at = slice(c * QBLOCK, (c + 1) * QBLOCK)
                weight[lines, at] = scale_block(out_codes[i, lines, at], out_scales[which * blocks + r, c])
        out_ref[:, width:] = dot_last(scaled[...], weight[...]).astype(jnp.bfloat16)
        if out_ref is far:
            far_copy = copy(far, far_out, 12)
    far_copy.wait()


def first_step(tokens, gain, shift, scales, codes, grad, layer_scale, out_scales, out_codes):
    lines, width = tokens.shape[1:]
    depth = codes.shape[0]
    return pl.pallas_call(
        first_kernel,
        out_shape=(
            VMEM((depth, 3 * HALF), jnp.bfloat16),
            VMEM((lines, width + HALF), jnp.bfloat16),
            jax.ShapeDtypeStruct((lines, width + HALF), jnp.bfloat16),
        ),
        in_specs=[spec(pltpu.HBM)] * 9,
        out_specs=(spec(), spec(), spec(pltpu.HBM)),
        scratch_shapes=[
            VMEM(tokens.shape, tokens.dtype),
            VMEM(gain.shape, gain.dtype),
            VMEM(shift.shape, shift.dtype),
            SMEM(scales.shape, scales.dtype),
            VMEM((3, depth, HALF), codes.dtype),
            VMEM(grad.shape, grad.dtype),
            VMEM(layer_scale.shape, layer_scale.dtype),
            SMEM(out_scales.shape, out_scales.dtype),
            VMEM((2, HALF, width), out_codes.dtype),
            VMEM((lines, width), jnp.bfloat16),
            VMEM((HALF, width), jnp.bfloat16),
            VMEM((lines, width + HALF), jnp.bfloat16),
            pltpu.SemaphoreType.DMA((13,)),
        ],
        compiler_params=pltpu.CompilerParams(vmem_limit_bytes=60 * 2**20),
        cost_estimate=cost(3),
        name="first_weights_and_rows",
    )(tokens, gain, shift, scales, codes, grad, layer_scale, out_scales, out_codes)


def far_kernel(scales_ref, codes_ref, after_ref, weight_out, scales, codes, sems):
    other = 1 - half_index()
    blocks = HALF // QBLOCK
    copies = [pltpu.make_async_copy(scales_ref, scales, sems.at[3])]
    for part in range(3):
        at = pl.ds(pl.multiple_of(part * HD + other * HALF, QBLOCK), HALF)
        copies.append(pltpu.make_async_copy(codes_ref.at[:, at], codes.at[part], sems.at[part]))
    for started in copies:
        started.start()
    for started in copies:
        started.wait()
    for part in range(3):
        for r in range(codes_ref.shape[0] // QBLOCK):
            for c in range(blocks):
                scale = scales[r, (part * HD) // QBLOCK + other * blocks + c]
                lines = slice(r * QBLOCK, (r + 1) * QBLOCK)
                weight_out[lines, part * HALF + c * QBLOCK : part * HALF + (c + 1) * QBLOCK] = scale_block(
                    codes[part, lines, c * QBLOCK : (c + 1) * QBLOCK], scale
                )


def far_step(scales, codes, after):
    depth = codes.shape[0]
    return pl.pallas_call(
        far_kernel,
        out_shape=jax.ShapeDtypeStruct((depth, 3 * HALF), jnp.bfloat16),
        in_specs=[spec(pltpu.HBM), spec(pltpu.HBM), spec()],
        out_specs=spec(),
        scratch_shapes=[
            SMEM(scales.shape, scales.dtype),
            VMEM((3, depth, HALF), codes.dtype),
            pltpu.SemaphoreType.DMA((4,)),
        ],
        compiler_params=pltpu.CompilerParams(vmem_limit_bytes=16 * 2**20),
        cost_estimate=cost(0.01),
        name="far_weight",
    )(scales, codes, after)


def dot_last(a, b):
    return lax.dot_general(a, b, (((1,), (1,)), ((), ())), preferred_element_type=jnp.float32)


def dot_plain(a, b):
    return jnp.dot(a, b, preferred_element_type=jnp.float32)


def norm_columns(norms, picks, depth):
    mine = lax.axis_index("weight")
    return jnp.concatenate(
        [
            jnp.concatenate(
                [norm_ref[:, pl.ds(pl.multiple_of((mine ^ j) * depth, QBLOCK), depth)] for j in picks],
                axis=1,
            )
            for norm_ref in norms
        ],
        axis=0,
    )


def project_part(norms, weights, bias_ref, proj, first, part):
    half = half_index()
    rows = norm_columns(norms, range(4), weights[0].shape[0])
    bias = row_vector(bias_ref)
    at = slice(part * HALF, (part + 1) * HALF)
    shift = jnp.where(
        half == 0,
        bias[:, part * HD : part * HD + HALF],
        bias[:, part * HD + HALF : (part + 1) * HD],
    )
    columns = jnp.concatenate([w[:, at] for w in weights], axis=0)
    value = (dot_plain(rows, columns) + shift).astype(jnp.bfloat16)
    if part == 0:
        value = value * jnp.bfloat16(HEAD_DIM**-0.5)
    proj[first : first + rows.shape[0], at] = value


def project_kernel(*refs):
    for part in range(3):
        project_part(refs[0:2], refs[2:7], refs[7], refs[8], 0, part)


def project_step(norms, weights, bias):
    tokens = norms[0].shape[0]
    return pl.pallas_call(
        project_kernel,
        out_shape=jax.ShapeDtypeStruct((2 * tokens, 3 * HALF), jnp.bfloat16),
        in_specs=[spec()] * 8,
        out_specs=spec(),
        compiler_params=pltpu.CompilerParams(vmem_limit_bytes=24 * 2**20),
        cost_estimate=cost(0.01),
        name="projection",
    )(*norms, *weights, bias)


PAIR = 2 * HEAD_DIM


def soft_part(scores, dprob):
    expo = jnp.exp(scores - jnp.max(scores, axis=0, keepdims=True))
    scale = 1.0 / jnp.sum(expo, axis=0, keepdims=True)
    delta = jnp.sum(expo * dprob, axis=0, keepdims=True) * scale
    prob = (expo * scale).astype(jnp.bfloat16)
    return prob, prob * (dprob - delta).astype(jnp.bfloat16)


def attention_kernel(pairs, held, *refs):
    proj, grads, before, outs = refs[0:2], refs[2:6], refs[6:-4], refs[-4:]
    attention(pairs, held, proj, grads, before, outs)


def project_attention_kernel(pairs, *refs):
    norms, weights, bias_ref, proj_in, grads = refs[0:2], refs[2:7], refs[7], refs[8], refs[9:13]
    proj, outs = refs[-5], refs[-4:]

    def project(part):
        project_part(norms, weights, bias_ref, proj, 0, part)

    project(0)
    project(1)
    attention(pairs, 0, (proj_in, proj), grads, (), outs, lambda: project(2))


def attention(pairs, held, proj, grads, before, outs, between=None):
    total = sum(ref.shape[0] for ref in proj)
    tokens = grads[0].shape[0]
    low = lax.broadcasted_iota(jnp.int32, (total, PAIR), 1) < HEAD_DIM
    zero = jnp.zeros((total, PAIR), jnp.bfloat16)

    def load(t):
        query, key, value = (
            jnp.concatenate([p[:, part * HALF + t * PAIR : part * HALF + (t + 1) * PAIR] for p in proj], axis=0)
            for part in range(3)
        )
        grad = jnp.concatenate(
            [g[:, g.shape[1] - HALF + t * PAIR : g.shape[1] - HALF + (t + 1) * PAIR] for g in grads], axis=0
        )
        return query, key, value, grad

    def mask(side, value):
        return jnp.where(low, value, zero) if side == 0 else jnp.where(low, zero, value)

    def before_soft(t, side, between=None):
        query, key, value, grad = load(t)
        scores = dot_last(mask(side, key), query)
        if between is not None:
            between()
            value = load(t)[2]
        return scores, dot_last(mask(side, value), grad)

    def after_soft(t, side, prob, dscore):
        query, key, _, grad = load(t)
        key_t = key.T[side * HEAD_DIM : (side + 1) * HEAD_DIM]
        return (
            dot_plain(key_t, dscore),
            dot_plain(dscore, mask(side, query)),
            dot_plain(prob, mask(side, grad)),
        )

    def store(t, first, second):
        place = pairs.index(t)
        query_grad = jnp.concatenate([first[0], second[0]], axis=0).T * HEAD_DIM**-0.5
        for part, piece in enumerate((query_grad, first[1] + second[1], first[2] + second[2])):
            piece = piece.astype(jnp.bfloat16)
            for i, out in enumerate(outs):
                whole = out.shape[1] == 3 * HALF
                at = part * HALF + t * PAIR if whole else (part * len(pairs) + place) * PAIR
                out[:, at : at + PAIR] = piece[i * tokens : (i + 1) * tokens]

    heads = [(t, side) for t in pairs for side in range(2)]
    done = {}

    def finish(t, side, *soft):
        done[t, side] = after_soft(t, side, *soft)
        if side == 1:
            store(t, done[t, 0], done[t, 1])

    ready, behind = before_soft(*heads[0], between), None
    for i, head in enumerate(heads):
        now = ready
        if i + 1 < len(heads):
            ready = before_soft(*heads[i + 1])
        if behind is not None:
            finish(*behind)
        behind = (*head, *soft_part(*now))
    finish(*behind)
    for old, out in zip(before, outs[0:3:2]):
        for part in range(3):
            out[:, part * HALF : part * HALF + held] = old[:, part * held : (part + 1) * held]


def project_attention_step(norms, weights, bias, proj, grads, pairs, after):
    tokens = grads[0].shape[0]
    out = jax.ShapeDtypeStruct((tokens, 3 * len(pairs) * PAIR), jnp.bfloat16)
    return pl.pallas_call(
        functools.partial(project_attention_kernel, pairs),
        out_shape=(jax.ShapeDtypeStruct(proj.shape, proj.dtype),) + (out,) * 4,
        in_specs=[spec()] * 14,
        out_specs=(spec(),) * 5,
        compiler_params=pltpu.CompilerParams(vmem_limit_bytes=24 * 2**20),
        cost_estimate=cost(12),
        name="projection_attention",
    )(*norms, *weights, bias, proj, *grads, after)


def attention_step(proj, grads, pairs, before):
    tokens = grads[0].shape[0]
    widths = [3 * len(pairs) * PAIR] * 4
    for i in range(len(before)):
        widths[2 * i] = 3 * HALF
    held = before[0].shape[1] // 3 if before else 0
    return pl.pallas_call(
        functools.partial(attention_kernel, pairs, held),
        out_shape=tuple(jax.ShapeDtypeStruct((tokens, width), jnp.bfloat16) for width in widths),
        in_specs=[spec()] * (6 + len(before)),
        out_specs=(spec(),) * 4,
        compiler_params=pltpu.CompilerParams(vmem_limit_bytes=24 * 2**20),
        cost_estimate=cost(12),
        name="attention",
    )(*proj, *grads, *before)


def near_shard(refs, j, pairs=None):
    def columns(ref):
        if pairs is None:
            return ref[...]
        first, last = pairs[0] * PAIR, (pairs[-1] + 1) * PAIR
        return jnp.concatenate([ref[:, part * HALF + first : part * HALF + last] for part in range(3)], axis=1)

    return columns(refs[j]) if j < 3 else jnp.concatenate([columns(ref) for ref in refs[3:5]], axis=0)


def join_skip(first, second):
    wide, narrow = first.shape[1] // 3, second.shape[1] // 3
    pieces = []
    for part in range(3):
        pieces += [first[:, part * wide : (part + 1) * wide], second[:, part * narrow : (part + 1) * narrow]]
    return jnp.concatenate(pieces, axis=1)


def on_middle():
    place = lax.axis_index("seq")
    return (place == 1) | (place == 2)


def early_kernel(*refs):
    near_w, far_w = refs[0:5], {0: refs[5], 2: refs[6]}
    own_ref, skip_first, skip_second, tokens_ref, sums, normed_out, inverse_out = refs[7:]
    middle = on_middle()
    mine = lax.axis_index("weight")
    depth = far_w[0].shape[0]

    def fill(value, weights, far):
        for j in range(4):
            at = pl.ds(pl.multiple_of((mine ^ j) * depth, QBLOCK), depth)
            if not far or j in weights:
                sums[:, at] = dot_last(value, weights[j][...] if far else near_shard(weights, j))
            else:
                sums[:, at] = jnp.zeros((value.shape[0], depth), jnp.float32)

    pl.when(middle)(lambda: fill(own_ref[...], near_w, False))
    pl.when(jnp.logical_not(middle))(lambda: fill(join_skip(skip_first, skip_second), far_w, True))
    for r in range(0, tokens_ref.shape[1], 16):
        normed, inverse = norm_rows(tokens_ref[0, r : r + 16, :].astype(jnp.float32))
        normed_out[r : r + 16, :] = normed
        inverse_out[r : r + 16, :] = jnp.broadcast_to(inverse, (16, QBLOCK))


def early_step(near_w, far_w, own, skips, tokens):
    rows, width = tokens.shape[1:]
    full = jax.ShapeDtypeStruct((rows, width), jnp.float32)
    return pl.pallas_call(
        early_kernel,
        out_shape=(full, full, jax.ShapeDtypeStruct((rows, QBLOCK), jnp.float32)),
        in_specs=[spec()] * 11,
        out_specs=(spec(),) * 3,
        compiler_params=pltpu.CompilerParams(vmem_limit_bytes=24 * 2**20),
        cost_estimate=cost(0.01),
        name="grad_norm_part",
    )(*near_w, *far_w, own, *skips, tokens)


def back_part_kernel(*refs):
    near_w, back_first, sums, out_ref = refs[0:5], refs[5], refs[6], refs[7]
    depth = near_w[0].shape[0]
    mine = lax.axis_index("weight")
    out_ref[...] = sums[...]

    @pl.when(jnp.logical_not(on_middle()))
    def _():
        back = back_first[...]
        for j in range(4):
            at = pl.ds(pl.multiple_of((mine ^ j) * depth, QBLOCK), depth)
            out_ref[:, at] = sums[:, at] + dot_last(back, near_shard(near_w, j, EARLY))


def back_part_step(near_w, back_first, sums):
    return pl.pallas_call(
        back_part_kernel,
        out_shape=jax.ShapeDtypeStruct(sums.shape, sums.dtype),
        in_specs=[spec()] * 7,
        out_specs=spec(),
        compiler_params=pltpu.CompilerParams(vmem_limit_bytes=24 * 2**20),
        cost_estimate=cost(50),
        name="back_part",
    )(*near_w, back_first, sums)


def pair_part_kernel(pair, skip_first, skip_second, sums, out_ref):
    mine = lax.axis_index("weight")
    depth = pair.shape[0] // 2
    out_ref[...] = sums[...]

    @pl.when(jnp.logical_not(on_middle()))
    def _():
        skip = join_skip(skip_first, skip_second)
        for i, j in enumerate((1, 3)):
            at = pl.ds(pl.multiple_of((mine ^ j) * depth, QBLOCK), depth)
            out_ref[:, at] = sums[:, at] + dot_last(skip, pair[i * depth : (i + 1) * depth])


def pair_part_step(pair, skips, sums):
    return pl.pallas_call(
        pair_part_kernel,
        out_shape=jax.ShapeDtypeStruct(sums.shape, sums.dtype),
        in_specs=[spec()] * 4,
        out_specs=spec(),
        compiler_params=pltpu.CompilerParams(vmem_limit_bytes=24 * 2**20),
        cost_estimate=cost(0.01),
        name="pair_part",
    )(pair, *skips, sums)


def last_kernel(*refs):
    near_w, pair = refs[0:5], refs[7]
    sums, cross_ref, back_ref, normed_ref, inverse_ref, gain_ref, out_ref = refs[8:15]
    gain, grad_hat, first_sum, second_sum, result, sems = refs[15:]
    middle = on_middle()
    mine = lax.axis_index("weight")
    depth = refs[5].shape[0]
    far_w = (refs[5], pair.at[:depth], refs[6], pair.at[depth:])
    gain[...] = row_vector(gain_ref)

    def fill(value_ref, weight_of):
        value = value_ref[...]
        first = second = jnp.zeros(first_sum.shape, jnp.float32)
        for j in range(4):
            at = pl.ds(pl.multiple_of((mine ^ j) * depth, QBLOCK), depth)
            hat = (sums[:, at] + dot_last(value, weight_of(j))) * gain[:, at]
            grad_hat[:, at] = hat
            mixed = hat * normed_ref[:, at]
            for c in range(0, depth, QBLOCK):
                first += hat[:, c : c + QBLOCK]
                second += mixed[:, c : c + QBLOCK]
        first_sum[...] = first
        second_sum[...] = second

    pl.when(middle)(lambda: fill(cross_ref, lambda j: far_w[j][...]))
    pl.when(jnp.logical_not(middle))(lambda: fill(back_ref, lambda j: near_shard(near_w, j, LATE)))
    rows, width = normed_ref.shape
    copies = []
    for i, first in enumerate(range(0, rows, ROWS_OUT)):
        for r in range(first, first + ROWS_OUT, 8):
            at = slice(r, r + 8)
            first_mean = jnp.sum(first_sum[at, :], axis=-1, keepdims=True) * (1.0 / width)
            second_mean = jnp.sum(second_sum[at, :], axis=-1, keepdims=True) * (1.0 / width)
            result[at, :] = inverse_ref[at, :1] * (
                grad_hat[at, :] - first_mean - normed_ref[at, :] * second_mean
            )
        lines = pl.ds(first, ROWS_OUT)
        copies.append(pltpu.make_async_copy(result.at[lines, :], out_ref.at[0, lines, :], sems.at[i]))
        copies[-1].start()
    for copy in copies:
        copy.wait()


def last_step(near_w, far_w, back, cross, sums, normed, inverse, gain):
    return pl.pallas_call(
        last_kernel,
        out_shape=jax.ShapeDtypeStruct((1, *normed.shape), jnp.float32),
        in_specs=[spec()] * 14,
        out_specs=spec(pltpu.HBM),
        scratch_shapes=[
            VMEM((1, normed.shape[1]), jnp.float32),
            VMEM(normed.shape, jnp.float32),
            VMEM((normed.shape[0], QBLOCK), jnp.float32),
            VMEM((normed.shape[0], QBLOCK), jnp.float32),
            VMEM(normed.shape, jnp.float32),
            pltpu.SemaphoreType.DMA((normed.shape[0] // ROWS_OUT,)),
        ],
        compiler_params=pltpu.CompilerParams(vmem_limit_bytes=24 * 2**20),
        cost_estimate=cost(2),
        name="input_grad",
    )(*near_w, *far_w, sums, cross, back, normed, inverse, gain)


def split_kernel(value_ref, upper_ref, lower_ref):
    middle = upper_ref.shape[0]
    upper_ref[...] = value_ref[:middle]
    lower_ref[...] = value_ref[middle:]


def split_step(value):
    half = jax.ShapeDtypeStruct((value.shape[0] // 2, value.shape[1]), value.dtype)
    return pl.pallas_call(
        split_kernel,
        out_shape=(half, half),
        in_specs=[spec()],
        out_specs=(spec(), spec()),
        compiler_params=pltpu.CompilerParams(vmem_limit_bytes=16 * 2**20),
        cost_estimate=cost(0.01),
        name="split_rows",
    )(value)


def pair_kernel(first_ref, second_ref, *refs):
    out_ref = refs[-1]
    middle = first_ref.shape[0]
    out_ref[:middle] = first_ref[...]
    out_ref[middle:] = second_ref[...]


def pair_step(first, second, *after):
    return pl.pallas_call(
        pair_kernel,
        out_shape=jax.ShapeDtypeStruct((2 * first.shape[0], first.shape[1]), first.dtype),
        in_specs=[spec()] * (2 + len(after)),
        out_specs=spec(),
        compiler_params=pltpu.CompilerParams(vmem_limit_bytes=16 * 2**20),
        cost_estimate=cost(0.01),
        name="chip_weight",
    )(first, second, *after)


EARLY = (0, 1)
LATE = (2,)
END_TO_MIDDLE = [(0, 1), (3, 2)]
MIDDLE = [(1, 2), (2, 1)]
END_TO_FAR = [(0, 2), (3, 1)]
MIDDLE_TO_END = [(1, 0), (2, 3)]
FAR_TO_END = [(1, 3), (2, 0)]


def flip(bit):
    return [(i, i ^ bit) for i in range(4)]


def local_middle(
    tokens,
    upstream_grad,
    norm_gain,
    norm_bias,
    input_codes,
    input_scales,
    input_bias,
    output_codes,
    output_scales,
    layer_scale,
):
    near, both_near, both_other = first_step(
        tokens, norm_gain, norm_bias, input_scales, input_codes, upstream_grad, layer_scale, output_scales, output_codes
    )
    both_mid = lax.ppermute(both_other, "seq", MIDDLE)
    both_far = lax.ppermute(both_other, "seq", END_TO_FAR)
    both_end = lax.ppermute(both_near, "seq", END_TO_MIDDLE)
    near_across = lax.ppermute(near, "weight", flip(2))
    near_beside = lax.ppermute(near, "weight", flip(1))
    near_diagonal = [lax.ppermute(w, "weight", flip(1)) for w in split_step(near_across)]
    far = far_step(input_scales, input_codes, near_across)
    far_across = lax.ppermute(far, "weight", flip(2))
    rows = (both_near, both_end, both_mid, both_far)
    near_w = (near, near_beside, near_across, *near_diagonal)
    proj = project_step(rows[:2], near_w, input_bias)
    grads = (both_near, both_end, both_mid, both_far)
    proj_last, own, end, mid, skip_first = project_attention_step(
        rows[2:], near_w, input_bias, proj, grads, EARLY, far
    )
    back_first = lax.ppermute(end, "seq", MIDDLE_TO_END)
    skip_first = lax.ppermute(skip_first, "seq", FAR_TO_END)
    own, end, mid, skip_second = attention_step((proj, proj_last), grads, LATE, (own, mid))
    skip_second = lax.ppermute(skip_second, "seq", FAR_TO_END)
    cross = lax.ppermute(mid, "seq", MIDDLE)
    back = lax.ppermute(end, "seq", MIDDLE_TO_END)
    far_pair = lax.ppermute(pair_step(far, far_across, skip_first, own), "weight", flip(1))
    far_w = (far, far_across)
    skips = (skip_first, skip_second)
    sums, normed, inverse = early_step(near_w, far_w, own, skips, tokens)
    sums = back_part_step(near_w, back_first, sums)
    sums = pair_part_step(far_pair, skips, sums)
    return last_step(near_w, (*far_w, far_pair), back, cross, sums, normed, inverse, norm_gain)


def dequantize(codes, scales):
    expanded = jnp.repeat(jnp.repeat(scales, QBLOCK, axis=0), QBLOCK, axis=1)
    return (codes.astype(jnp.float32) * expanded).astype(jnp.bfloat16)


def normalize(rows, gain, shift):
    mean_value = jnp.mean(rows, axis=-1, keepdims=True)
    centered = rows - mean_value
    variance = jnp.mean(centered * centered, axis=-1, keepdims=True)
    inverse = lax.rsqrt(variance + 1e-06)
    normed = centered * inverse
    return (normed, inverse, (normed * gain + shift).astype(jnp.bfloat16))


def norm_backward(grad_norm, normed, inverse, gain):
    grad_hat = grad_norm * gain
    first_mean = jnp.mean(grad_hat, axis=-1, keepdims=True)
    second_mean = jnp.mean(grad_hat * normed, axis=-1, keepdims=True)
    return inverse * (grad_hat - first_mean - normed * second_mean)


def score_block(queries, head_grads, pair_block):
    row_count = pair_block.shape[0]
    keys_blk = pair_block[:, :HD].reshape(row_count, HEADS, HEAD_DIM)
    values_blk = pair_block[:, HD:].reshape(row_count, HEADS, HEAD_DIM)
    scores = jnp.einsum(
        "qhd,khd->hqk", queries, keys_blk, preferred_element_type=jnp.float32
    ) * HEAD_DIM ** (-0.5)
    dprob = jnp.einsum("qhd,khd->hqk", head_grads, values_blk, preferred_element_type=jnp.float32)
    return (keys_blk, scores, dprob)


def update_stats(statistics, queries, head_grads, pair_rows):
    sub_size = math.gcd(pair_rows.shape[0], 512)

    def visit_block(block_index, running):
        run_max, run_total, run_mix = running
        pair_block = lax.dynamic_slice_in_dim(pair_rows, block_index * sub_size, sub_size, 0)
        keys_blk, scores, dprob = score_block(queries, head_grads, pair_block)
        new_max = jnp.maximum(run_max, jnp.max(scores, axis=-1))
        factor = jnp.exp(run_max - new_max)
        expo = jnp.exp(scores - new_max[..., None])
        return (
            new_max,
            run_total * factor + jnp.sum(expo, axis=-1),
            run_mix * factor + jnp.sum(expo * dprob, axis=-1),
        )

    return lax.fori_loop(0, pair_rows.shape[0] // sub_size, visit_block, statistics)


def block_backward(queries, head_grads, pair_block, log_total, row_delta):
    keys_blk, scores, dprob = score_block(queries, head_grads, pair_block)
    weights = jnp.exp(scores - log_total[..., None])
    prob_weights = weights.astype(jnp.bfloat16)
    dscore = (weights * (dprob - row_delta[..., None])).astype(jnp.bfloat16)
    return (keys_blk, prob_weights, dscore)


def key_terms_from(queries, head_grads, prob_weights, dscore):
    key_part = jnp.einsum(
        "hqk,qhd->khd", dscore, queries, preferred_element_type=jnp.float32
    ) * HEAD_DIM ** (-0.5)
    value_part = jnp.einsum(
        "hqk,qhd->khd", prob_weights, head_grads, preferred_element_type=jnp.float32
    )
    row_count = key_part.shape[0]
    return jnp.concatenate(
        [key_part.reshape(row_count, HD), value_part.reshape(row_count, HD)], axis=1
    )


def query_side(queries, head_grads, keys_values, local_rows):
    seq_rows = local_rows * lax.axis_size("seq")
    start_stats = (
        jnp.full((HEADS, local_rows), -1e30, jnp.float32),
        jnp.zeros((HEADS, local_rows), jnp.float32),
        jnp.zeros((HEADS, local_rows), jnp.float32),
    )
    all_pairs = lax.all_gather(keys_values, "seq", axis=0, tiled=True)
    statistics = update_stats(start_stats, queries, head_grads, all_pairs)
    row_max, row_total, row_mix = statistics
    log_total = row_max + jnp.log(row_total)
    row_delta = row_mix / row_total
    sub_size = math.gcd(seq_rows, 512)
    block_count = seq_rows // sub_size
    empty_query = jnp.zeros((local_rows, HEADS, HEAD_DIM), jnp.float32)

    def backward_step(block_index, running):
        query_grad, buffer = running
        pair_block = lax.dynamic_slice_in_dim(all_pairs, block_index * sub_size, sub_size, 0)
        keys_blk, prob_weights, dscore = block_backward(
            queries, head_grads, pair_block, log_total, row_delta
        )
        query_grad = query_grad + jnp.einsum(
            "hqk,khd->qhd", dscore, keys_blk, preferred_element_type=jnp.float32
        )
        block_terms = key_terms_from(queries, head_grads, prob_weights, dscore)
        buffer = lax.dynamic_update_slice_in_dim(buffer, block_terms, block_index * sub_size, 0)
        return (query_grad, buffer)

    empty_terms = jnp.zeros((seq_rows, 2 * HD), jnp.float32)
    query_grad, buffer = lax.fori_loop(0, block_count, backward_step, (empty_query, empty_terms))
    pair_grads = lax.psum_scatter(
        buffer.astype(jnp.bfloat16), "seq", scatter_dimension=0, tiled=True
    ).astype(jnp.float32)
    return (query_grad, pair_grads)


def local(
    tokens,
    upstream_grad,
    norm_gain,
    norm_bias,
    input_codes,
    input_scales,
    input_bias,
    output_codes,
    output_scales,
    layer_scale,
):
    all_codes, all_scales = (
        lax.all_gather(input_codes.astype(jnp.float32), "weight", axis=0, tiled=True).astype(
            input_codes.dtype
        ),
        lax.all_gather(input_scales, "weight", axis=0, tiled=True),
    )
    input_weight = dequantize(all_codes, all_scales)
    output_weight = dequantize(output_codes, output_scales)
    normed, inverse, norm_out = normalize(tokens[0].astype(jnp.float32), norm_gain, norm_bias)
    projected = (
        jnp.dot(norm_out, input_weight, preferred_element_type=jnp.float32) + input_bias
    ).astype(jnp.bfloat16)
    local_rows = projected.shape[0]
    queries = projected[:, :HD].reshape(local_rows, HEADS, HEAD_DIM)
    keys_values = projected[:, HD:]
    scaled_grad = (upstream_grad[0].astype(jnp.float32) * layer_scale).astype(jnp.bfloat16)
    head_grads = jnp.dot(scaled_grad, output_weight.T, preferred_element_type=jnp.float32).astype(
        jnp.bfloat16
    )
    head_grads = head_grads.reshape(local_rows, HEADS, HEAD_DIM)
    query_grad, pair_grads = query_side(queries, head_grads, keys_values, local_rows)
    query_grad = (query_grad * HEAD_DIM ** (-0.5)).reshape(local_rows, HD)
    grad_proj = jnp.concatenate([query_grad, pair_grads], axis=1).astype(jnp.bfloat16)
    grad_norm = jnp.dot(grad_proj, input_weight.T, preferred_element_type=jnp.float32)
    result = norm_backward(grad_norm, normed, inverse, norm_gain)
    return result[None]


def solution(mesh):
    in_specs = (
        P(("groups", "weight"), "seq", None),
        P(("groups", "weight"), "seq", None),
        P(),
        P(),
        P("weight", None),
        P("weight", None),
        P(),
        P(),
        P(),
        P(),
    )
    out_specs = P(("groups", "weight"), "seq", None)
    fits = mesh.shape["seq"] == 4 and mesh.shape["weight"] == 4
    plan = local_middle if fits else local
    return jax.shard_map(plan, mesh=mesh, in_specs=in_specs, out_specs=out_specs, check_vma=False)
```
